32 devices in a mesh: groups: 2 (over y), row: 4 (over z), col: 2 (over x), sub: 2 (over core).
Axes of the slice: x: 2, y: 2, z: 4, core: 2. Of those that a mesh axis runs over, the one named last changes fastest.
Arguments:
- density: bfloat16 [4096, 2048], P(('groups', 'row'), ('col', 'sub')), parts along dimension 0, as said below
- margin: bfloat16 [4096, 2048], P(('groups', 'row'), ('col', 'sub')), parts along dimension 0, as said below
- pattern_d: int32 [32, 16], P(('groups', 'row'), ('col', 'sub')), parts along dimension 0, may hold values from 0 to 1, as said below
- pattern_s: int32 [32, 16], P(('groups', 'row'), ('col', 'sub')), parts along dimension 0, may hold values from 0 to 1, as said below
- dipole: bfloat16 [3, 4096], P(None, ('groups', 'col', 'sub')), parts along dimension 1, may hold values from -0.125 to 0.125
- owner: int32 [3, 32768], P(None, ('groups', 'row', 'col', 'sub')), parts along dimension 1, may hold values from 0 to 2047
- centres: float32 [3, 32768], P(None, ('groups', 'row', 'col', 'sub')), parts along dimension 1, may hold values from 0 to 3
- angles: float32 [3, 32768], P(None, ('groups', 'row', 'col', 'sub')), parts along dimension 1, may hold values from -3.140625 to 3.140625
- velocity: float32 [3, 32768], P(None, ('groups', 'row', 'col', 'sub')), parts along dimension 1, may hold values from -6 to 6
- angmom: float32 [3, 32768], P(None, ('groups', 'row', 'col', 'sub')), parts along dimension 1, may hold values from -6 to 6
- halo_list: int32 [2, 8192], P(None, ('groups', 'row', 'col', 'sub')), parts along dimension 1, may hold values from 0 to 1023
- neighbours: int32 [32, 32768], P(None, ('groups', 'row', 'col', 'sub')), parts along dimension 1, may hold values from 0 to 1535
Outputs:
- qm_out: bfloat16 [4096, 2048], P(('groups', 'row'), ('col', 'sub')), parts along dimension 0
- centres_new: float32 [3, 32768], P(None, ('groups', 'row', 'col', 'sub')), parts along dimension 1
- velocity_new: float32 [3, 32768], P(None, ('groups', 'row', 'col', 'sub')), parts along dimension 1
- angmom_new: float32 [3, 32768], P(None, ('groups', 'row', 'col', 'sub')), parts along dimension 1
- orient_new: float32 [4, 32768], P(None, ('groups', 'row', 'col', 'sub')), parts along dimension 1
The draws below stay inside these ranges and needn't reach their ends.
There are 2 independent parts, one for each index of `groups`. The reference program is written for one: setup_inputs(seed, part) draws one part's arguments, and reference() takes and returns one part's arrays. A program takes and returns all parts, laid end to end along the dimension named above; each array names one. Nothing has to cross between parts.
Inputs may be any that keep to these rules, and one draw needn't show every extreme that they name: density is symmetric. margin is symmetric. `pattern_d`: symmetric, ones on the diagonal. `pattern_s`: every block row holds exactly 1 ones in each aligned run of 4 block columns.
All inputs are finite; a program needn't handle non-finite values.
Results may differ from the reference program's by a relative error of at most 0.0075.
Values may be sent and summed in bfloat16 or wider, within the bound.
A program may use at most 128 MiB of HBM per device.

```python
import math
import jax
import jax.numpy as jnp
import numpy as np
from jax import lax

BLOCK = 128
ROW_CAP = 1
NB = 16
CW = 4
ORDER = 2048
WATERS = 1024
NEIGH = 32
HALO_DEV = 256
NWAT = 16384
HALO = 4096
N_ROW = 4
N_COL = 2
N_SUB = 2


def symmetric_normal(key, spread):
    base_draw = jnp.clip(jax.random.normal(key, (ORDER, ORDER), jnp.float32), -4.0, 4.0)
    return (base_draw + base_draw.T) * (0.5 * spread)


def block_distance(count):
    row_ids = jnp.arange(count, dtype=jnp.int32)
    return jnp.abs(row_ids[:, None] - row_ids[None, :])


def draw_density(key, part):
    return symmetric_normal(jax.random.fold_in(key, 101), 1.0).astype(jnp.bfloat16)


def draw_margin(key, part):
    return symmetric_normal(jax.random.fold_in(key, 202), 0.0125).astype(jnp.bfloat16)


def draw_pattern_d(key, part):
    coin_flips = (jax.random.randint(jax.random.fold_in(key, 303), (NB, NB), 0, 8) == 0).astype(jnp.int32)
    scattered = jnp.maximum(coin_flips, coin_flips.T)
    banded = (block_distance(NB) <= 1).astype(jnp.int32)
    return jnp.maximum(scattered, banded).astype(jnp.int32)


def draw_pattern_s(key, part):
    column_ids = jnp.arange(NB, dtype=jnp.int32)
    scores = jax.random.randint(jax.random.fold_in(key, 404), (NB, NB), 0, 65536) * NB + column_ids[None, :]
    distance = block_distance(NB)
    scores = scores + jnp.where(distance == 0, 1 << 28, 0) + jnp.where(distance == 1, 1 << 27, 0)
    runs = scores.reshape(NB, NB // CW, CW)
    higher = jnp.sum((runs[:, :, None, :] > runs[:, :, :, None]).astype(jnp.int32), axis=3)
    chosen = (higher < ROW_CAP).astype(jnp.int32)
    return chosen.reshape(NB, NB).astype(jnp.int32)


def touch_ends(result, key, low, top_value):
    longest = result.shape.index(max(result.shape))
    spots = []
    for shift in (0, 1):
        where = [jax.random.randint(jax.random.fold_in(key, axis), (), 0, length) for axis, length in enumerate(result.shape)]
        where[longest] = (where[longest] + shift) % result.shape[longest]
        spots.append(tuple(where))
    return result.at[spots[0]].set(low).at[spots[1]].set(top_value)


def levels(own_key, dims, cuts, smallest, largest):
    level = 1.0
    for axis_at, shards_of in cuts:
        steps = jax.random.uniform(jax.random.fold_in(jax.random.fold_in(own_key, 6), axis_at), (shards_of,), jnp.float32, smallest / len(cuts), largest / len(cuts))
        level = level * jnp.repeat(jnp.exp(steps), dims[axis_at] // shards_of).reshape((-1,) + (1,) * (len(dims) - 1 - axis_at))
    return level


def cumulative_ranks(count, slope):
    weights = [(1 << 20) // math.isqrt(standing ** slope) + 1 for standing in range(1, count + 1)]
    scale = 1 + sum(weights) // (1 << 30)
    return np.cumsum(np.array([max(1, weight // scale) for weight in weights]))


def ranked(stream_key, dims, count, slope):
    listing = cumulative_ranks(count, slope)
    lot = jax.random.randint(jax.random.fold_in(stream_key, 1), dims, 0, int(listing[count - 1]))
    standing = jnp.searchsorted(jnp.asarray(listing, jnp.int32), lot, side="right")
    return jax.random.permutation(jax.random.fold_in(stream_key, 2), count)[standing].astype(jnp.int32)


def bell_draw(stream_key, dims, scale, most, cuts=(), held_as=jnp.bfloat16):
    drawn = jax.random.normal(stream_key, dims, jnp.float32) * scale
    if len(cuts) > 0:
        drawn = levels(stream_key, dims, cuts, -0.22, 0.18) * drawn
    return jnp.clip(drawn, min=-most, max=most).astype(held_as)


def setup_inputs(seed: int = 0, part: int = 0) -> dict:
    streams_of = jax.random.split(jax.random.key(seed), 13)
    part_keys = jax.random.split(jax.random.fold_in(streams_of[12], part), 13)
    return {
        "density": draw_density(jax.random.fold_in(jax.random.fold_in(streams_of[12], part), 71), part),
        "margin": draw_margin(jax.random.fold_in(jax.random.fold_in(streams_of[12], part), 71), part),
        "pattern_d": draw_pattern_d(jax.random.fold_in(jax.random.fold_in(streams_of[12], part), 71), part),
        "pattern_s": draw_pattern_s(jax.random.fold_in(jax.random.fold_in(streams_of[12], part), 71), part),
        "dipole": bell_draw(part_keys[4], (3, ORDER), ORDER ** -0.5, 0.125, ((1, 4),)),
        "owner": touch_ends(ranked(part_keys[5], (3, NWAT), ORDER, 2), jax.random.fold_in(part_keys[5], 3), 0, ORDER - 1).astype(jnp.int32),
        "centres": jnp.clip(3.0 * jax.random.uniform(part_keys[6], (3, NWAT), jnp.float32) ** levels(part_keys[6], (3, NWAT), ((1, 16),), -0.2, 0.2), 0.0, 3.0),
        "angles": jnp.clip(jax.random.uniform(part_keys[7], (3, NWAT), jnp.float32, -3.140625, 3.140625), -3.140625, 3.140625),
        "velocity": bell_draw(part_keys[8], (3, NWAT), 1.0, 6.0, ((1, 16),), jnp.float32),
        "angmom": bell_draw(part_keys[9], (3, NWAT), 1.0, 6.0, ((1, 16),), jnp.float32),
        "halo_list": touch_ends(jax.random.randint(part_keys[10], (2, HALO), 0, WATERS), jax.random.fold_in(part_keys[10], 1), 0, WATERS - 1).astype(jnp.int32),
        "neighbours": touch_ends(jax.random.randint(part_keys[11], (NEIGH, NWAT), 0, WATERS + 2 * HALO_DEV), jax.random.fold_in(part_keys[11], 1), 0, (WATERS + 2 * HALO_DEV) - 1).astype(jnp.int32),
    }


CHARGE = (-0.834, 0.417, 0.417)
OFFSET = ((0.0, 0.0, -0.12), (0.76, 0.0, 0.47), (-0.76, 0.0, 0.47))
COUPLE = 0.1
STEP_DT = 0.5
WATER_MASS = 1.0
INERTIA = 0.5
SOFTEN = 1.0

def expand(pattern, width):
    return jnp.repeat(jnp.repeat(pattern, width, axis=0), width, axis=1)

def quaternion(angles):
    half_angle = 0.5 * angles
    cos_r, cos_p, cos_y = (jnp.cos(half_angle[0]), jnp.cos(half_angle[1]), jnp.cos(half_angle[2]))
    sin_r, sin_p, sin_y = (jnp.sin(half_angle[0]), jnp.sin(half_angle[1]), jnp.sin(half_angle[2]))
    comp_w = cos_r * cos_p * cos_y + sin_r * sin_p * sin_y
    comp_x = sin_r * cos_p * cos_y - cos_r * sin_p * sin_y
    comp_y = cos_r * sin_p * cos_y + sin_r * cos_p * sin_y
    comp_z = cos_r * cos_p * sin_y - sin_r * sin_p * cos_y
    return jnp.stack([comp_w, comp_x, comp_y, comp_z])

def rotation(quat):
    comp_w, comp_x, comp_y, comp_z = (quat[0], quat[1], quat[2], quat[3])
    return ((1.0 - 2.0 * (comp_y * comp_y + comp_z * comp_z), 2.0 * (comp_x * comp_y - comp_w * comp_z), 2.0 * (comp_x * comp_z + comp_w * comp_y)), (2.0 * (comp_x * comp_y + comp_w * comp_z), 1.0 - 2.0 * (comp_x * comp_x + comp_z * comp_z), 2.0 * (comp_y * comp_z - comp_w * comp_x)), (2.0 * (comp_x * comp_z - comp_w * comp_y), 2.0 * (comp_y * comp_z + comp_w * comp_x), 1.0 - 2.0 * (comp_x * comp_x + comp_y * comp_y)))

def site_positions(centres, quat):
    matrix = rotation(quat)
    layers = []
    for source in range(3):
        for compo in range(3):
            layers.append(centres[compo] + matrix[compo][0] * OFFSET[source][0] + matrix[compo][1] * OFFSET[source][1] + matrix[compo][2] * OFFSET[source][2])
    return jnp.stack(layers)

def pair_forces(own_sites, partner_sites):
    pieces = []
    for source in range(3):
        own_part = own_sites[3 * source:3 * source + 3][:, None]
        total = jnp.zeros(own_sites.shape[1:], jnp.float32)[None] * jnp.zeros((3,) + (1,) * (own_sites.ndim - 1), jnp.float32)
        for target in range(3):
            offset_vec = own_part - partner_sites[3 * target:3 * target + 3]
            dist_sq = lax.optimization_barrier(jnp.sum(offset_vec * offset_vec, axis=0)) + SOFTEN
            weight = CHARGE[source] * CHARGE[target] * dist_sq ** (-1.5)
            total = total + lax.optimization_barrier(jnp.sum(offset_vec * weight[None], axis=1))
        pieces.append(total)
    return jnp.concatenate(pieces, axis=0)

def advance(centres, quat, velocity, angmom, sites, forces):
    total = forces[0:3] + forces[3:6] + forces[6:9]
    torque = jnp.zeros_like(centres)
    for source in range(3):
        lever = sites[3 * source:3 * source + 3] - centres
        torque = torque + jnp.cross(lever, forces[3 * source:3 * source + 3], axis=0)
    velocity_new = velocity + STEP_DT * total / WATER_MASS
    centres_new = centres + STEP_DT * velocity_new
    angmom_new = angmom + STEP_DT * torque
    omega = angmom_new / INERTIA
    vector = quat[1:4]
    delta_w = -lax.optimization_barrier(jnp.sum(omega * vector, axis=0))
    delta_vec = quat[0][None] * omega + jnp.cross(omega, vector, axis=0)
    moved = quat + 0.5 * STEP_DT * jnp.concatenate([delta_w[None], delta_vec], axis=0)
    length = jnp.sqrt(lax.optimization_barrier(jnp.sum(moved * moved, axis=0)))
    return (centres_new, velocity_new, angmom_new, moved / length[None])

def reference(density, margin, pattern_d, pattern_s, dipole, owner, centres, angles, velocity, angmom, halo_list, neighbours):
    dens_mask = density * expand(pattern_d, BLOCK).astype(jnp.bfloat16)
    over_mask = margin * expand(pattern_s, BLOCK).astype(jnp.bfloat16)
    product = jnp.dot(dens_mask, over_mask, preferred_element_type=jnp.float32)
    site_charge = jnp.broadcast_to(jnp.array(CHARGE, jnp.float32)[:, None], owner.shape)
    potential = jax.ops.segment_sum(site_charge.reshape(-1), owner.reshape(-1), num_segments=ORDER)
    qm_out = (product + COUPLE * (potential[:, None] + potential[None, :]) * dens_mask.astype(jnp.float32)).astype(jnp.bfloat16)
    qm_field = jnp.dot(dipole, qm_out.T, preferred_element_type=jnp.float32)
    quat = quaternion(angles)
    sites = site_positions(centres, quat)
    groups_cs = N_COL * N_SUB
    grid = sites.reshape(9, N_ROW, groups_cs, WATERS)
    halo_grid = halo_list.reshape(2, N_ROW, groups_cs, HALO_DEV)
    send_up = jnp.take_along_axis(grid, jnp.broadcast_to(halo_grid[0][None], (9, N_ROW, groups_cs, HALO_DEV)), axis=3)
    send_down = jnp.take_along_axis(grid, jnp.broadcast_to(halo_grid[1][None], (9, N_ROW, groups_cs, HALO_DEV)), axis=3)
    table = jnp.concatenate([grid, jnp.roll(send_up, 1, axis=1), jnp.roll(send_down, -1, axis=1)], axis=3)
    width = WATERS + 2 * HALO_DEV
    slots = neighbours.reshape(NEIGH, N_ROW, groups_cs, WATERS)
    partner = jnp.take_along_axis(jnp.broadcast_to(table[:, None], (9, NEIGH, N_ROW, groups_cs, width)), jnp.broadcast_to(slots[None], (9, NEIGH, N_ROW, groups_cs, WATERS)), axis=4)
    partner = partner.reshape(9, NEIGH, NWAT)
    forces = pair_forces(sites, partner)
    field_parts = []
    for source in range(3):
        field_parts.append(forces[3 * source:3 * source + 3] + CHARGE[source] * jnp.take(qm_field, owner[source], axis=1))
    forces = jnp.concatenate(field_parts, axis=0)
    centres_new, velocity_new, angmom_new, orient_new = advance(centres, quat, velocity, angmom, sites, forces)
    return (qm_out, centres_new, velocity_new, angmom_new, orient_new)
```

```python
import jax
import jax.numpy as jnp
from jax import lax
from jax.experimental import pallas as pl
from jax.experimental.pallas import tpu as pltpu
from jax.sharding import PartitionSpec as P

BLOCK = 128
UNIT = 0.417
OFFSET = ((0.0, 0.0, -0.12), (0.76, 0.0, 0.47), (-0.76, 0.0, 0.47))
WEIGHT = (-2.0, 1.0, 1.0)
CHARGE = (-0.834, 0.417, 0.417)
COUPLE = 0.1
STEP_DT = 0.5
WATER_MASS = 1.0
INERTIA = 0.5
SOFTEN = 1.0
CHUNKS = 4
F32 = jnp.float32
BF16 = jnp.bfloat16


def lookup(row, low):
    return jnp.take_along_axis(
        jnp.broadcast_to(row, low.shape), low, axis=1, mode="promise_in_bounds"
    )


def dense(ref, compo):
    count = ref.shape[1] // BLOCK
    return jnp.concatenate(
        [ref[compo : compo + 1, j * BLOCK : (j + 1) * BLOCK] for j in range(count)], axis=0
    )


def spread(ref, compo, value):
    for j in range(ref.shape[1] // BLOCK):
        ref[compo : compo + 1, j * BLOCK : (j + 1) * BLOCK] = value[j : j + 1, :]


def cross(a, b):
    return (
        a[1] * b[2] - a[2] * b[1],
        a[2] * b[0] - a[0] * b[2],
        a[0] * b[1] - a[1] * b[0],
    )


def quaternion(angles):
    cos_r, cos_p, cos_y = [jnp.cos(0.5 * a) for a in angles]
    sin_r, sin_p, sin_y = [jnp.sin(0.5 * a) for a in angles]
    return (
        cos_r * cos_p * cos_y + sin_r * sin_p * sin_y,
        sin_r * cos_p * cos_y - cos_r * sin_p * sin_y,
        cos_r * sin_p * cos_y + sin_r * cos_p * sin_y,
        cos_r * cos_p * sin_y - sin_r * sin_p * cos_y,
    )


def rotation(quat):
    w, x, y, z = quat
    return (
        (1.0 - 2.0 * (y * y + z * z), 2.0 * (x * y - w * z), 2.0 * (x * z + w * y)),
        (2.0 * (x * y + w * z), 1.0 - 2.0 * (x * x + z * z), 2.0 * (y * z - w * x)),
        (2.0 * (x * z - w * y), 2.0 * (y * z + w * x), 1.0 - 2.0 * (x * x + y * y)),
    )


def make_kernel(n_row, n_col, n_sub, rows, cols, waters, neigh, halo):
    n_m = n_col * n_sub
    n_all = n_row * n_m
    order = rows * n_row
    rb, cb, nb = rows // BLOCK, cols // BLOCK, order // BLOCK
    wt, nh = waters // BLOCK, halo // BLOCK
    wide = cols // rows
    step = rows // CHUNKS
    hr = 9 * nh

    def kernel(
        density_hbm, margin_hbm, pat_d_hbm, pat_s_hbm, dipole_hbm, owner_hbm, centres_hbm,
        angles_hbm, velocity_hbm, angmom_hbm, halo_list_hbm, neighbours_hbm,
        coupled, centres_new, velocity_new, angmom_new, orient_new,
        density, margin, pat_d, pat_s, dipole, owner, centres,
        angles, velocity, angmom, halo_list, neighbours,
        panel, comp, full, hist, inner, parts, field, halo_out, halo_in,
        table, force, quats, potential, sums,
        l_sem, c_sem, d_send, d_recv, f_send, s_send, s_recv, h_send, h_recv, v_send, v_recv,
        q_send, q_recv, e_send, e_recv,
    ):
        row, col, sub = lax.axis_index("row"), lax.axis_index("col"), lax.axis_index("sub")
        me = col * n_sub + sub

        def peer(dc, du):
            return {"col": lax.rem(col + dc, n_col), "sub": lax.rem(sub + du, n_sub)}

        def peer_row(dr):
            return {"row": lax.rem(row + dr, n_row)}

        def other(q):
            dr, dm = lax.div(q, n_m), lax.rem(q, n_m)
            return {
                "row": lax.rem(row + dr, n_row),
                "col": lax.rem(col + lax.div(dm, n_sub), n_col),
                "sub": lax.rem(sub + lax.rem(dm, n_sub), n_sub),
            }

        def source(dc, du):
            return (
                lax.rem(col + n_col - dc, n_col) * n_sub + lax.rem(sub + n_sub - du, n_sub)
            )

        started = []

        def remote(src, dst, ssem, rsem, dev):
            return pltpu.make_async_remote_copy(
                src_ref=src, dst_ref=dst, send_sem=ssem, recv_sem=rsem,
                device_id=dev, device_id_type=pl.DeviceIdType.MESH,
            )

        def send(src, dst, ssem, rsem, dev):
            copy = remote(src, dst, ssem, rsem, dev)
            copy.start()
            return copy

        def arrived(ref, sem):
            pltpu.make_async_copy(ref, ref, sem).wait()

        barrier = pltpu.get_barrier_semaphore()

        def greet(q, carry):
            pl.semaphore_signal(
                barrier, inc=1, device_id=other(q), device_id_type=pl.DeviceIdType.MESH
            )
            return carry

        small = [
            pltpu.make_async_copy(src, dst, l_sem.at[n])
            for n, (src, dst) in enumerate((
                (pat_d_hbm, pat_d), (pat_s_hbm, pat_s), (dipole_hbm, dipole),
                (owner_hbm, owner), (angles_hbm, angles), (centres_hbm, centres),
                (halo_list_hbm, halo_list), (neighbours_hbm, neighbours),
                (velocity_hbm, velocity), (angmom_hbm, angmom), (margin_hbm, margin),
            ))
        ]
        loads = [
            pltpu.make_async_copy(
                density_hbm.at[pl.ds(k * step, step)], density.at[pl.ds(k * step, step)],
                c_sem.at[k],
            )
            for k in range(CHUNKS)
        ]
        small[0].start()
        loads[0].start()
        for load in loads[1:]:
            load.start()
        small[10].start()
        for load in small[1:10]:
            load.start()
        lax.fori_loop(1, n_all, greet, 0)

        small[0].wait()
        for k in range(CHUNKS):
            loads[k].wait()
            for i in range(k * step // BLOCK, (k + 1) * step // BLOCK):
                at = slice(i * BLOCK, (i + 1) * BLOCK)
                for j in range(cb):
                    ac = slice(j * BLOCK, (j + 1) * BLOCK)
                    factor = pat_d[i, j].astype(F32)
                    panel[me, at, ac] = (density[at, ac].astype(F32) * factor).astype(BF16)
        small[1].wait()
        small[2].wait()
        small[10].wait()
        low_u = []
        for i in range(rb):
            at = slice(i * BLOCK, (i + 1) * BLOCK)
            total, chosen = None, None
            for j in range(cb):
                ac = slice(j * BLOCK, (j + 1) * BLOCK)
                factor = pat_s[i, j].astype(F32)
                term = margin[at, ac].astype(F32) * factor
                dip = dipole[:, ac].astype(F32) * factor
                total = term if total is None else total + term
                chosen = dip if chosen is None else chosen + dip
            tile = total.astype(BF16)
            comp[row, at, :] = tile
            low_u.append(
                lax.dot_general(
                    chosen.astype(BF16), tile, (((1,), (1,)), ((), ())),
                    preferred_element_type=F32,
                )
            )
        for base in range(0, rb * cb, 16):
            comp[row, rows + base : rows + base + 16, :] = jnp.concatenate(
                [
                    jnp.full((1, BLOCK), pat_s[q // cb, q % cb].astype(F32), F32)
                    for q in range(base, base + 16)
                ],
                axis=0,
            ).astype(BF16)
        target, lane = lax.div(row, wide), lax.rem(row, wide)
        for i in range(rb):
            inner[4 * i : 4 * i + 3, :] = low_u[i]
            inner[4 * i + 3 : 4 * i + 4, :] = low_u[i][0:1, :]

        small[3].wait()
        lane_ids = lax.broadcasted_iota(jnp.int32, (BLOCK, waters), 0)
        high_ids = lax.broadcasted_iota(jnp.int32, (nb, waters), 0)
        counts = jnp.zeros((nb, BLOCK), F32)
        for site in range(3):
            own = owner[site : site + 1, :]
            low_hot = jnp.where(lane_ids == (own & (BLOCK - 1)), 1.0, 0.0).astype(BF16)
            high_hot = jnp.where(high_ids == (own >> 7), WEIGHT[site], 0.0).astype(BF16)
            counts = counts + lax.dot_general(
                high_hot, low_hot, (((1,), (1,)), ((), ())), preferred_element_type=F32
            )
        hist[0] = counts.astype(jnp.int32).astype(jnp.int16)
        for load in small[4:8]:
            load.wait()
        cent = [dense(centres, c) for c in range(3)]
        quat = quaternion([dense(angles, c) for c in range(3)])
        for c in range(4):
            quats[c] = quat[c]
        matrix = rotation(quat)
        for a in range(3):
            for c in range(3):
                table[3 * a + c] = (
                    cent[c]
                    + matrix[c][0] * OFFSET[a][0]
                    + matrix[c][1] * OFFSET[a][1]
                    + matrix[c][2] * OFFSET[a][2]
                )
        listed = [
            halo_list[side : side + 1, j * BLOCK : (j + 1) * BLOCK]
            for side in range(2) for j in range(nh)
        ]
        picks = jnp.concatenate(listed + [listed[0]] * (8 - len(listed)), axis=0)
        low, high = picks & (BLOCK - 1), picks >> 7
        for t in range(9):
            value = lookup(table[t, 0:1, :], low)
            for h in range(1, wt):
                value = jnp.where(high == h, lookup(table[t, h : h + 1, :], low), value)
            for side in range(2):
                halo_out[side, t * nh : (t + 1) * nh, :] = value[side * nh : (side + 1) * nh, :]
        pl.semaphore_wait(barrier, n_all - 1)

        def share(q, carry):
            remote(hist.at[0], hist.at[q], h_send, h_recv, other(q)).start()
            return carry

        lax.fori_loop(1, n_all, share, 0)

        def pass_inner(dr):
            there = peer_row(dr)
            there["col"], there["sub"] = lax.div(target, n_sub), lax.rem(target, n_sub)
            return remote(
                inner, parts.at[lane, me], v_send.at[dr], v_recv.at[lane, me], there
            )

        @pl.when(target == me)
        def _():
            parts[lane, me] = inner[...]

        pl.when(target != me)(lambda: pass_inner(0).start())
        for dr in range(1, n_row):
            pass_inner(dr).start()
        for side, by in ((0, 1), (1, n_row - 1)):
            started.append(
                send(halo_out.at[side], halo_in.at[side], e_send.at[side], e_recv.at[side],
                     peer_row(by))
            )
        for k in range(CHUNKS):
            at = pl.ds(k * step, step)
            for dc in range(1, n_col):
                started.append(
                    send(panel.at[me, at], panel.at[me, at], d_send.at[dc, 0, k],
                         d_recv.at[dc, 0, k], peer(dc, 0))
                )
            if k == 0:
                for dr in range(1, n_row):
                    started.append(
                        send(comp.at[row], comp.at[row], s_send.at[dr], s_recv.at[dr],
                             peer_row(dr))
                    )
        for k in range(CHUNKS):
            at = pl.ds(k * step, step)
            for du in range(1, n_sub):
                started.append(
                    send(panel.at[me, at], panel.at[me, at], d_send.at[0, du, k],
                         d_recv.at[0, du, k], peer(0, du))
                )

        def expand(r):
            marks = comp[r, rows : rows + rb * cb, :].astype(F32)
            for i in range(rb):
                tile = comp[r, i * BLOCK : (i + 1) * BLOCK, :].astype(F32)
                at = pl.ds(pl.multiple_of(r * rows + i * BLOCK, BLOCK), BLOCK)
                for j in range(cb):
                    q = i * cb + j
                    full[at, j * BLOCK : (j + 1) * BLOCK] = (tile * marks[q : q + 1, :]).astype(BF16)

        def pass_on(k):
            at = pl.ds(k * step, step)
            for dc in range(1, n_col):
                slot = source(dc, 0)
                arrived(panel.at[slot, at], d_recv.at[dc, 0, k])
                for du in range(1, n_sub):
                    started.append(
                        send(panel.at[slot, at], panel.at[slot, at], f_send.at[dc, du, k],
                             d_recv.at[dc, du, k], peer(0, du))
                    )

        def pair_tile(j, carry):
            lanes = pl.ds(pl.multiple_of(j * BLOCK, BLOCK), BLOCK)
            own = [jnp.broadcast_to(table[t, pl.ds(j, 1), :], (8, BLOCK)) for t in range(9)]
            totals = [jnp.zeros((8, BLOCK), F32) for _ in range(9)]
            for s in range(0, neigh, 8):
                idx = neighbours[s : s + 8, lanes]
                low, high = idx & (BLOCK - 1), idx >> 7
                part = [lookup(table[t, 0:1, :], low) for t in range(9)]
                for h in range(1, wt + 2 * nh):
                    hit = high == h
                    for t in range(9):
                        if h < wt:
                            line = table[t, h : h + 1, :]
                        else:
                            side, at = (h - wt) // nh, t * nh + (h - wt) % nh
                            line = halo_in[side, at : at + 1, :]
                        part[t] = jnp.where(hit, lookup(line, low), part[t])
                for a in range(3):
                    for b in range(3):
                        d = [own[3 * a + c] - part[3 * b + c] for c in range(3)]
                        inv = lax.rsqrt(d[0] * d[0] + d[1] * d[1] + d[2] * d[2] + SOFTEN)
                        weight = (CHARGE[a] * CHARGE[b]) * (inv * inv * inv)
                        for c in range(3):
                            totals[3 * a + c] = totals[3 * a + c] + d[c] * weight
            for t in range(9):
                force[t, pl.ds(j, 1), :] = jnp.sum(totals[t], axis=0, keepdims=True)
            return carry

        expand(row)
        for side in range(2):
            arrived(halo_in.at[side], e_recv.at[side])
        lax.fori_loop(0, wt // 2, pair_tile, 0)

        arrived(hist.at[pl.ds(1, n_all - 1)], h_recv)
        counts = lax.fori_loop(
            1, n_all, lambda q, c: c + hist[q].astype(jnp.int32), hist[0].astype(jnp.int32)
        )
        potential[...] = counts.astype(F32) * UNIT
        for s in range(wide):
            for m in range(n_m):
                is_own = jnp.logical_and(target == me, jnp.logical_and(lane == s, me == m))
                pl.when(jnp.logical_not(is_own))(
                    lambda s=s, m=m: arrived(parts.at[s, m], v_recv.at[s, m])
                )
        lines = [[], [], []]
        for s in range(wide):
            total = parts[s, 0]
            for m in range(1, n_m):
                total = total + parts[s, m]
            for i in range(rb):
                j = s * rb + i
                weigh = COUPLE * potential[pl.ds(me * cb + j, 1), :]
                dip = dipole[:, j * BLOCK : (j + 1) * BLOCK].astype(F32)
                for c in range(3):
                    lines[c].append(total[4 * i + c : 4 * i + c + 1, :] + weigh * dip[c : c + 1, :])
        vector = jnp.concatenate([jnp.concatenate(line, axis=1) for line in lines], axis=0)
        coarse = vector.astype(BF16).astype(F32)
        stack = jnp.concatenate(
            [coarse, vector - coarse, dipole[...].astype(F32), jnp.zeros((7, cols), F32)], axis=0
        ).astype(BF16)
        for i in range(rb):
            got = lax.dot_general(
                stack, panel[me, i * BLOCK : (i + 1) * BLOCK, :], (((1,), (1,)), ((), ())),
                preferred_element_type=F32,
            )
            weigh = COUPLE * potential[pl.ds(row * rb + i, 1), :]
            inner2 = got[0:3, :] + got[3:6, :] + weigh * got[6:9, :]
            low_u[i] = jnp.concatenate([inner2, jnp.zeros((1, BLOCK), F32)], axis=0)
        field[0] = jnp.concatenate(low_u, axis=0).astype(BF16)

        def tell(q, carry):
            remote(field.at[0], field.at[q], q_send, q_recv, other(q)).start()
            return carry

        lax.fori_loop(1, n_all, tell, 0)
        pass_on(0)
        lax.fori_loop(wt // 2, wt, pair_tile, 0)
        pass_on(1)

        arrived(field.at[pl.ds(1, n_all - 1)], q_recv)
        small[8].wait()
        small[9].wait()
        for dr in range(n_row):
            total = field[dr * n_m].astype(F32)
            for m in range(1, n_m):
                total = total + field[dr * n_m + m].astype(F32)
            sums[lax.rem(row + n_row - dr, n_row)] = total

        forces = []
        for a in range(3):
            own = dense(owner, a)
            low, high = own & (BLOCK - 1), own >> 7
            value = [jnp.zeros((wt, BLOCK), F32)] * 3
            for h in range(nb):
                hit = high == h
                at = 4 * (h % rb)
                for c in range(3):
                    value[c] = jnp.where(
                        hit, lookup(sums[h // rb, at + c : at + c + 1, :], low), value[c]
                    )
            forces.append([force[3 * a + c] + CHARGE[a] * value[c] for c in range(3)])
        cent = [dense(centres, c) for c in range(3)]
        quat = [quats[c] for c in range(4)]
        torque = [jnp.zeros((wt, BLOCK), F32)] * 3
        for a in range(3):
            lever = [table[3 * a + c] - cent[c] for c in range(3)]
            turn = cross(lever, forces[a])
            torque = [torque[c] + turn[c] for c in range(3)]
        omega = []
        for c in range(3):
            pull = forces[0][c] + forces[1][c] + forces[2][c]
            fast = dense(velocity, c) + STEP_DT * pull / WATER_MASS
            spread(velocity_new, c, fast)
            spread(centres_new, c, cent[c] + STEP_DT * fast)
            spin = dense(angmom, c) + STEP_DT * torque[c]
            spread(angmom_new, c, spin)
            omega.append(spin / INERTIA)
        vector = quat[1:4]
        delta = [-(omega[0] * vector[0] + omega[1] * vector[1] + omega[2] * vector[2])]
        turn = cross(omega, vector)
        delta += [quat[0] * omega[c] + turn[c] for c in range(3)]
        moved = [quat[c] + 0.5 * STEP_DT * delta[c] for c in range(4)]
        length = jnp.sqrt(sum(m * m for m in moved))
        for c in range(4):
            spread(orient_new, c, moved[c] / length)
        pass_on(2)

        def unfold(dr, carry):
            r = lax.rem(row + n_row - dr, n_row)
            arrived(comp.at[r], s_recv.at[dr])
            expand(r)
            return carry

        lax.fori_loop(1, n_row, unfold, 0)
        pass_on(3)
        col_pot = jnp.concatenate(
            [potential[pl.ds(me * cb + j, 1), :] for j in range(cb)], axis=1
        )
        eye = (
            lax.broadcasted_iota(jnp.int32, (BLOCK, BLOCK), 0)
            == lax.broadcasted_iota(jnp.int32, (BLOCK, BLOCK), 1)
        )

        def product(k, _):
            at = pl.ds(pl.multiple_of(k * step, step), step)
            total = jnp.zeros((step, cols), F32)
            for dc in range(n_col):
                for du in range(n_sub):
                    slot = source(dc, du)
                    if du > 0:
                        arrived(panel.at[slot, at], d_recv.at[dc, du, k])
                    depth = pl.ds(pl.multiple_of(slot * cols, cols), cols)
                    total = total + jnp.dot(
                        panel[slot, at, :], full[depth, :], preferred_element_type=F32
                    )
            line = potential[pl.ds(row * rb + k, 1), :]
            row_pot = jnp.sum(jnp.where(eye, line, 0.0), axis=1, keepdims=True)
            mine = panel[me, at, :].astype(F32)
            coupled[at, :] = (total + COUPLE * (row_pot + col_pot) * mine).astype(BF16)
            return 0

        lax.fori_loop(0, CHUNKS, product, 0)

        arrived(hist.at[pl.ds(1, n_all - 1)], h_send)
        arrived(field.at[pl.ds(1, n_all - 1)], q_send)
        pl.when(target != me)(lambda: pass_inner(0).wait_send())
        for dr in range(1, n_row):
            pass_inner(dr).wait_send()
        for copy in started:
            copy.wait_send()

    hbm = pl.BlockSpec(memory_space=pltpu.HBM)
    vmem = pl.BlockSpec(memory_space=pltpu.VMEM)
    dma = lambda *s: pltpu.SemaphoreType.DMA(s)
    one = pltpu.SemaphoreType.DMA(())
    call = pl.pallas_call(
        kernel,
        out_shape=(
            pltpu.VMEM((rows, cols), BF16),
            pltpu.VMEM((3, waters), F32),
            pltpu.VMEM((3, waters), F32),
            pltpu.VMEM((3, waters), F32),
            pltpu.VMEM((4, waters), F32),
        ),
        in_specs=[hbm] * 12,
        out_specs=(vmem,) * 5,
        scratch_shapes=[
            pltpu.VMEM((rows, cols), BF16),
            pltpu.VMEM((rows, cols), BF16),
            pltpu.SMEM((rb, cb), jnp.int32),
            pltpu.SMEM((rb, cb), jnp.int32),
            pltpu.VMEM((3, cols), BF16),
            pltpu.VMEM((3, waters), jnp.int32),
            pltpu.VMEM((3, waters), F32),
            pltpu.VMEM((3, waters), F32),
            pltpu.VMEM((3, waters), F32),
            pltpu.VMEM((3, waters), F32),
            pltpu.VMEM((2, halo), jnp.int32),
            pltpu.VMEM((neigh, waters), jnp.int32),
            pltpu.VMEM((n_m, rows, cols), BF16),
            pltpu.VMEM((n_row, rows + rb * cb, BLOCK), BF16),
            pltpu.VMEM((order, cols), BF16),
            pltpu.VMEM((n_all, nb, BLOCK), jnp.int16),
            pltpu.VMEM((rb * 4, BLOCK), F32),
            pltpu.VMEM((wide, n_m, rb * 4, BLOCK), F32),
            pltpu.VMEM((n_all, rb * 4, BLOCK), BF16),
            pltpu.VMEM((2, 24, BLOCK), F32),
            pltpu.VMEM((2, 24, BLOCK), F32),
            pltpu.VMEM((9, wt, BLOCK), F32),
            pltpu.VMEM((9, wt, BLOCK), F32),
            pltpu.VMEM((4, wt, BLOCK), F32),
            pltpu.VMEM((nb, BLOCK), F32),
            pltpu.VMEM((n_row, rb * 4, BLOCK), F32),
            dma(11), dma(CHUNKS),
            dma(n_col, n_sub, CHUNKS), dma(n_col, n_sub, CHUNKS), dma(n_col, n_sub, CHUNKS),
            dma(n_row), dma(n_row), one, one, dma(n_row), dma(wide, n_m),
            one, one, dma(2), dma(2),
        ],
        compiler_params=pltpu.CompilerParams(
            collective_id=0, has_side_effects=True, vmem_limit_bytes=48 << 20
        ),
    )
    return call


def deliver(results):
    count = len(results)

    def kernel(*refs):
        sem = refs[2 * count]
        stores = [
            pltpu.make_async_copy(refs[n], refs[count + n], sem.at[n]) for n in range(count)
        ]
        for store in stores:
            store.start()
        for store in stores:
            store.wait()

    return pl.pallas_call(
        kernel,
        out_shape=tuple(jax.ShapeDtypeStruct(r.shape, r.dtype) for r in results),
        in_specs=[pl.BlockSpec(memory_space=pltpu.VMEM)] * count,
        out_specs=(pl.BlockSpec(memory_space=pltpu.HBM),) * count,
        scratch_shapes=[pltpu.SemaphoreType.DMA((count,))],
    )(*[pltpu.with_memory_space_constraint(r, pltpu.VMEM) for r in results])


def solution(mesh):
    n_row, n_col, n_sub = mesh.shape["row"], mesh.shape["col"], mesh.shape["sub"]

    def shards(density, margin, pattern_d, pattern_s, dipole, owner, centres, angles,
               velocity, angmom, halo_list, neighbours):
        call = make_kernel(
            n_row, n_col, n_sub, density.shape[0], density.shape[1], owner.shape[1],
            neighbours.shape[0], halo_list.shape[1],
        )
        return deliver(
            call(*[
                pltpu.with_memory_space_constraint(x, pltpu.HBM)
                for x in (density, margin, pattern_d, pattern_s, dipole, owner, centres,
                          angles, velocity, angmom, halo_list, neighbours)
            ])
        )

    block = P(("groups", "row"), ("col", "sub"))
    water = P(None, ("groups", "row", "col", "sub"))
    return jax.shard_map(
        shards,
        mesh=mesh,
        in_specs=(block,) * 4 + (P(None, ("groups", "col", "sub")),) + (water,) * 7,
        out_specs=(block,) + (water,) * 4,
        check_vma=False,
    )
```

```python
import jax
import jax.numpy as jnp
from jax import lax
from jax.experimental import pallas as pl
from jax.experimental.pallas import tpu as pltpu
from jax.sharding import PartitionSpec as P

BLOCK = 128
UNIT = 0.417
OFFSET = ((0.0, 0.0, -0.12), (0.76, 0.0, 0.47), (-0.76, 0.0, 0.47))
WEIGHT = (-2.0, 1.0, 1.0)
CHARGE = (-0.834, 0.417, 0.417)
COUPLE = 0.1
STEP_DT = 0.5
WATER_MASS = 1.0
INERTIA = 0.5
SOFTEN = 1.0
CHUNKS = 4
F32 = jnp.float32
BF16 = jnp.bfloat16


def lookup(row, low):
    return jnp.take_along_axis(
        jnp.broadcast_to(row, low.shape), low, axis=1, mode="promise_in_bounds"
    )


def dense(ref, compo):
    count = ref.shape[1] // BLOCK
    return jnp.concatenate(
        [ref[compo : compo + 1, j * BLOCK : (j + 1) * BLOCK] for j in range(count)], axis=0
    )


def spread(ref, compo, value):
    for j in range(ref.shape[1] // BLOCK):
        ref[compo : compo + 1, j * BLOCK : (j + 1) * BLOCK] = value[j : j + 1, :]


def cross(a, b):
    return (
        a[1] * b[2] - a[2] * b[1],
        a[2] * b[0] - a[0] * b[2],
        a[0] * b[1] - a[1] * b[0],
    )


def quaternion(angles):
    cos_r, cos_p, cos_y = [jnp.cos(0.5 * a) for a in angles]
    sin_r, sin_p, sin_y = [jnp.sin(0.5 * a) for a in angles]
    return (
        cos_r * cos_p * cos_y + sin_r * sin_p * sin_y,
        sin_r * cos_p * cos_y - cos_r * sin_p * sin_y,
        cos_r * sin_p * cos_y + sin_r * cos_p * sin_y,
        cos_r * cos_p * sin_y - sin_r * sin_p * cos_y,
    )


def rotation(quat):
    w, x, y, z = quat
    return (
        (1.0 - 2.0 * (y * y + z * z), 2.0 * (x * y - w * z), 2.0 * (x * z + w * y)),
        (2.0 * (x * y + w * z), 1.0 - 2.0 * (x * x + z * z), 2.0 * (y * z - w * x)),
        (2.0 * (x * z - w * y), 2.0 * (y * z + w * x), 1.0 - 2.0 * (x * x + y * y)),
    )


def make_kernel(n_row, n_col, n_sub, rows, cols, waters, neigh, halo):
    n_m = n_col * n_sub
    n_all = n_row * n_m
    n_chip = n_row * n_col
    order = rows * n_row
    rb, cb, nb = rows // BLOCK, cols // BLOCK, order // BLOCK
    wt, nh = waters // BLOCK, halo // BLOCK
    wide = cols // rows
    step = rows // CHUNKS
    hr = 9 * nh

    def kernel(
        density_hbm, margin_hbm, pat_d_hbm, pat_s_hbm, dipole_hbm, owner_hbm, centres_hbm,
        angles_hbm, velocity_hbm, angmom_hbm, halo_list_hbm, neighbours_hbm,
        coupled, centres_new, velocity_new, angmom_new, orient_new,
        density, margin, pat_d, pat_s, dipole, owner, centres,
        angles, velocity, angmom, halo_list, neighbours,
        panel, comp, full, hist, inner, parts, field, halo_out, halo_in,
        table, force, quats, potential, sums, hist1, field1,
        l_sem, c_sem, d_send, d_recv, f_send, s_send, s_recv, h_send, h_recv, v_send, v_recv,
        q_send, q_recv, e_send, e_recv, i_send, i_recv, g_send, g_recv,
    ):
        row, col, sub = lax.axis_index("row"), lax.axis_index("col"), lax.axis_index("sub")
        me = col * n_sub + sub

        def peer(dc, du):
            return {"col": lax.rem(col + dc, n_col), "sub": lax.rem(sub + du, n_sub)}

        def peer_row(dr):
            return {"row": lax.rem(row + dr, n_row)}

        def other(q):
            dr, dm = lax.div(q, n_m), lax.rem(q, n_m)
            return {
                "row": lax.rem(row + dr, n_row),
                "col": lax.rem(col + lax.div(dm, n_sub), n_col),
                "sub": lax.rem(sub + lax.rem(dm, n_sub), n_sub),
            }

        def chip(q):
            return {
                "row": lax.rem(row + lax.div(q, n_col), n_row),
                "col": lax.rem(col + lax.rem(q, n_col), n_col),
            }

        def source(dc, du):
            return (
                lax.rem(col + n_col - dc, n_col) * n_sub + lax.rem(sub + n_sub - du, n_sub)
            )

        started = []

        def remote(src, dst, ssem, rsem, dev):
            return pltpu.make_async_remote_copy(
                src_ref=src, dst_ref=dst, send_sem=ssem, recv_sem=rsem,
                device_id=dev, device_id_type=pl.DeviceIdType.MESH,
            )

        def send(src, dst, ssem, rsem, dev):
            copy = remote(src, dst, ssem, rsem, dev)
            copy.start()
            return copy

        def arrived(ref, sem):
            pltpu.make_async_copy(ref, ref, sem).wait()

        barrier = pltpu.get_barrier_semaphore()

        def greet(q, carry):
            pl.semaphore_signal(
                barrier, inc=1, device_id=other(q), device_id_type=pl.DeviceIdType.MESH
            )
            return carry

        small = [
            pltpu.make_async_copy(src, dst, l_sem.at[n])
            for n, (src, dst) in enumerate((
                (pat_d_hbm, pat_d), (pat_s_hbm, pat_s), (dipole_hbm, dipole),
                (owner_hbm, owner), (angles_hbm, angles), (centres_hbm, centres),
                (halo_list_hbm, halo_list), (neighbours_hbm, neighbours),
                (velocity_hbm, velocity), (angmom_hbm, angmom), (margin_hbm, margin),
            ))
        ]
        loads = [
            pltpu.make_async_copy(
                density_hbm.at[pl.ds(k * step, step)], density.at[pl.ds(k * step, step)],
                c_sem.at[k],
            )
            for k in range(CHUNKS)
        ]
        small[0].start()
        loads[0].start()
        for load in loads[1:]:
            load.start()
        small[10].start()
        for load in small[1:10]:
            load.start()
        lax.fori_loop(1, n_all, greet, 0)

        small[0].wait()
        for k in range(CHUNKS):
            loads[k].wait()
            for i in range(k * step // BLOCK, (k + 1) * step // BLOCK):
                at = slice(i * BLOCK, (i + 1) * BLOCK)
                for j in range(cb):
                    ac = slice(j * BLOCK, (j + 1) * BLOCK)
                    factor = pat_d[i, j].astype(F32)
                    panel[me, at, ac] = (density[at, ac].astype(F32) * factor).astype(BF16)
        small[1].wait()
        small[2].wait()
        small[10].wait()
        low_u = []
        for i in range(rb):
            at = slice(i * BLOCK, (i + 1) * BLOCK)
            total, chosen = None, None
            for j in range(cb):
                ac = slice(j * BLOCK, (j + 1) * BLOCK)
                factor = pat_s[i, j].astype(F32)
                term = margin[at, ac].astype(F32) * factor
                dip = dipole[:, ac].astype(F32) * factor
                total = term if total is None else total + term
                chosen = dip if chosen is None else chosen + dip
            tile = total.astype(BF16)
            comp[row, at, :] = tile
            low_u.append(
                lax.dot_general(
                    chosen.astype(BF16), tile, (((1,), (1,)), ((), ())),
                    preferred_element_type=F32,
                )
            )
        for base in range(0, rb * cb, 16):
            comp[row, rows + base : rows + base + 16, :] = jnp.concatenate(
                [
                    jnp.full((1, BLOCK), pat_s[q // cb, q % cb].astype(F32), F32)
                    for q in range(base, base + 16)
                ],
                axis=0,
            ).astype(BF16)
        target, lane = lax.div(row, wide), lax.rem(row, wide)
        for i in range(rb):
            inner[4 * i : 4 * i + 3, :] = low_u[i]
            inner[4 * i + 3 : 4 * i + 4, :] = low_u[i][0:1, :]

        small[3].wait()
        lane_ids = lax.broadcasted_iota(jnp.int32, (BLOCK, waters), 0)
        high_ids = lax.broadcasted_iota(jnp.int32, (nb, waters), 0)
        counts = jnp.zeros((nb, BLOCK), F32)
        for site in range(3):
            own = owner[site : site + 1, :]
            low_hot = jnp.where(lane_ids == (own & (BLOCK - 1)), 1.0, 0.0).astype(BF16)
            high_hot = jnp.where(high_ids == (own >> 7), WEIGHT[site], 0.0).astype(BF16)
            counts = counts + lax.dot_general(
                high_hot, low_hot, (((1,), (1,)), ((), ())), preferred_element_type=F32
            )
        hist1[0] = counts.astype(jnp.int32).astype(jnp.int16)
        for load in small[4:8]:
            load.wait()
        cent = [dense(centres, c) for c in range(3)]
        quat = quaternion([dense(angles, c) for c in range(3)])
        for c in range(4):
            quats[c] = quat[c]
        matrix = rotation(quat)
        for a in range(3):
            for c in range(3):
                table[3 * a + c] = (
                    cent[c]
                    + matrix[c][0] * OFFSET[a][0]
                    + matrix[c][1] * OFFSET[a][1]
                    + matrix[c][2] * OFFSET[a][2]
                )
        listed = [
            halo_list[side : side + 1, j * BLOCK : (j + 1) * BLOCK]
            for side in range(2) for j in range(nh)
        ]
        picks = jnp.concatenate(listed + [listed[0]] * (8 - len(listed)), axis=0)
        low, high = picks & (BLOCK - 1), picks >> 7
        for t in range(9):
            value = lookup(table[t, 0:1, :], low)
            for h in range(1, wt):
                value = jnp.where(high == h, lookup(table[t, h : h + 1, :], low), value)
            for side in range(2):
                halo_out[side, t * nh : (t + 1) * nh, :] = value[side * nh : (side + 1) * nh, :]
        pl.semaphore_wait(barrier, n_all - 1)

        for du in range(1, n_sub):
            started.append(
                send(hist1.at[0], hist1.at[du], i_send.at[du], i_recv.at[du], peer(0, du))
            )

        def pass_inner(dr):
            there = peer_row(dr)
            there["col"], there["sub"] = lax.div(target, n_sub), lax.rem(target, n_sub)
            return remote(
                inner, parts.at[lane, me], v_send.at[dr], v_recv.at[lane, me], there
            )

        @pl.when(target == me)
        def _():
            parts[lane, me] = inner[...]

        pl.when(target != me)(lambda: pass_inner(0).start())
        for dr in range(1, n_row):
            pass_inner(dr).start()
        for side, by in ((0, 1), (1, n_row - 1)):
            started.append(
                send(halo_out.at[side], halo_in.at[side], e_send.at[side], e_recv.at[side],
                     peer_row(by))
            )
        def send_panel(k):
            at = pl.ds(k * step, step)
            for dc in range(1, n_col):
                started.append(
                    send(panel.at[me, at], panel.at[me, at], d_send.at[dc, 0, k],
                         d_recv.at[dc, 0, k], peer(dc, 0))
                )

        send_panel(0)
        total = hist1[0].astype(jnp.int32)
        for du in range(1, n_sub):
            arrived(hist1.at[du], i_recv.at[du])
            total = total + hist1[du].astype(jnp.int32)
        hist[0] = total.astype(jnp.int16)

        def share(q, carry):
            remote(hist.at[0], hist.at[q], h_send, h_recv, chip(q)).start()
            return carry

        lax.fori_loop(1, n_chip, share, 0)
        for dr in range(1, n_row):
            started.append(
                send(comp.at[row], comp.at[row], s_send.at[dr], s_recv.at[dr], peer_row(dr))
            )
        for k in range(1, CHUNKS):
            send_panel(k)
        for k in range(CHUNKS):
            at = pl.ds(k * step, step)
            for du in range(1, n_sub):
                started.append(
                    send(panel.at[me, at], panel.at[me, at], d_send.at[0, du, k],
                         d_recv.at[0, du, k], peer(0, du))
                )

        def expand(r):
            marks = comp[r, rows : rows + rb * cb, :].astype(F32)
            for i in range(rb):
                tile = comp[r, i * BLOCK : (i + 1) * BLOCK, :].astype(F32)
                at = pl.ds(pl.multiple_of(r * rows + i * BLOCK, BLOCK), BLOCK)
                for j in range(cb):
                    q = i * cb + j
                    full[at, j * BLOCK : (j + 1) * BLOCK] = (tile * marks[q : q + 1, :]).astype(BF16)

        def pass_on(k):
            at = pl.ds(k * step, step)
            for dc in range(1, n_col):
                slot = source(dc, 0)
                arrived(panel.at[slot, at], d_recv.at[dc, 0, k])
                for du in range(1, n_sub):
                    started.append(
                        send(panel.at[slot, at], panel.at[slot, at], f_send.at[dc, du, k],
                             d_recv.at[dc, du, k], peer(0, du))
                    )

        def pair_tile(j, carry):
            lanes = pl.ds(pl.multiple_of(j * BLOCK, BLOCK), BLOCK)
            own = [jnp.broadcast_to(table[t, pl.ds(j, 1), :], (8, BLOCK)) for t in range(9)]
            totals = [jnp.zeros((8, BLOCK), F32) for _ in range(9)]
            for s in range(0, neigh, 8):
                idx = neighbours[s : s + 8, lanes]
                low, high = idx & (BLOCK - 1), idx >> 7
                part = [lookup(table[t, 0:1, :], low) for t in range(9)]
                for h in range(1, wt + 2 * nh):
                    hit = high == h
                    for t in range(9):
                        if h < wt:
                            line = table[t, h : h + 1, :]
                        else:
                            side, at = (h - wt) // nh, t * nh + (h - wt) % nh
                            line = halo_in[side, at : at + 1, :]
                        part[t] = jnp.where(hit, lookup(line, low), part[t])
                for a in range(3):
                    for b in range(3):
                        d = [own[3 * a + c] - part[3 * b + c] for c in range(3)]
                        inv = lax.rsqrt(d[0] * d[0] + d[1] * d[1] + d[2] * d[2] + SOFTEN)
                        weight = (CHARGE[a] * CHARGE[b]) * (inv * inv * inv)
                        for c in range(3):
                            totals[3 * a + c] = totals[3 * a + c] + d[c] * weight
            for t in range(9):
                force[t, pl.ds(j, 1), :] = jnp.sum(totals[t], axis=0, keepdims=True)
            return carry

        expand(row)
        for side in range(2):
            arrived(halo_in.at[side], e_recv.at[side])
        lax.fori_loop(0, wt // 2, pair_tile, 0)

        arrived(hist.at[pl.ds(1, n_chip - 1)], h_recv)
        counts = lax.fori_loop(
            1, n_chip, lambda q, c: c + hist[q].astype(jnp.int32), hist[0].astype(jnp.int32)
        )
        potential[...] = counts.astype(F32) * UNIT
        for s in range(wide):
            for m in range(n_m):
                is_own = jnp.logical_and(target == me, jnp.logical_and(lane == s, me == m))
                pl.when(jnp.logical_not(is_own))(
                    lambda s=s, m=m: arrived(parts.at[s, m], v_recv.at[s, m])
                )
        lines = [[], [], []]
        for s in range(wide):
            total = parts[s, 0]
            for m in range(1, n_m):
                total = total + parts[s, m]
            for i in range(rb):
                j = s * rb + i
                weigh = COUPLE * potential[pl.ds(me * cb + j, 1), :]
                dip = dipole[:, j * BLOCK : (j + 1) * BLOCK].astype(F32)
                for c in range(3):
                    lines[c].append(total[4 * i + c : 4 * i + c + 1, :] + weigh * dip[c : c + 1, :])
        vector = jnp.concatenate([jnp.concatenate(line, axis=1) for line in lines], axis=0)
        coarse = vector.astype(BF16).astype(F32)
        stack = jnp.concatenate(
            [coarse, vector - coarse, dipole[...].astype(F32), jnp.zeros((7, cols), F32)], axis=0
        ).astype(BF16)
        for i in range(rb):
            got = lax.dot_general(
                stack, panel[me, i * BLOCK : (i + 1) * BLOCK, :], (((1,), (1,)), ((), ())),
                preferred_element_type=F32,
            )
            weigh = COUPLE * potential[pl.ds(row * rb + i, 1), :]
            inner2 = got[0:3, :] + got[3:6, :] + weigh * got[6:9, :]
            low_u[i] = jnp.concatenate([inner2, jnp.zeros((1, BLOCK), F32)], axis=0)
        local = jnp.concatenate(low_u, axis=0)
        field1[0] = local
        for du in range(1, n_sub):
            started.append(
                send(field1.at[0], field1.at[du], g_send.at[du], g_recv.at[du], peer(0, du))
            )
        for du in range(1, n_sub):
            arrived(field1.at[du], g_recv.at[du])
            local = local + field1[du]
        field[0] = local.astype(BF16)

        def tell(q, carry):
            remote(field.at[0], field.at[q], q_send, q_recv, chip(q)).start()
            return carry

        lax.fori_loop(1, n_chip, tell, 0)
        pass_on(0)
        lax.fori_loop(wt // 2, wt, pair_tile, 0)
        pass_on(1)

        pass_on(2)

        def unfold(dr, carry):
            r = lax.rem(row + n_row - dr, n_row)
            arrived(comp.at[r], s_recv.at[dr])
            expand(r)
            return carry

        lax.fori_loop(1, n_row, unfold, 0)
        pass_on(3)
        col_pot = jnp.concatenate(
            [potential[pl.ds(me * cb + j, 1), :] for j in range(cb)], axis=1
        )
        eye = (
            lax.broadcasted_iota(jnp.int32, (BLOCK, BLOCK), 0)
            == lax.broadcasted_iota(jnp.int32, (BLOCK, BLOCK), 1)
        )

        def product(k, _):
            at = pl.ds(pl.multiple_of(k * step, step), step)
            total = jnp.zeros((step, cols), F32)
            for dc in range(n_col):
                for du in range(n_sub):
                    slot = source(dc, du)
                    if du > 0:
                        arrived(panel.at[slot, at], d_recv.at[dc, du, k])
                    depth = pl.ds(pl.multiple_of(slot * cols, cols), cols)
                    total = total + jnp.dot(
                        panel[slot, at, :], full[depth, :], preferred_element_type=F32
                    )
            line = potential[pl.ds(row * rb + k, 1), :]
            row_pot = jnp.sum(jnp.where(eye, line, 0.0), axis=1, keepdims=True)
            mine = panel[me, at, :].astype(F32)
            coupled[at, :] = (total + COUPLE * (row_pot + col_pot) * mine).astype(BF16)
            return 0

        lax.fori_loop(0, CHUNKS, product, 0)

        arrived(field.at[pl.ds(1, n_chip - 1)], q_recv)
        small[8].wait()
        small[9].wait()
        for dr in range(n_row):
            total = field[dr * n_col].astype(F32)
            for m in range(1, n_col):
                total = total + field[dr * n_col + m].astype(F32)
            sums[lax.rem(row + n_row - dr, n_row)] = total

        forces = []
        for a in range(3):
            own = dense(owner, a)
            low, high = own & (BLOCK - 1), own >> 7
            value = [jnp.zeros((wt, BLOCK), F32)] * 3
            for h in range(nb):
                hit = high == h
                at = 4 * (h % rb)
                for c in range(3):
                    value[c] = jnp.where(
                        hit, lookup(sums[h // rb, at + c : at + c + 1, :], low), value[c]
                    )
            forces.append([force[3 * a + c] + CHARGE[a] * value[c] for c in range(3)])
        cent = [dense(centres, c) for c in range(3)]
        quat = [quats[c] for c in range(4)]
        torque = [jnp.zeros((wt, BLOCK), F32)] * 3
        for a in range(3):
            lever = [table[3 * a + c] - cent[c] for c in range(3)]
            turn = cross(lever, forces[a])
            torque = [torque[c] + turn[c] for c in range(3)]
        omega = []
        for c in range(3):
            pull = forces[0][c] + forces[1][c] + forces[2][c]
            fast = dense(velocity, c) + STEP_DT * pull / WATER_MASS
            spread(velocity_new, c, fast)
            spread(centres_new, c, cent[c] + STEP_DT * fast)
            spin = dense(angmom, c) + STEP_DT * torque[c]
            spread(angmom_new, c, spin)
            omega.append(spin / INERTIA)
        vector = quat[1:4]
        delta = [-(omega[0] * vector[0] + omega[1] * vector[1] + omega[2] * vector[2])]
        turn = cross(omega, vector)
        delta += [quat[0] * omega[c] + turn[c] for c in range(3)]
        moved = [quat[c] + 0.5 * STEP_DT * delta[c] for c in range(4)]
        length = jnp.sqrt(sum(m * m for m in moved))
        for c in range(4):
            spread(orient_new, c, moved[c] / length)

        arrived(hist.at[pl.ds(1, n_chip - 1)], h_send)
        arrived(field.at[pl.ds(1, n_chip - 1)], q_send)
        pl.when(target != me)(lambda: pass_inner(0).wait_send())
        for dr in range(1, n_row):
            pass_inner(dr).wait_send()
        for copy in started:
            copy.wait_send()

    hbm = pl.BlockSpec(memory_space=pltpu.HBM)
    vmem = pl.BlockSpec(memory_space=pltpu.VMEM)
    dma = lambda *s: pltpu.SemaphoreType.DMA(s)
    one = pltpu.SemaphoreType.DMA(())
    call = pl.pallas_call(
        kernel,
        out_shape=(
            pltpu.VMEM((rows, cols), BF16),
            pltpu.VMEM((3, waters), F32),
            pltpu.VMEM((3, waters), F32),
            pltpu.VMEM((3, waters), F32),
            pltpu.VMEM((4, waters), F32),
        ),
        in_specs=[hbm] * 12,
        out_specs=(vmem,) * 5,
        scratch_shapes=[
            pltpu.VMEM((rows, cols), BF16),
            pltpu.VMEM((rows, cols), BF16),
            pltpu.SMEM((rb, cb), jnp.int32),
            pltpu.SMEM((rb, cb), jnp.int32),
            pltpu.VMEM((3, cols), BF16),
            pltpu.VMEM((3, waters), jnp.int32),
            pltpu.VMEM((3, waters), F32),
            pltpu.VMEM((3, waters), F32),
            pltpu.VMEM((3, waters), F32),
            pltpu.VMEM((3, waters), F32),
            pltpu.VMEM((2, halo), jnp.int32),
            pltpu.VMEM((neigh, waters), jnp.int32),
            pltpu.VMEM((n_m, rows, cols), BF16),
            pltpu.VMEM((n_row, rows + rb * cb, BLOCK), BF16),
            pltpu.VMEM((order, cols), BF16),
            pltpu.VMEM((n_chip, nb, BLOCK), jnp.int16),
            pltpu.VMEM((rb * 4, BLOCK), F32),
            pltpu.VMEM((wide, n_m, rb * 4, BLOCK), F32),
            pltpu.VMEM((n_chip, rb * 4, BLOCK), BF16),
            pltpu.VMEM((2, 24, BLOCK), F32),
            pltpu.VMEM((2, 24, BLOCK), F32),
            pltpu.VMEM((9, wt, BLOCK), F32),
            pltpu.VMEM((9, wt, BLOCK), F32),
            pltpu.VMEM((4, wt, BLOCK), F32),
            pltpu.VMEM((nb, BLOCK), F32),
            pltpu.VMEM((n_row, rb * 4, BLOCK), F32),
            pltpu.VMEM((n_sub, nb, BLOCK), jnp.int16),
            pltpu.VMEM((n_sub, rb * 4, BLOCK), F32),
            dma(11), dma(CHUNKS),
            dma(n_col, n_sub, CHUNKS), dma(n_col, n_sub, CHUNKS), dma(n_col, n_sub, CHUNKS),
            dma(n_row), dma(n_row), one, one, dma(n_row), dma(wide, n_m),
            one, one, dma(2), dma(2), dma(n_sub), dma(n_sub), dma(n_sub), dma(n_sub),
        ],
        compiler_params=pltpu.CompilerParams(
            collective_id=0, has_side_effects=True, vmem_limit_bytes=48 << 20
        ),
    )
    return call


def deliver(results):
    count = len(results)

    def kernel(*refs):
        sem = refs[2 * count]
        stores = [
            pltpu.make_async_copy(refs[n], refs[count + n], sem.at[n]) for n in range(count)
        ]
        for store in stores:
            store.start()
        for store in stores:
            store.wait()

    return pl.pallas_call(
        kernel,
        out_shape=tuple(jax.ShapeDtypeStruct(r.shape, r.dtype) for r in results),
        in_specs=[pl.BlockSpec(memory_space=pltpu.VMEM)] * count,
        out_specs=(pl.BlockSpec(memory_space=pltpu.HBM),) * count,
        scratch_shapes=[pltpu.SemaphoreType.DMA((count,))],
    )(*[pltpu.with_memory_space_constraint(r, pltpu.VMEM) for r in results])


def solution(mesh):
    n_row, n_col, n_sub = mesh.shape["row"], mesh.shape["col"], mesh.shape["sub"]

    def shards(density, margin, pattern_d, pattern_s, dipole, owner, centres, angles,
               velocity, angmom, halo_list, neighbours):
        call = make_kernel(
            n_row, n_col, n_sub, density.shape[0], density.shape[1], owner.shape[1],
            neighbours.shape[0], halo_list.shape[1],
        )
        return deliver(
            call(*[
                pltpu.with_memory_space_constraint(x, pltpu.HBM)
                for x in (density, margin, pattern_d, pattern_s, dipole, owner, centres,
                          angles, velocity, angmom, halo_list, neighbours)
            ])
        )

    block = P(("groups", "row"), ("col", "sub"))
    water = P(None, ("groups", "row", "col", "sub"))
    return jax.shard_map(
        shards,
        mesh=mesh,
        in_specs=(block,) * 4 + (P(None, ("groups", "col", "sub")),) + (water,) * 7,
        out_specs=(block,) + (water,) * 4,
        check_vma=False,
    )
```

```python
import jax
import jax.numpy as jnp
from jax import lax
from jax.experimental import pallas as pl
from jax.experimental.pallas import tpu as pltpu
from jax.sharding import PartitionSpec as P

BLOCK = 128
UNIT = 0.417
OFFSET = ((0.0, 0.0, -0.12), (0.76, 0.0, 0.47), (-0.76, 0.0, 0.47))
WEIGHT = (-2.0, 1.0, 1.0)
CHARGE = (-0.834, 0.417, 0.417)
COUPLE = 0.1
STEP_DT = 0.5
WATER_MASS = 1.0
INERTIA = 0.5
SOFTEN = 1.0
CHUNKS = 4
SPLIT = 2
F32 = jnp.float32
BF16 = jnp.bfloat16


def lookup(row, low):
    return jnp.take_along_axis(
        jnp.broadcast_to(row, low.shape), low, axis=1, mode="promise_in_bounds"
    )


def dense(ref, compo):
    count = ref.shape[1] // BLOCK
    return jnp.concatenate(
        [ref[compo : compo + 1, j * BLOCK : (j + 1) * BLOCK] for j in range(count)], axis=0
    )


def spread(ref, compo, value):
    for j in range(ref.shape[1] // BLOCK):
        ref[compo : compo + 1, j * BLOCK : (j + 1) * BLOCK] = value[j : j + 1, :]


def cross(a, b):
    return (
        a[1] * b[2] - a[2] * b[1],
        a[2] * b[0] - a[0] * b[2],
        a[0] * b[1] - a[1] * b[0],
    )


def quaternion(angles):
    cos_r, cos_p, cos_y = [jnp.cos(0.5 * a) for a in angles]
    sin_r, sin_p, sin_y = [jnp.sin(0.5 * a) for a in angles]
    return (
        cos_r * cos_p * cos_y + sin_r * sin_p * sin_y,
        sin_r * cos_p * cos_y - cos_r * sin_p * sin_y,
        cos_r * sin_p * cos_y + sin_r * cos_p * sin_y,
        cos_r * cos_p * sin_y - sin_r * sin_p * cos_y,
    )


def rotation(quat):
    w, x, y, z = quat
    return (
        (1.0 - 2.0 * (y * y + z * z), 2.0 * (x * y - w * z), 2.0 * (x * z + w * y)),
        (2.0 * (x * y + w * z), 1.0 - 2.0 * (x * x + z * z), 2.0 * (y * z - w * x)),
        (2.0 * (x * z - w * y), 2.0 * (y * z + w * x), 1.0 - 2.0 * (x * x + y * y)),
    )


def make_kernel(n_row, n_col, n_sub, rows, cols, waters, neigh, halo):
    n_m = n_col * n_sub
    n_all = n_row * n_m
    n_chip = n_row * n_col
    order = rows * n_row
    rb, cb, nb = rows // BLOCK, cols // BLOCK, order // BLOCK
    wt, nh = waters // BLOCK, halo // BLOCK
    wide = cols // rows
    step = rows // CHUNKS
    hr = 9 * nh

    def kernel(
        density_hbm, margin_hbm, pat_d_hbm, pat_s_hbm, dipole_hbm, owner_hbm, centres_hbm,
        angles_hbm, velocity_hbm, angmom_hbm, halo_list_hbm, neighbours_hbm,
        coupled, centres_new, velocity_new, angmom_new, orient_new,
        density, margin, pat_d, pat_s, dipole, owner, centres,
        angles, velocity, angmom, halo_list, neighbours,
        panel, comp, full, total_out, picked, hist, inner, parts, field, halo_out, halo_in,
        table, force, quats, potential, sums, hist1, field1,
        l_sem, c_sem, d_send, d_recv, f_send, s_send, s_recv, h_send, h_recv, v_send, v_recv,
        q_send, q_recv, e_send, e_recv, row_ready, all_ready, i_send, i_recv, g_send, g_recv,
    ):
        row, col, sub = lax.axis_index("row"), lax.axis_index("col"), lax.axis_index("sub")
        me = col * n_sub + sub

        def peer(dc, du):
            return {"col": lax.rem(col + dc, n_col), "sub": lax.rem(sub + du, n_sub)}

        def peer_row(dr):
            return {"row": lax.rem(row + dr, n_row)}

        def other(q):
            dr, dm = lax.div(q, n_m), lax.rem(q, n_m)
            return {
                "row": lax.rem(row + dr, n_row),
                "col": lax.rem(col + lax.div(dm, n_sub), n_col),
                "sub": lax.rem(sub + lax.rem(dm, n_sub), n_sub),
            }

        def chip(q):
            return {
                "row": lax.rem(row + lax.div(q, n_col), n_row),
                "col": lax.rem(col + lax.rem(q, n_col), n_col),
            }

        def source(dc, du):
            return (
                lax.rem(col + n_col - dc, n_col) * n_sub + lax.rem(sub + n_sub - du, n_sub)
            )

        started = []

        def remote(src, dst, ssem, rsem, dev):
            return pltpu.make_async_remote_copy(
                src_ref=src, dst_ref=dst, send_sem=ssem, recv_sem=rsem,
                device_id=dev, device_id_type=pl.DeviceIdType.MESH,
            )

        def send(src, dst, ssem, rsem, dev):
            copy = remote(src, dst, ssem, rsem, dev)
            copy.start()
            return copy

        def arrived(ref, sem):
            pltpu.make_async_copy(ref, ref, sem).wait()

        barrier = pltpu.get_barrier_semaphore()

        def greet(dev):
            pl.semaphore_signal(
                barrier, inc=1, device_id=dev, device_id_type=pl.DeviceIdType.MESH
            )

        near, far = 0, n_sub - 1

        def greet_near(q, carry):
            greet({"col": lax.rem(col + q, n_col), "sub": near})
            return carry

        def greet_far(q, carry):
            greet({
                "row": lax.rem(row + lax.div(q, n_col), n_row),
                "col": lax.rem(col + lax.rem(q, n_col), n_col), "sub": far,
            })
            return carry

        def in_row():
            @pl.when(sub == near)
            def _():
                pl.semaphore_wait(barrier, n_m - 1)
                for du in range(1, n_sub):
                    pl.semaphore_signal(
                        row_ready, inc=1, device_id=peer(0, du),
                        device_id_type=pl.DeviceIdType.MESH,
                    )

            pl.when(sub != near)(lambda: pl.semaphore_wait(row_ready, 1))

        def in_all():
            @pl.when(sub == far)
            def _():
                pl.semaphore_wait(barrier, n_all - n_m)
                for du in range(1, n_sub):
                    pl.semaphore_signal(
                        all_ready, inc=1, device_id=peer(0, du),
                        device_id_type=pl.DeviceIdType.MESH,
                    )

            pl.when(sub != far)(lambda: pl.semaphore_wait(all_ready, 1))

        small = [
            pltpu.make_async_copy(src, dst, l_sem.at[n])
            for n, (src, dst) in enumerate((
                (pat_d_hbm, pat_d), (pat_s_hbm, pat_s), (dipole_hbm, dipole),
                (owner_hbm, owner), (angles_hbm, angles), (centres_hbm, centres),
                (halo_list_hbm, halo_list), (neighbours_hbm, neighbours),
                (velocity_hbm, velocity), (angmom_hbm, angmom), (margin_hbm, margin),
            ))
        ]
        loads = [
            pltpu.make_async_copy(
                density_hbm.at[pl.ds(k * step, step)], density.at[pl.ds(k * step, step)],
                c_sem.at[k],
            )
            for k in range(CHUNKS)
        ]
        small[0].start()
        loads[0].start()
        for load in loads[1:]:
            load.start()
        small[10].start()
        for load in small[1:10]:
            load.start()
        lax.fori_loop(1, n_col, greet_near, 0)
        pl.when(sub != near)(lambda: greet({"sub": near}))
        lax.fori_loop(n_col, n_chip, greet_far, 0)

        small[0].wait()
        for k in range(CHUNKS):
            loads[k].wait()
            for i in range(k * step // BLOCK, (k + 1) * step // BLOCK):
                at = slice(i * BLOCK, (i + 1) * BLOCK)
                for j in range(cb):
                    ac = slice(j * BLOCK, (j + 1) * BLOCK)
                    factor = pat_d[i, j].astype(F32)
                    panel[me, at, ac] = (density[at, ac].astype(F32) * factor).astype(BF16)
        in_row()
        def panel_copy(dc, k):
            at = panel.at[me, pl.ds(k * step, step)]
            return remote(at, at, d_send.at[dc, 0, k], d_recv.at[dc, 0, k], peer(dc, 0))

        rank = jnp.minimum(row, 2)

        def send_panels(first, end):
            for k in range(CHUNKS):
                @pl.when(jnp.logical_and(k + rank >= first, k + rank < end))
                def _(k=k):
                    for dc in range(1, n_col):
                        panel_copy(dc, k).start()

        send_panels(0, 2)
        for k in range(CHUNKS):
            at = pl.ds(k * step, step)
            for du in range(1, n_sub):
                started.append(
                    send(panel.at[me, at], panel.at[me, at], d_send.at[0, du, k],
                         d_recv.at[0, du, k], peer(0, du))
                )

        small[1].wait()
        small[2].wait()
        small[10].wait()
        low_u = []
        for i in range(rb):
            at = slice(i * BLOCK, (i + 1) * BLOCK)
            total, chosen = None, None
            for j in range(cb):
                ac = slice(j * BLOCK, (j + 1) * BLOCK)
                factor = pat_s[i, j].astype(F32)
                term = margin[at, ac].astype(F32) * factor
                dip = dipole[:, ac].astype(F32) * factor
                total = term if total is None else total + term
                chosen = dip if chosen is None else chosen + dip
            tile = total.astype(BF16)
            comp[row, at, :] = tile
            low_u.append(
                lax.dot_general(
                    chosen.astype(BF16), tile, (((1,), (1,)), ((), ())),
                    preferred_element_type=F32,
                )
            )
        for base in range(0, rb * cb, 16):
            comp[row, rows + base : rows + base + 16, :] = jnp.concatenate(
                [
                    jnp.full((1, BLOCK), pat_s[q // cb, q % cb].astype(F32), F32)
                    for q in range(base, base + 16)
                ],
                axis=0,
            ).astype(BF16)
        target, lane = lax.div(row, wide), lax.rem(row, wide)
        for i in range(rb):
            inner[4 * i : 4 * i + 3, :] = low_u[i]
            inner[4 * i + 3 : 4 * i + 4, :] = low_u[i][0:1, :]

        small[3].wait()
        lane_ids = lax.broadcasted_iota(jnp.int32, (BLOCK, waters), 0)
        high_ids = lax.broadcasted_iota(jnp.int32, (nb, waters), 0)
        counts = jnp.zeros((nb, BLOCK), F32)
        for site in range(3):
            own = owner[site : site + 1, :]
            low_hot = jnp.where(lane_ids == (own & (BLOCK - 1)), 1.0, 0.0).astype(BF16)
            high_hot = jnp.where(high_ids == (own >> 7), WEIGHT[site], 0.0).astype(BF16)
            counts = counts + lax.dot_general(
                high_hot, low_hot, (((1,), (1,)), ((), ())), preferred_element_type=F32
            )
        hist1[0] = counts.astype(jnp.int32).astype(jnp.int16)
        for du in range(1, n_sub):
            started.append(
                send(hist1.at[0], hist1.at[du], i_send.at[du], i_recv.at[du], peer(0, du))
            )

        for load in small[4:8]:
            load.wait()
        cent = [dense(centres, c) for c in range(3)]
        quat = quaternion([dense(angles, c) for c in range(3)])
        for c in range(4):
            quats[c] = quat[c]
        matrix = rotation(quat)
        for a in range(3):
            for c in range(3):
                table[3 * a + c] = (
                    cent[c]
                    + matrix[c][0] * OFFSET[a][0]
                    + matrix[c][1] * OFFSET[a][1]
                    + matrix[c][2] * OFFSET[a][2]
                )
        listed = [
            halo_list[side : side + 1, j * BLOCK : (j + 1) * BLOCK]
            for side in range(2) for j in range(nh)
        ]
        picks = jnp.concatenate(listed + [listed[0]] * (8 - len(listed)), axis=0)
        low, high = picks & (BLOCK - 1), picks >> 7
        for t in range(9):
            value = lookup(table[t, 0:1, :], low)
            for h in range(1, wt):
                value = jnp.where(high == h, lookup(table[t, h : h + 1, :], low), value)
            for side in range(2):
                halo_out[side, t * nh : (t + 1) * nh, :] = value[side * nh : (side + 1) * nh, :]
        in_all()

        def pass_inner(dr):
            there = peer_row(dr)
            there["col"], there["sub"] = lax.div(target, n_sub), lax.rem(target, n_sub)
            return remote(
                inner, parts.at[lane, me], v_send.at[dr], v_recv.at[lane, me], there
            )

        @pl.when(target == me)
        def _():
            parts[lane, me] = inner[...]

        pl.when(target != me)(lambda: pass_inner(0).start())
        for dr in range(1, n_row):
            pass_inner(dr).start()
        for side, by in ((0, 1), (1, n_row - 1)):
            started.append(
                send(halo_out.at[side], halo_in.at[side], e_send.at[side], e_recv.at[side],
                     peer_row(by))
            )
        total = hist1[0].astype(jnp.int32)
        for du in range(1, n_sub):
            arrived(hist1.at[du], i_recv.at[du])
            total = total + hist1[du].astype(jnp.int32)
        hist[0] = total.astype(jnp.int16)

        def share(q, carry):
            remote(hist.at[0], hist.at[q], h_send, h_recv, chip(q)).start()
            return carry

        lax.fori_loop(1, n_chip, share, 0)

        def pass_block(to):
            return remote(
                comp.at[row], comp.at[row], s_send.at[to], s_recv.at[row], {"row": to}
            )

        upper = lax.div(row, n_row // 2)
        inner_row = n_row // 2 - upper

        def pass_blocks(early):
            for to in range(n_row):
                held = to == inner_row
                go = jnp.logical_not(held) if early else held
                pl.when(jnp.logical_and(row != to, go))(lambda to=to: pass_block(to).start())

        pass_blocks(True)
        send_panels(2, 6)
        def expand(r):
            marks = comp[r, rows : rows + rb * cb, :].astype(F32)
            for i in range(rb):
                tile = comp[r, i * BLOCK : (i + 1) * BLOCK, :].astype(F32)
                at = slice(i * BLOCK, (i + 1) * BLOCK)
                for j in range(cb):
                    q = i * cb + j
                    full[at, j * BLOCK : (j + 1) * BLOCK] = (tile * marks[q : q + 1, :]).astype(BF16)

        def pass_on(k):
            at = pl.ds(k * step, step)
            for dc in range(1, n_col):
                slot = source(dc, 0)
                arrived(panel.at[slot, at], d_recv.at[dc, 0, k])
                for du in range(1, n_sub):
                    started.append(
                        send(panel.at[slot, at], panel.at[slot, at], f_send.at[dc, du, k],
                             d_recv.at[dc, du, k], peer(0, du))
                    )

        def pick_own(j, carry):
            lanes = pl.ds(pl.multiple_of(j * BLOCK, BLOCK), BLOCK)
            for s in range(neigh // 8):
                idx = neighbours[8 * s : 8 * s + 8, lanes]
                low, high = idx & (BLOCK - 1), idx >> 7
                part = [lookup(table[t, 0:1, :], low) for t in range(9)]
                for h in range(1, wt):
                    hit = high == h
                    for t in range(9):
                        part[t] = jnp.where(hit, lookup(table[t, h : h + 1, :], low), part[t])
                for t in range(9):
                    picked[j, s, t] = part[t]
            return carry

        def pair_tile(j, carry):
            lanes = pl.ds(pl.multiple_of(j * BLOCK, BLOCK), BLOCK)
            own = [jnp.broadcast_to(table[t, pl.ds(j, 1), :], (8, BLOCK)) for t in range(9)]
            totals = [jnp.zeros((8, BLOCK), F32) for _ in range(9)]
            for s in range(neigh // 8):
                idx = neighbours[8 * s : 8 * s + 8, lanes]
                low, high = idx & (BLOCK - 1), idx >> 7
                part = [picked[j, s, t] for t in range(9)]
                for h in range(wt, wt + 2 * nh):
                    hit = high == h
                    side, at = (h - wt) // nh, (h - wt) % nh
                    for t in range(9):
                        line = halo_in[side, t * nh + at : t * nh + at + 1, :]
                        part[t] = jnp.where(hit, lookup(line, low), part[t])
                for a in range(3):
                    for b in range(3):
                        d = [own[3 * a + c] - part[3 * b + c] for c in range(3)]
                        inv = lax.rsqrt(d[0] * d[0] + d[1] * d[1] + d[2] * d[2] + SOFTEN)
                        weight = (CHARGE[a] * CHARGE[b]) * (inv * inv * inv)
                        for c in range(3):
                            totals[3 * a + c] = totals[3 * a + c] + d[c] * weight
            for t in range(9):
                force[t, pl.ds(j, 1), :] = jnp.sum(totals[t], axis=0, keepdims=True)
            return carry

        lax.fori_loop(0, wt, pick_own, 0)

        arrived(hist.at[pl.ds(1, n_chip - 1)], h_recv)
        counts = lax.fori_loop(
            1, n_chip, lambda q, c: c + hist[q].astype(jnp.int32), hist[0].astype(jnp.int32)
        )
        potential[...] = counts.astype(F32) * UNIT
        for s in range(wide):
            for m in range(n_m):
                is_own = jnp.logical_and(target == me, jnp.logical_and(lane == s, me == m))
                pl.when(jnp.logical_not(is_own))(
                    lambda s=s, m=m: arrived(parts.at[s, m], v_recv.at[s, m])
                )
        lines = [[], [], []]
        for s in range(wide):
            total = parts[s, 0]
            for m in range(1, n_m):
                total = total + parts[s, m]
            for i in range(rb):
                j = s * rb + i
                weigh = COUPLE * potential[pl.ds(me * cb + j, 1), :]
                dip = dipole[:, j * BLOCK : (j + 1) * BLOCK].astype(F32)
                for c in range(3):
                    lines[c].append(total[4 * i + c : 4 * i + c + 1, :] + weigh * dip[c : c + 1, :])
        vector = jnp.concatenate([jnp.concatenate(line, axis=1) for line in lines], axis=0)
        coarse = vector.astype(BF16).astype(F32)
        stack = jnp.concatenate(
            [coarse, vector - coarse, dipole[...].astype(F32), jnp.zeros((7, cols), F32)], axis=0
        ).astype(BF16)
        for i in range(rb):
            got = lax.dot_general(
                stack, panel[me, i * BLOCK : (i + 1) * BLOCK, :], (((1,), (1,)), ((), ())),
                preferred_element_type=F32,
            )
            weigh = COUPLE * potential[pl.ds(row * rb + i, 1), :]
            inner2 = got[0:3, :] + got[3:6, :] + weigh * got[6:9, :]
            low_u[i] = jnp.concatenate([inner2, jnp.zeros((1, BLOCK), F32)], axis=0)
        local = jnp.concatenate(low_u, axis=0)
        field1[0] = local
        for du in range(1, n_sub):
            started.append(
                send(field1.at[0], field1.at[du], g_send.at[du], g_recv.at[du], peer(0, du))
            )
        for side in range(2):
            arrived(halo_in.at[side], e_recv.at[side])
        lax.fori_loop(0, wt // 4, pair_tile, 0)
        for du in range(1, n_sub):
            arrived(field1.at[du], g_recv.at[du])
            local = local + field1[du]
        field[0] = local.astype(BF16)

        def tell(q, carry):
            remote(field.at[0], field.at[q], q_send, q_recv, chip(q)).start()
            return carry

        lax.fori_loop(1, n_chip, tell, 0)
        pass_blocks(False)
        send_panels(6, CHUNKS + 2)
        pass_on(0)
        lax.fori_loop(wt // 4, wt, pair_tile, 0)
        pass_on(1)

        col_pot = jnp.concatenate(
            [potential[pl.ds(me * cb + j, 1), :] for j in range(cb)], axis=1
        )
        eye = (
            lax.broadcasted_iota(jnp.int32, (BLOCK, BLOCK), 0)
            == lax.broadcasted_iota(jnp.int32, (BLOCK, BLOCK), 1)
        )

        def term(r, at):
            depth = pl.ds(pl.multiple_of(lax.rem(r, wide) * rows, rows), rows)
            return jnp.dot(
                panel[lax.div(r, wide), at, depth], full[...], preferred_element_type=F32
            )

        def source_row(t):
            return t - 1 + lax.div(t - 1 + n_row - row, n_row)

        def block(r):
            arrived(comp.at[r], s_recv.at[r])
            expand(r)

        pass_on(2)
        pass_on(3)
        for dc in range(n_col):
            for du in range(1, n_sub):
                for k in range(CHUNKS):
                    at = pl.ds(k * step, step)
                    arrived(panel.at[source(dc, du), at], d_recv.at[dc, du, k])
        parts_of = [slice(k * rows // SPLIT, (k + 1) * rows // SPLIT) for k in range(SPLIT)]
        expand(row)
        for at in parts_of:
            total_out[at, :] = term(row, at)

        def add_block(t, carry):
            r = source_row(t)
            block(r)
            for at in parts_of:
                total_out[at, :] += term(r, at)
            return carry

        lax.fori_loop(1, n_row - 1, add_block, 0)
        last = source_row(n_row - 1)
        block(last)
        for k in range(rb):
            at = slice(k * BLOCK, (k + 1) * BLOCK)
            line = potential[pl.ds(row * rb + k, 1), :]
            row_pot = jnp.sum(jnp.where(eye, line, 0.0), axis=1, keepdims=True)
            mine = panel[me, at, :].astype(F32)
            coupled[at, :] = (
                total_out[at, :] + term(last, at) + COUPLE * (row_pot + col_pot) * mine
            ).astype(BF16)

        arrived(field.at[pl.ds(1, n_chip - 1)], q_recv)
        small[8].wait()
        small[9].wait()
        for dr in range(n_row):
            total = field[dr * n_col].astype(F32)
            for m in range(1, n_col):
                total = total + field[dr * n_col + m].astype(F32)
            sums[lax.rem(row + n_row - dr, n_row)] = total

        forces = []
        for a in range(3):
            own = dense(owner, a)
            low, high = own & (BLOCK - 1), own >> 7
            value = [jnp.zeros((wt, BLOCK), F32)] * 3
            for h in range(nb):
                hit = high == h
                at = 4 * (h % rb)
                for c in range(3):
                    value[c] = jnp.where(
                        hit, lookup(sums[h // rb, at + c : at + c + 1, :], low), value[c]
                    )
            forces.append([force[3 * a + c] + CHARGE[a] * value[c] for c in range(3)])
        cent = [dense(centres, c) for c in range(3)]
        quat = [quats[c] for c in range(4)]
        torque = [jnp.zeros((wt, BLOCK), F32)] * 3
        for a in range(3):
            lever = [table[3 * a + c] - cent[c] for c in range(3)]
            turn = cross(lever, forces[a])
            torque = [torque[c] + turn[c] for c in range(3)]
        omega = []
        for c in range(3):
            pull = forces[0][c] + forces[1][c] + forces[2][c]
            fast = dense(velocity, c) + STEP_DT * pull / WATER_MASS
            spread(velocity_new, c, fast)
            spread(centres_new, c, cent[c] + STEP_DT * fast)
            spin = dense(angmom, c) + STEP_DT * torque[c]
            spread(angmom_new, c, spin)
            omega.append(spin / INERTIA)
        vector = quat[1:4]
        delta = [-(omega[0] * vector[0] + omega[1] * vector[1] + omega[2] * vector[2])]
        turn = cross(omega, vector)
        delta += [quat[0] * omega[c] + turn[c] for c in range(3)]
        moved = [quat[c] + 0.5 * STEP_DT * delta[c] for c in range(4)]
        length = jnp.sqrt(sum(m * m for m in moved))
        for c in range(4):
            spread(orient_new, c, moved[c] / length)

        arrived(hist.at[pl.ds(1, n_chip - 1)], h_send)
        arrived(field.at[pl.ds(1, n_chip - 1)], q_send)
        pl.when(target != me)(lambda: pass_inner(0).wait_send())
        for dr in range(1, n_row):
            pass_inner(dr).wait_send()
        for to in range(n_row):
            pl.when(row != to)(lambda to=to: pass_block(to).wait_send())
        for dc in range(1, n_col):
            for k in range(CHUNKS):
                panel_copy(dc, k).wait_send()
        for copy in started:
            copy.wait_send()

    hbm = pl.BlockSpec(memory_space=pltpu.HBM)
    vmem = pl.BlockSpec(memory_space=pltpu.VMEM)
    dma = lambda *s: pltpu.SemaphoreType.DMA(s)
    one = pltpu.SemaphoreType.DMA(())
    call = pl.pallas_call(
        kernel,
        out_shape=(
            pltpu.VMEM((rows, cols), BF16),
            pltpu.VMEM((3, waters), F32),
            pltpu.VMEM((3, waters), F32),
            pltpu.VMEM((3, waters), F32),
            pltpu.VMEM((4, waters), F32),
        ),
        in_specs=[hbm] * 12,
        out_specs=(vmem,) * 5,
        scratch_shapes=[
            pltpu.VMEM((rows, cols), BF16),
            pltpu.VMEM((rows, cols), BF16),
            pltpu.SMEM((rb, cb), jnp.int32),
            pltpu.SMEM((rb, cb), jnp.int32),
            pltpu.VMEM((3, cols), BF16),
            pltpu.VMEM((3, waters), jnp.int32),
            pltpu.VMEM((3, waters), F32),
            pltpu.VMEM((3, waters), F32),
            pltpu.VMEM((3, waters), F32),
            pltpu.VMEM((3, waters), F32),
            pltpu.VMEM((2, halo), jnp.int32),
            pltpu.VMEM((neigh, waters), jnp.int32),
            pltpu.VMEM((n_m, rows, cols), BF16),
            pltpu.VMEM((n_row, rows + rb * cb, BLOCK), BF16),
            pltpu.VMEM((rows, cols), BF16),
            pltpu.VMEM((rows, cols), F32),
            pltpu.VMEM((wt, neigh // 8, 9, 8, BLOCK), F32),
            pltpu.VMEM((n_chip, nb, BLOCK), jnp.int16),
            pltpu.VMEM((rb * 4, BLOCK), F32),
            pltpu.VMEM((wide, n_m, rb * 4, BLOCK), F32),
            pltpu.VMEM((n_chip, rb * 4, BLOCK), BF16),
            pltpu.VMEM((2, 24, BLOCK), F32),
            pltpu.VMEM((2, 24, BLOCK), F32),
            pltpu.VMEM((9, wt, BLOCK), F32),
            pltpu.VMEM((9, wt, BLOCK), F32),
            pltpu.VMEM((4, wt, BLOCK), F32),
            pltpu.VMEM((nb, BLOCK), F32),
            pltpu.VMEM((n_row, rb * 4, BLOCK), F32),
            pltpu.VMEM((n_sub, nb, BLOCK), jnp.int16),
            pltpu.VMEM((n_sub, rb * 4, BLOCK), F32),
            dma(11), dma(CHUNKS),
            dma(n_col, n_sub, CHUNKS), dma(n_col, n_sub, CHUNKS), dma(n_col, n_sub, CHUNKS),
            dma(n_row), dma(n_row), one, one, dma(n_row), dma(wide, n_m),
            one, one, dma(2), dma(2), pltpu.SemaphoreType.REGULAR, pltpu.SemaphoreType.REGULAR,
            dma(n_sub), dma(n_sub), dma(n_sub), dma(n_sub),
        ],
        compiler_params=pltpu.CompilerParams(
            collective_id=0, has_side_effects=True, vmem_limit_bytes=48 << 20
        ),
    )
    return call


def deliver(results):
    count = len(results)

    def kernel(*refs):
        sem = refs[2 * count]
        stores = [
            pltpu.make_async_copy(refs[n], refs[count + n], sem.at[n]) for n in range(count)
        ]
        for store in stores:
            store.start()
        for store in stores:
            store.wait()

    return pl.pallas_call(
        kernel,
        out_shape=tuple(jax.ShapeDtypeStruct(r.shape, r.dtype) for r in results),
        in_specs=[pl.BlockSpec(memory_space=pltpu.VMEM)] * count,
        out_specs=(pl.BlockSpec(memory_space=pltpu.HBM),) * count,
        scratch_shapes=[pltpu.SemaphoreType.DMA((count,))],
    )(*[pltpu.with_memory_space_constraint(r, pltpu.VMEM) for r in results])


def solution(mesh):
    n_row, n_col, n_sub = mesh.shape["row"], mesh.shape["col"], mesh.shape["sub"]

    def shards(density, margin, pattern_d, pattern_s, dipole, owner, centres, angles,
               velocity, angmom, halo_list, neighbours):
        call = make_kernel(
            n_row, n_col, n_sub, density.shape[0], density.shape[1], owner.shape[1],
            neighbours.shape[0], halo_list.shape[1],
        )
        return deliver(
            call(*[
                pltpu.with_memory_space_constraint(x, pltpu.HBM)
                for x in (density, margin, pattern_d, pattern_s, dipole, owner, centres,
                          angles, velocity, angmom, halo_list, neighbours)
            ])
        )

    block = P(("groups", "row"), ("col", "sub"))
    water = P(None, ("groups", "row", "col", "sub"))
    return jax.shard_map(
        shards,
        mesh=mesh,
        in_specs=(block,) * 4 + (P(None, ("groups", "col", "sub")),) + (water,) * 7,
        out_specs=(block,) + (water,) * 4,
        check_vma=False,
    )
```

```python
import jax
import jax.numpy as jnp
from jax import lax
from jax.experimental import pallas as pl
from jax.experimental.pallas import tpu as pltpu
from jax.sharding import PartitionSpec as P

BLOCK = 128
UNIT = 0.417
OFFSET = ((0.0, 0.0, -0.12), (0.76, 0.0, 0.47), (-0.76, 0.0, 0.47))
WEIGHT = (-2.0, 1.0, 1.0)
CHARGE = (-0.834, 0.417, 0.417)
COUPLE = 0.1
STEP_DT = 0.5
WATER_MASS = 1.0
INERTIA = 0.5
SOFTEN = 1.0
CHUNKS = 4
SPLIT = 2
F32 = jnp.float32
BF16 = jnp.bfloat16


def lookup(row, low):
    return jnp.take_along_axis(
        jnp.broadcast_to(row, low.shape), low, axis=1, mode="promise_in_bounds"
    )


def dense(ref, compo):
    count = ref.shape[1] // BLOCK
    return jnp.concatenate(
        [ref[compo : compo + 1, j * BLOCK : (j + 1) * BLOCK] for j in range(count)], axis=0
    )


def spread(ref, compo, value):
    for j in range(ref.shape[1] // BLOCK):
        ref[compo : compo + 1, j * BLOCK : (j + 1) * BLOCK] = value[j : j + 1, :]


def cross(a, b):
    return (
        a[1] * b[2] - a[2] * b[1],
        a[2] * b[0] - a[0] * b[2],
        a[0] * b[1] - a[1] * b[0],
    )


def quaternion(angles):
    cos_r, cos_p, cos_y = [jnp.cos(0.5 * a) for a in angles]
    sin_r, sin_p, sin_y = [jnp.sin(0.5 * a) for a in angles]
    return (
        cos_r * cos_p * cos_y + sin_r * sin_p * sin_y,
        sin_r * cos_p * cos_y - cos_r * sin_p * sin_y,
        cos_r * sin_p * cos_y + sin_r * cos_p * sin_y,
        cos_r * cos_p * sin_y - sin_r * sin_p * cos_y,
    )


def rotation(quat):
    w, x, y, z = quat
    return (
        (1.0 - 2.0 * (y * y + z * z), 2.0 * (x * y - w * z), 2.0 * (x * z + w * y)),
        (2.0 * (x * y + w * z), 1.0 - 2.0 * (x * x + z * z), 2.0 * (y * z - w * x)),
        (2.0 * (x * z - w * y), 2.0 * (y * z + w * x), 1.0 - 2.0 * (x * x + y * y)),
    )


def make_kernel(n_row, n_col, n_sub, rows, cols, waters, neigh, halo):
    n_m = n_col * n_sub
    n_all = n_row * n_m
    n_chip = n_row * n_col
    order = rows * n_row
    rb, cb, nb = rows // BLOCK, cols // BLOCK, order // BLOCK
    wt, nh = waters // BLOCK, halo // BLOCK
    wide = cols // rows
    step = rows // CHUNKS
    hr = 9 * nh

    def kernel(
        density_hbm, margin_hbm, pat_d_hbm, pat_s_hbm, dipole_hbm, owner_hbm, centres_hbm,
        angles_hbm, velocity_hbm, angmom_hbm, halo_list_hbm, neighbours_hbm,
        coupled, centres_new, velocity_new, angmom_new, orient_new,
        density, margin, pat_d, pat_s, dipole, owner, centres,
        angles, velocity, angmom, halo_list, neighbours,
        panel, comp, full, total_out, picked, hist, inner, parts, field, halo_out, halo_in,
        table, force, quats, potential, sums, hist1, field1,
        l_sem, c_sem, d_send, d_recv, f_send, s_send, s_recv, h_send, h_recv, v_send, v_recv,
        q_send, q_recv, e_send, e_recv, row_ready, all_ready, i_send, i_recv, g_send, g_recv,
    ):
        row, col, sub = lax.axis_index("row"), lax.axis_index("col"), lax.axis_index("sub")
        me = col * n_sub + sub

        def peer(dc, du):
            return {"col": lax.rem(col + dc, n_col), "sub": lax.rem(sub + du, n_sub)}

        def peer_row(dr):
            return {"row": lax.rem(row + dr, n_row)}

        def other(q):
            dr, dm = lax.div(q, n_m), lax.rem(q, n_m)
            return {
                "row": lax.rem(row + dr, n_row),
                "col": lax.rem(col + lax.div(dm, n_sub), n_col),
                "sub": lax.rem(sub + lax.rem(dm, n_sub), n_sub),
            }

        def chip(q):
            return {
                "row": lax.rem(row + lax.div(q, n_col), n_row),
                "col": lax.rem(col + lax.rem(q, n_col), n_col),
            }

        def source(dc, du):
            return (
                lax.rem(col + n_col - dc, n_col) * n_sub + lax.rem(sub + n_sub - du, n_sub)
            )

        started = []

        def remote(src, dst, ssem, rsem, dev):
            return pltpu.make_async_remote_copy(
                src_ref=src, dst_ref=dst, send_sem=ssem, recv_sem=rsem,
                device_id=dev, device_id_type=pl.DeviceIdType.MESH,
            )

        def send(src, dst, ssem, rsem, dev):
            copy = remote(src, dst, ssem, rsem, dev)
            copy.start()
            return copy

        def arrived(ref, sem):
            pltpu.make_async_copy(ref, ref, sem).wait()

        barrier = pltpu.get_barrier_semaphore()

        def greet(dev):
            pl.semaphore_signal(
                barrier, inc=1, device_id=dev, device_id_type=pl.DeviceIdType.MESH
            )

        near, far = 0, n_sub - 1

        def greet_near(q, carry):
            greet({"col": lax.rem(col + q, n_col), "sub": near})
            return carry

        def greet_far(q, carry):
            greet({
                "row": lax.rem(row + lax.div(q, n_col), n_row),
                "col": lax.rem(col + lax.rem(q, n_col), n_col), "sub": far,
            })
            return carry

        def in_row():
            @pl.when(sub == near)
            def _():
                pl.semaphore_wait(barrier, n_m - 1)
                for du in range(1, n_sub):
                    pl.semaphore_signal(
                        row_ready, inc=1, device_id=peer(0, du),
                        device_id_type=pl.DeviceIdType.MESH,
                    )

            pl.when(sub != near)(lambda: pl.semaphore_wait(row_ready, 1))

        def in_all():
            @pl.when(sub == far)
            def _():
                pl.semaphore_wait(barrier, n_all - n_m)
                for du in range(1, n_sub):
                    pl.semaphore_signal(
                        all_ready, inc=1, device_id=peer(0, du),
                        device_id_type=pl.DeviceIdType.MESH,
                    )

            pl.when(sub != far)(lambda: pl.semaphore_wait(all_ready, 1))

        small = [
            pltpu.make_async_copy(src, dst, l_sem.at[n])
            for n, (src, dst) in enumerate((
                (pat_d_hbm, pat_d), (pat_s_hbm, pat_s), (dipole_hbm, dipole),
                (owner_hbm, owner), (angles_hbm, angles), (centres_hbm, centres),
                (halo_list_hbm, halo_list), (neighbours_hbm, neighbours),
                (velocity_hbm, velocity), (angmom_hbm, angmom), (margin_hbm, margin),
            ))
        ]
        loads = [
            pltpu.make_async_copy(
                density_hbm.at[pl.ds(k * step, step)], density.at[pl.ds(k * step, step)],
                c_sem.at[k],
            )
            for k in range(CHUNKS)
        ]
        small[3].start()
        small[0].start()
        loads[0].start()
        for load in loads[1:]:
            load.start()
        small[10].start()
        for n in (1, 2, 4, 5, 6, 7, 8, 9):
            small[n].start()
        lax.fori_loop(1, n_col, greet_near, 0)
        pl.when(sub != near)(lambda: greet({"sub": near}))
        lax.fori_loop(n_col, n_chip, greet_far, 0)

        small[3].wait()
        lane_ids = lax.broadcasted_iota(jnp.int32, (BLOCK, waters), 0)
        high_ids = lax.broadcasted_iota(jnp.int32, (nb, waters), 0)
        counts = jnp.zeros((nb, BLOCK), F32)
        for site in range(3):
            own = owner[site : site + 1, :]
            low_hot = jnp.where(lane_ids == (own & (BLOCK - 1)), 1.0, 0.0).astype(BF16)
            high_hot = jnp.where(high_ids == (own >> 7), WEIGHT[site], 0.0).astype(BF16)
            counts = counts + lax.dot_general(
                high_hot, low_hot, (((1,), (1,)), ((), ())), preferred_element_type=F32
            )
        hist1[0] = counts.astype(jnp.int32).astype(jnp.int16)
        in_row()
        for du in range(1, n_sub):
            started.append(
                send(hist1.at[0], hist1.at[du], i_send.at[du], i_recv.at[du], peer(0, du))
            )

        small[0].wait()
        for k in range(CHUNKS):
            loads[k].wait()
            for i in range(k * step // BLOCK, (k + 1) * step // BLOCK):
                at = slice(i * BLOCK, (i + 1) * BLOCK)
                for j in range(cb):
                    ac = slice(j * BLOCK, (j + 1) * BLOCK)
                    factor = pat_d[i, j].astype(F32)
                    panel[me, at, ac] = (density[at, ac].astype(F32) * factor).astype(BF16)
        def panel_copy(dc, k):
            at = panel.at[me, pl.ds(k * step, step)]
            return remote(at, at, d_send.at[dc, 0, k], d_recv.at[dc, 0, k], peer(dc, 0))

        rank = jnp.minimum(row, 2)

        def send_panels(first, end):
            for k in range(CHUNKS):
                @pl.when(jnp.logical_and(k + rank >= first, k + rank < end))
                def _(k=k):
                    for dc in range(1, n_col):
                        panel_copy(dc, k).start()

        send_panels(0, 2)
        for k in range(CHUNKS):
            at = pl.ds(k * step, step)
            for du in range(1, n_sub):
                started.append(
                    send(panel.at[me, at], panel.at[me, at], d_send.at[0, du, k],
                         d_recv.at[0, du, k], peer(0, du))
                )

        small[1].wait()
        small[2].wait()
        small[10].wait()
        low_u = []
        for i in range(rb):
            at = slice(i * BLOCK, (i + 1) * BLOCK)
            total, chosen = None, None
            for j in range(cb):
                ac = slice(j * BLOCK, (j + 1) * BLOCK)
                factor = pat_s[i, j].astype(F32)
                term = margin[at, ac].astype(F32) * factor
                dip = dipole[:, ac].astype(F32) * factor
                total = term if total is None else total + term
                chosen = dip if chosen is None else chosen + dip
            tile = total.astype(BF16)
            comp[row, at, :] = tile
            low_u.append(
                lax.dot_general(
                    chosen.astype(BF16), tile, (((1,), (1,)), ((), ())),
                    preferred_element_type=F32,
                )
            )
        for base in range(0, rb * cb, 16):
            comp[row, rows + base : rows + base + 16, :] = jnp.concatenate(
                [
                    jnp.full((1, BLOCK), pat_s[q // cb, q % cb].astype(F32), F32)
                    for q in range(base, base + 16)
                ],
                axis=0,
            ).astype(BF16)
        target, lane = lax.div(row, wide), lax.rem(row, wide)
        for i in range(rb):
            inner[4 * i : 4 * i + 3, :] = low_u[i]
            inner[4 * i + 3 : 4 * i + 4, :] = low_u[i][0:1, :]

        for load in small[4:8]:
            load.wait()
        cent = [dense(centres, c) for c in range(3)]
        quat = quaternion([dense(angles, c) for c in range(3)])
        for c in range(4):
            quats[c] = quat[c]
        matrix = rotation(quat)
        for a in range(3):
            for c in range(3):
                table[3 * a + c] = (
                    cent[c]
                    + matrix[c][0] * OFFSET[a][0]
                    + matrix[c][1] * OFFSET[a][1]
                    + matrix[c][2] * OFFSET[a][2]
                )
        listed = [
            halo_list[side : side + 1, j * BLOCK : (j + 1) * BLOCK]
            for side in range(2) for j in range(nh)
        ]
        picks = jnp.concatenate(listed + [listed[0]] * (8 - len(listed)), axis=0)
        low, high = picks & (BLOCK - 1), picks >> 7
        for t in range(9):
            value = lookup(table[t, 0:1, :], low)
            for h in range(1, wt):
                value = jnp.where(high == h, lookup(table[t, h : h + 1, :], low), value)
            for side in range(2):
                halo_out[side, t * nh : (t + 1) * nh, :] = value[side * nh : (side + 1) * nh, :]
        in_all()

        def pass_inner(dr):
            there = peer_row(dr)
            there["col"], there["sub"] = lax.div(target, n_sub), lax.rem(target, n_sub)
            return remote(
                inner, parts.at[lane, me], v_send.at[dr], v_recv.at[lane, me], there
            )

        @pl.when(target == me)
        def _():
            parts[lane, me] = inner[...]

        pl.when(target != me)(lambda: pass_inner(0).start())
        for dr in range(1, n_row):
            pass_inner(dr).start()
        for side, by in ((0, 1), (1, n_row - 1)):
            started.append(
                send(halo_out.at[side], halo_in.at[side], e_send.at[side], e_recv.at[side],
                     peer_row(by))
            )
        total = hist1[0].astype(jnp.int32)
        for du in range(1, n_sub):
            arrived(hist1.at[du], i_recv.at[du])
            total = total + hist1[du].astype(jnp.int32)
        hist[0] = total.astype(jnp.int16)

        def share(q, carry):
            remote(hist.at[0], hist.at[q], h_send, h_recv, chip(q)).start()
            return carry

        lax.fori_loop(1, n_chip, share, 0)

        def pass_block(to):
            return remote(
                comp.at[row], comp.at[row], s_send.at[to], s_recv.at[row], {"row": to}
            )

        upper = lax.div(row, n_row // 2)
        inner_row = n_row - 1 - upper * (n_row // 2)

        def pass_blocks(early):
            for to in range(n_row):
                held = to == inner_row
                go = jnp.logical_not(held) if early else held
                pl.when(jnp.logical_and(row != to, go))(lambda to=to: pass_block(to).start())

        pass_blocks(True)
        send_panels(2, 6)
        def expand(r):
            marks = comp[r, rows : rows + rb * cb, :].astype(F32)
            for i in range(rb):
                tile = comp[r, i * BLOCK : (i + 1) * BLOCK, :].astype(F32)
                at = slice(i * BLOCK, (i + 1) * BLOCK)
                for j in range(cb):
                    q = i * cb + j
                    full[r, at, j * BLOCK : (j + 1) * BLOCK] = (tile * marks[q : q + 1, :]).astype(BF16)

        def pass_on(k):
            at = pl.ds(k * step, step)
            for dc in range(1, n_col):
                slot = source(dc, 0)
                arrived(panel.at[slot, at], d_recv.at[dc, 0, k])
                for du in range(1, n_sub):
                    started.append(
                        send(panel.at[slot, at], panel.at[slot, at], f_send.at[dc, du, k],
                             d_recv.at[dc, du, k], peer(0, du))
                    )

        def pick_own(j, carry):
            lanes = pl.ds(pl.multiple_of(j * BLOCK, BLOCK), BLOCK)
            for s in range(neigh // 8):
                idx = neighbours[8 * s : 8 * s + 8, lanes]
                low, high = idx & (BLOCK - 1), idx >> 7
                part = [lookup(table[t, 0:1, :], low) for t in range(9)]
                for h in range(1, wt):
                    hit = high == h
                    for t in range(9):
                        part[t] = jnp.where(hit, lookup(table[t, h : h + 1, :], low), part[t])
                for t in range(9):
                    picked[j, s, t] = part[t]
            return carry

        def pair_tile(j, carry):
            lanes = pl.ds(pl.multiple_of(j * BLOCK, BLOCK), BLOCK)
            own = [jnp.broadcast_to(table[t, pl.ds(j, 1), :], (8, BLOCK)) for t in range(9)]
            totals = [jnp.zeros((8, BLOCK), F32) for _ in range(9)]
            for s in range(neigh // 8):
                idx = neighbours[8 * s : 8 * s + 8, lanes]
                low, high = idx & (BLOCK - 1), idx >> 7
                part = [picked[j, s, t] for t in range(9)]
                for h in range(wt, wt + 2 * nh):
                    hit = high == h
                    side, at = (h - wt) // nh, (h - wt) % nh
                    for t in range(9):
                        line = halo_in[side, t * nh + at : t * nh + at + 1, :]
                        part[t] = jnp.where(hit, lookup(line, low), part[t])
                for a in range(3):
                    for b in range(3):
                        d = [own[3 * a + c] - part[3 * b + c] for c in range(3)]
                        inv = lax.rsqrt(d[0] * d[0] + d[1] * d[1] + d[2] * d[2] + SOFTEN)
                        weight = (CHARGE[a] * CHARGE[b]) * (inv * inv * inv)
                        for c in range(3):
                            totals[3 * a + c] = totals[3 * a + c] + d[c] * weight
            for t in range(9):
                force[t, pl.ds(j, 1), :] = jnp.sum(totals[t], axis=0, keepdims=True)
            return carry

        lax.fori_loop(0, wt, pick_own, 0)

        arrived(hist.at[pl.ds(1, n_chip - 1)], h_recv)
        counts = lax.fori_loop(
            1, n_chip, lambda q, c: c + hist[q].astype(jnp.int32), hist[0].astype(jnp.int32)
        )
        potential[...] = counts.astype(F32) * UNIT
        for s in range(wide):
            for m in range(n_m):
                is_own = jnp.logical_and(target == me, jnp.logical_and(lane == s, me == m))
                pl.when(jnp.logical_not(is_own))(
                    lambda s=s, m=m: arrived(parts.at[s, m], v_recv.at[s, m])
                )
        lines = [[], [], []]
        for s in range(wide):
            total = parts[s, 0]
            for m in range(1, n_m):
                total = total + parts[s, m]
            for i in range(rb):
                j = s * rb + i
                weigh = COUPLE * potential[pl.ds(me * cb + j, 1), :]
                dip = dipole[:, j * BLOCK : (j + 1) * BLOCK].astype(F32)
                for c in range(3):
                    lines[c].append(total[4 * i + c : 4 * i + c + 1, :] + weigh * dip[c : c + 1, :])
        vector = jnp.concatenate([jnp.concatenate(line, axis=1) for line in lines], axis=0)
        coarse = vector.astype(BF16).astype(F32)
        stack = jnp.concatenate(
            [coarse, vector - coarse, dipole[...].astype(F32), jnp.zeros((7, cols), F32)], axis=0
        ).astype(BF16)
        for i in range(rb):
            got = lax.dot_general(
                stack, panel[me, i * BLOCK : (i + 1) * BLOCK, :], (((1,), (1,)), ((), ())),
                preferred_element_type=F32,
            )
            weigh = COUPLE * potential[pl.ds(row * rb + i, 1), :]
            inner2 = got[0:3, :] + got[3:6, :] + weigh * got[6:9, :]
            low_u[i] = jnp.concatenate([inner2, jnp.zeros((1, BLOCK), F32)], axis=0)
        local = jnp.concatenate(low_u, axis=0)
        field1[0] = local
        for du in range(1, n_sub):
            started.append(
                send(field1.at[0], field1.at[du], g_send.at[du], g_recv.at[du], peer(0, du))
            )
        for side in range(2):
            arrived(halo_in.at[side], e_recv.at[side])
        lax.fori_loop(0, wt // 4, pair_tile, 0)
        for du in range(1, n_sub):
            arrived(field1.at[du], g_recv.at[du])
            local = local + field1[du]
        field[0] = local.astype(BF16)

        def tell(q, carry):
            remote(field.at[0], field.at[q], q_send, q_recv, chip(q)).start()
            return carry

        lax.fori_loop(1, n_chip, tell, 0)
        pass_blocks(False)
        send_panels(6, CHUNKS + 2)
        pass_on(0)
        lax.fori_loop(wt // 4, wt, pair_tile, 0)
        pass_on(1)

        col_pot = jnp.concatenate(
            [potential[pl.ds(me * cb + j, 1), :] for j in range(cb)], axis=1
        )
        eye = (
            lax.broadcasted_iota(jnp.int32, (BLOCK, BLOCK), 0)
            == lax.broadcasted_iota(jnp.int32, (BLOCK, BLOCK), 1)
        )

        def term(slot, at):
            total = None
            for s in range(wide):
                part = jnp.dot(
                    panel[slot, at, s * rows : (s + 1) * rows], full[slot * wide + s],
                    preferred_element_type=F32,
                )
                total = part if total is None else total + part
            return total

        def blocks(slot):
            for s in range(wide):
                r = slot * wide + s
                pl.when(r != row)(lambda r=r: arrived(comp.at[r], s_recv.at[r]))
                expand(r)

        pass_on(2)
        arrived(field.at[pl.ds(1, n_chip - 1)], q_recv)
        small[8].wait()
        small[9].wait()
        for dr in range(n_row):
            total = field[dr * n_col].astype(F32)
            for m in range(1, n_col):
                total = total + field[dr * n_col + m].astype(F32)
            sums[lax.rem(row + n_row - dr, n_row)] = total

        forces = []
        for a in range(3):
            own = dense(owner, a)
            low, high = own & (BLOCK - 1), own >> 7
            value = [jnp.zeros((wt, BLOCK), F32)] * 3
            for h in range(nb):
                hit = high == h
                at = 4 * (h % rb)
                for c in range(3):
                    value[c] = jnp.where(
                        hit, lookup(sums[h // rb, at + c : at + c + 1, :], low), value[c]
                    )
            forces.append([force[3 * a + c] + CHARGE[a] * value[c] for c in range(3)])
        cent = [dense(centres, c) for c in range(3)]
        quat = [quats[c] for c in range(4)]
        torque = [jnp.zeros((wt, BLOCK), F32)] * 3
        for a in range(3):
            lever = [table[3 * a + c] - cent[c] for c in range(3)]
            turn = cross(lever, forces[a])
            torque = [torque[c] + turn[c] for c in range(3)]
        omega = []
        for c in range(3):
            pull = forces[0][c] + forces[1][c] + forces[2][c]
            fast = dense(velocity, c) + STEP_DT * pull / WATER_MASS
            spread(velocity_new, c, fast)
            spread(centres_new, c, cent[c] + STEP_DT * fast)
            spin = dense(angmom, c) + STEP_DT * torque[c]
            spread(angmom_new, c, spin)
            omega.append(spin / INERTIA)
        vector = quat[1:4]
        delta = [-(omega[0] * vector[0] + omega[1] * vector[1] + omega[2] * vector[2])]
        turn = cross(omega, vector)
        delta += [quat[0] * omega[c] + turn[c] for c in range(3)]
        moved = [quat[c] + 0.5 * STEP_DT * delta[c] for c in range(4)]
        length = jnp.sqrt(sum(m * m for m in moved))
        for c in range(4):
            spread(orient_new, c, moved[c] / length)

        pass_on(3)
        flip = lax.rem(upper + lax.div(col, n_col // 2), 2)
        for p in range(n_col - 1):
            dc = lax.rem(p + flip, n_col)
            for du in range(n_sub):
                slot = source(dc, du)
                if du > 0:
                    for k in range(CHUNKS):
                        arrived(panel.at[slot, pl.ds(k * step, step)], d_recv.at[dc, du, k])
                blocks(slot)
                for q in range(SPLIT):
                    at = slice(q * rows // SPLIT, (q + 1) * rows // SPLIT)
                    if p + du == 0:
                        total_out[at, :] = term(slot, at)
                    else:
                        total_out[at, :] += term(slot, at)
        dc = lax.rem(n_col - 1 + flip, n_col)
        for du in range(n_sub):
            blocks(source(dc, du))
        for k in range(CHUNKS):
            at = slice(k * step, (k + 1) * step)
            total = total_out[at, :]
            for du in range(n_sub):
                slot = source(dc, du)
                if du > 0:
                    arrived(panel.at[slot, at], d_recv.at[dc, du, k])
                total = total + term(slot, at)
            line = potential[pl.ds(row * rb + k, 1), :]
            row_pot = jnp.sum(jnp.where(eye, line, 0.0), axis=1, keepdims=True)
            mine = panel[me, at, :].astype(F32)
            coupled[at, :] = (total + COUPLE * (row_pot + col_pot) * mine).astype(BF16)

        arrived(hist.at[pl.ds(1, n_chip - 1)], h_send)
        arrived(field.at[pl.ds(1, n_chip - 1)], q_send)
        pl.when(target != me)(lambda: pass_inner(0).wait_send())
        for dr in range(1, n_row):
            pass_inner(dr).wait_send()
        for to in range(n_row):
            pl.when(row != to)(lambda to=to: pass_block(to).wait_send())
        for dc in range(1, n_col):
            for k in range(CHUNKS):
                panel_copy(dc, k).wait_send()
        for copy in started:
            copy.wait_send()

    hbm = pl.BlockSpec(memory_space=pltpu.HBM)
    vmem = pl.BlockSpec(memory_space=pltpu.VMEM)
    dma = lambda *s: pltpu.SemaphoreType.DMA(s)
    one = pltpu.SemaphoreType.DMA(())
    call = pl.pallas_call(
        kernel,
        out_shape=(
            pltpu.VMEM((rows, cols), BF16),
            pltpu.VMEM((3, waters), F32),
            pltpu.VMEM((3, waters), F32),
            pltpu.VMEM((3, waters), F32),
            pltpu.VMEM((4, waters), F32),
        ),
        in_specs=[hbm] * 12,
        out_specs=(vmem,) * 5,
        scratch_shapes=[
            pltpu.VMEM((rows, cols), BF16),
            pltpu.VMEM((rows, cols), BF16),
            pltpu.SMEM((rb, cb), jnp.int32),
            pltpu.SMEM((rb, cb), jnp.int32),
            pltpu.VMEM((3, cols), BF16),
            pltpu.VMEM((3, waters), jnp.int32),
            pltpu.VMEM((3, waters), F32),
            pltpu.VMEM((3, waters), F32),
            pltpu.VMEM((3, waters), F32),
            pltpu.VMEM((3, waters), F32),
            pltpu.VMEM((2, halo), jnp.int32),
            pltpu.VMEM((neigh, waters), jnp.int32),
            pltpu.VMEM((n_m, rows, cols), BF16),
            pltpu.VMEM((n_row, rows + rb * cb, BLOCK), BF16),
            pltpu.VMEM((n_row, rows, cols), BF16),
            pltpu.VMEM((rows, cols), F32),
            pltpu.VMEM((wt, neigh // 8, 9, 8, BLOCK), F32),
            pltpu.VMEM((n_chip, nb, BLOCK), jnp.int16),
            pltpu.VMEM((rb * 4, BLOCK), F32),
            pltpu.VMEM((wide, n_m, rb * 4, BLOCK), F32),
            pltpu.VMEM((n_chip, rb * 4, BLOCK), BF16),
            pltpu.VMEM((2, 24, BLOCK), F32),
            pltpu.VMEM((2, 24, BLOCK), F32),
            pltpu.VMEM((9, wt, BLOCK), F32),
            pltpu.VMEM((9, wt, BLOCK), F32),
            pltpu.VMEM((4, wt, BLOCK), F32),
            pltpu.VMEM((nb, BLOCK), F32),
            pltpu.VMEM((n_row, rb * 4, BLOCK), F32),
            pltpu.VMEM((n_sub, nb, BLOCK), jnp.int16),
            pltpu.VMEM((n_sub, rb * 4, BLOCK), F32),
            dma(11), dma(CHUNKS),
            dma(n_col, n_sub, CHUNKS), dma(n_col, n_sub, CHUNKS), dma(n_col, n_sub, CHUNKS),
            dma(n_row), dma(n_row), one, one, dma(n_row), dma(wide, n_m),
            one, one, dma(2), dma(2), pltpu.SemaphoreType.REGULAR, pltpu.SemaphoreType.REGULAR,
            dma(n_sub), dma(n_sub), dma(n_sub), dma(n_sub),
        ],
        compiler_params=pltpu.CompilerParams(
            collective_id=0, has_side_effects=True, vmem_limit_bytes=48 << 20
        ),
    )
    return call


def deliver(results):
    count = len(results)

    def kernel(*refs):
        sem = refs[2 * count]
        stores = [
            pltpu.make_async_copy(refs[n], refs[count + n], sem.at[n]) for n in range(count)
        ]
        for store in stores:
            store.start()
        for store in stores:
            store.wait()

    return pl.pallas_call(
        kernel,
        out_shape=tuple(jax.ShapeDtypeStruct(r.shape, r.dtype) for r in results),
        in_specs=[pl.BlockSpec(memory_space=pltpu.VMEM)] * count,
        out_specs=(pl.BlockSpec(memory_space=pltpu.HBM),) * count,
        scratch_shapes=[pltpu.SemaphoreType.DMA((count,))],
    )(*[pltpu.with_memory_space_constraint(r, pltpu.VMEM) for r in results])


def solution(mesh):
    n_row, n_col, n_sub = mesh.shape["row"], mesh.shape["col"], mesh.shape["sub"]

    def shards(density, margin, pattern_d, pattern_s, dipole, owner, centres, angles,
               velocity, angmom, halo_list, neighbours):
        call = make_kernel(
            n_row, n_col, n_sub, density.shape[0], density.shape[1], owner.shape[1],
            neighbours.shape[0], halo_list.shape[1],
        )
        return deliver(
            call(*[
                pltpu.with_memory_space_constraint(x, pltpu.HBM)
                for x in (density, margin, pattern_d, pattern_s, dipole, owner, centres,
                          angles, velocity, angmom, halo_list, neighbours)
            ])
        )

    block = P(("groups", "row"), ("col", "sub"))
    water = P(None, ("groups", "row", "col", "sub"))
    return jax.shard_map(
        shards,
        mesh=mesh,
        in_specs=(block,) * 4 + (P(None, ("groups", "col", "sub")),) + (water,) * 7,
        out_specs=(block,) + (water,) * 4,
        check_vma=False,
    )
```

```python
import jax
import jax.numpy as jnp
from jax import lax
from jax.experimental import pallas as pl
from jax.experimental.pallas import tpu as pltpu
from jax.sharding import PartitionSpec as P

BLOCK = 128
UNIT = 0.417
OFFSET = ((0.0, 0.0, -0.12), (0.76, 0.0, 0.47), (-0.76, 0.0, 0.47))
WEIGHT = (-2.0, 1.0, 1.0)
CHARGE = (-0.834, 0.417, 0.417)
COUPLE = 0.1
STEP_DT = 0.5
WATER_MASS = 1.0
INERTIA = 0.5
SOFTEN = 1.0
CHUNKS = 4
SPLIT = 2
F32 = jnp.float32
BF16 = jnp.bfloat16


def lookup(row, low):
    return jnp.take_along_axis(
        jnp.broadcast_to(row, low.shape), low, axis=1, mode="promise_in_bounds"
    )


def dense(ref, compo):
    count = ref.shape[1] // BLOCK
    return jnp.concatenate(
        [ref[compo : compo + 1, j * BLOCK : (j + 1) * BLOCK] for j in range(count)], axis=0
    )


def spread(ref, compo, value):
    for j in range(ref.shape[1] // BLOCK):
        ref[compo : compo + 1, j * BLOCK : (j + 1) * BLOCK] = value[j : j + 1, :]


def cross(a, b):
    return (
        a[1] * b[2] - a[2] * b[1],
        a[2] * b[0] - a[0] * b[2],
        a[0] * b[1] - a[1] * b[0],
    )


def quaternion(angles):
    cos_r, cos_p, cos_y = [jnp.cos(0.5 * a) for a in angles]
    sin_r, sin_p, sin_y = [jnp.sin(0.5 * a) for a in angles]
    return (
        cos_r * cos_p * cos_y + sin_r * sin_p * sin_y,
        sin_r * cos_p * cos_y - cos_r * sin_p * sin_y,
        cos_r * sin_p * cos_y + sin_r * cos_p * sin_y,
        cos_r * cos_p * sin_y - sin_r * sin_p * cos_y,
    )


def rotation(quat):
    w, x, y, z = quat
    return (
        (1.0 - 2.0 * (y * y + z * z), 2.0 * (x * y - w * z), 2.0 * (x * z + w * y)),
        (2.0 * (x * y + w * z), 1.0 - 2.0 * (x * x + z * z), 2.0 * (y * z - w * x)),
        (2.0 * (x * z - w * y), 2.0 * (y * z + w * x), 1.0 - 2.0 * (x * x + y * y)),
    )


def make_kernel(n_row, n_col, n_sub, rows, cols, waters, neigh, halo):
    n_m = n_col * n_sub
    n_all = n_row * n_m
    n_chip = n_row * n_col
    order = rows * n_row
    rb, cb, nb = rows // BLOCK, cols // BLOCK, order // BLOCK
    wt, nh = waters // BLOCK, halo // BLOCK
    wide = cols // rows
    step = rows // CHUNKS
    hr = 9 * nh

    def kernel(
        density_hbm, margin_hbm, pat_d_hbm, pat_s_hbm, dipole_hbm, owner_hbm, centres_hbm,
        angles_hbm, velocity_hbm, angmom_hbm, halo_list_hbm, neighbours_hbm,
        coupled, centres_new, velocity_new, angmom_new, orient_new,
        density, margin, pat_d, pat_s, dipole, owner, centres,
        angles, velocity, angmom, halo_list, neighbours,
        panel, comp, full, total_out, picked, hist, inner, parts, field, halo_out, halo_in,
        table, force, quats, potential, sums, hist1, field1,
        l_sem, c_sem, d_send, d_recv, f_send, s_send, s_recv, h_send, h_recv, v_send, v_recv,
        q_send, q_recv, e_send, e_recv, row_ready, all_ready, i_send, i_recv, g_send, g_recv,
    ):
        row, col, sub = lax.axis_index("row"), lax.axis_index("col"), lax.axis_index("sub")
        me = col * n_sub + sub

        def peer(dc, du):
            return {"col": lax.rem(col + dc, n_col), "sub": lax.rem(sub + du, n_sub)}

        def peer_row(dr):
            return {"row": lax.rem(row + dr, n_row)}

        def other(q):
            dr, dm = lax.div(q, n_m), lax.rem(q, n_m)
            return {
                "row": lax.rem(row + dr, n_row),
                "col": lax.rem(col + lax.div(dm, n_sub), n_col),
                "sub": lax.rem(sub + lax.rem(dm, n_sub), n_sub),
            }

        def chip(q):
            return {
                "row": lax.rem(row + lax.div(q, n_col), n_row),
                "col": lax.rem(col + lax.rem(q, n_col), n_col),
            }

        def source(dc, du):
            return (
                lax.rem(col + n_col - dc, n_col) * n_sub + lax.rem(sub + n_sub - du, n_sub)
            )

        started = []

        def remote(src, dst, ssem, rsem, dev):
            return pltpu.make_async_remote_copy(
                src_ref=src, dst_ref=dst, send_sem=ssem, recv_sem=rsem,
                device_id=dev, device_id_type=pl.DeviceIdType.MESH,
            )

        def send(src, dst, ssem, rsem, dev):
            copy = remote(src, dst, ssem, rsem, dev)
            copy.start()
            return copy

        def arrived(ref, sem):
            pltpu.make_async_copy(ref, ref, sem).wait()

        barrier = pltpu.get_barrier_semaphore()

        def greet(dev):
            pl.semaphore_signal(
                barrier, inc=1, device_id=dev, device_id_type=pl.DeviceIdType.MESH
            )

        near, far = 0, n_sub - 1

        def greet_near(q, carry):
            greet({"col": lax.rem(col + q, n_col), "sub": near})
            return carry

        def greet_far(q, carry):
            greet({
                "row": lax.rem(row + lax.div(q, n_col), n_row),
                "col": lax.rem(col + lax.rem(q, n_col), n_col), "sub": far,
            })
            return carry

        def in_row():
            @pl.when(sub == near)
            def _():
                pl.semaphore_wait(barrier, n_m - 1)
                for du in range(1, n_sub):
                    pl.semaphore_signal(
                        row_ready, inc=1, device_id=peer(0, du),
                        device_id_type=pl.DeviceIdType.MESH,
                    )

            pl.when(sub != near)(lambda: pl.semaphore_wait(row_ready, 1))

        def in_all():
            @pl.when(sub == far)
            def _():
                pl.semaphore_wait(barrier, n_all - n_m)
                for du in range(1, n_sub):
                    pl.semaphore_signal(
                        all_ready, inc=1, device_id=peer(0, du),
                        device_id_type=pl.DeviceIdType.MESH,
                    )

            pl.when(sub != far)(lambda: pl.semaphore_wait(all_ready, 1))

        small = [
            pltpu.make_async_copy(src, dst, l_sem.at[n])
            for n, (src, dst) in enumerate((
                (pat_d_hbm, pat_d), (pat_s_hbm, pat_s), (dipole_hbm, dipole),
                (owner_hbm, owner), (angles_hbm, angles), (centres_hbm, centres),
                (halo_list_hbm, halo_list), (neighbours_hbm, neighbours),
                (velocity_hbm, velocity), (angmom_hbm, angmom), (margin_hbm, margin),
            ))
        ]
        loads = [
            pltpu.make_async_copy(
                density_hbm.at[pl.ds(k * step, step)], density.at[pl.ds(k * step, step)],
                c_sem.at[k],
            )
            for k in range(CHUNKS)
        ]
        small[3].start()
        small[0].start()
        loads[0].start()
        for load in loads[1:]:
            load.start()
        small[10].start()
        for n in (1, 2, 4, 5, 6, 7, 8, 9):
            small[n].start()
        lax.fori_loop(1, n_col, greet_near, 0)
        pl.when(sub != near)(lambda: greet({"sub": near}))
        lax.fori_loop(n_col, n_chip, greet_far, 0)

        small[3].wait()
        lane_ids = lax.broadcasted_iota(jnp.int32, (BLOCK, waters), 0)
        high_ids = lax.broadcasted_iota(jnp.int32, (nb, waters), 0)
        counts = jnp.zeros((nb, BLOCK), F32)
        for site in range(3):
            own = owner[site : site + 1, :]
            low_hot = jnp.where(lane_ids == (own & (BLOCK - 1)), 1.0, 0.0).astype(BF16)
            high_hot = jnp.where(high_ids == (own >> 7), WEIGHT[site], 0.0).astype(BF16)
            counts = counts + lax.dot_general(
                high_hot, low_hot, (((1,), (1,)), ((), ())), preferred_element_type=F32
            )
        hist1[0] = counts.astype(jnp.int32).astype(jnp.int16)
        in_row()
        for du in range(1, n_sub):
            started.append(
                send(hist1.at[0], hist1.at[du], i_send.at[du], i_recv.at[du], peer(0, du))
            )

        small[0].wait()
        for k in range(CHUNKS):
            loads[k].wait()
            for i in range(k * step // BLOCK, (k + 1) * step // BLOCK):
                at = slice(i * BLOCK, (i + 1) * BLOCK)
                for j in range(cb):
                    ac = slice(j * BLOCK, (j + 1) * BLOCK)
                    factor = pat_d[i, j].astype(F32)
                    panel[me, at, ac] = (density[at, ac].astype(F32) * factor).astype(BF16)
        def panel_copy(dc, k):
            at = panel.at[me, pl.ds(k * step, step)]
            return remote(at, at, d_send.at[dc, 0, k], d_recv.at[dc, 0, k], peer(dc, 0))

        rank = jnp.minimum(row, 2)

        def send_panels(first, end):
            for k in range(CHUNKS):
                @pl.when(jnp.logical_and(k + rank >= first, k + rank < end))
                def _(k=k):
                    for dc in range(1, n_col):
                        panel_copy(dc, k).start()

        send_panels(0, 2)
        for k in range(CHUNKS):
            at = pl.ds(k * step, step)
            for du in range(1, n_sub):
                started.append(
                    send(panel.at[me, at], panel.at[me, at], d_send.at[0, du, k],
                         d_recv.at[0, du, k], peer(0, du))
                )

        small[1].wait()
        small[2].wait()
        small[10].wait()
        low_u = []
        for i in range(rb):
            at = slice(i * BLOCK, (i + 1) * BLOCK)
            total, chosen = None, None
            for j in range(cb):
                ac = slice(j * BLOCK, (j + 1) * BLOCK)
                factor = pat_s[i, j].astype(F32)
                term = margin[at, ac].astype(F32) * factor
                dip = dipole[:, ac].astype(F32) * factor
                total = term if total is None else total + term
                chosen = dip if chosen is None else chosen + dip
            tile = total.astype(BF16)
            comp[row, at, :] = tile
            low_u.append(
                lax.dot_general(
                    chosen.astype(BF16), tile, (((1,), (1,)), ((), ())),
                    preferred_element_type=F32,
                )
            )
        for base in range(0, rb * cb, 16):
            comp[row, rows + base : rows + base + 16, :] = jnp.concatenate(
                [
                    jnp.full((1, BLOCK), pat_s[q // cb, q % cb].astype(F32), F32)
                    for q in range(base, base + 16)
                ],
                axis=0,
            ).astype(BF16)
        target, lane = lax.div(row, wide), lax.rem(row, wide)
        for i in range(rb):
            inner[4 * i : 4 * i + 3, :] = low_u[i]
            inner[4 * i + 3 : 4 * i + 4, :] = low_u[i][0:1, :]

        for load in small[4:8]:
            load.wait()
        cent = [dense(centres, c) for c in range(3)]
        quat = quaternion([dense(angles, c) for c in range(3)])
        for c in range(4):
            quats[c] = quat[c]
        matrix = rotation(quat)
        for a in range(3):
            for c in range(3):
                table[3 * a + c] = (
                    cent[c]
                    + matrix[c][0] * OFFSET[a][0]
                    + matrix[c][1] * OFFSET[a][1]
                    + matrix[c][2] * OFFSET[a][2]
                )
        listed = [
            halo_list[side : side + 1, j * BLOCK : (j + 1) * BLOCK]
            for side in range(2) for j in range(nh)
        ]
        picks = jnp.concatenate(listed + [listed[0]] * (8 - len(listed)), axis=0)
        low, high = picks & (BLOCK - 1), picks >> 7
        for t in range(9):
            value = lookup(table[t, 0:1, :], low)
            for h in range(1, wt):
                value = jnp.where(high == h, lookup(table[t, h : h + 1, :], low), value)
            for side in range(2):
                halo_out[side, t * nh : (t + 1) * nh, :] = value[side * nh : (side + 1) * nh, :]
        in_all()

        total = hist1[0].astype(jnp.int32)
        for du in range(1, n_sub):
            arrived(hist1.at[du], i_recv.at[du])
            total = total + hist1[du].astype(jnp.int32)
        hist[0] = total.astype(jnp.int16)

        def share(q, carry):
            remote(hist.at[0], hist.at[q], h_send, h_recv, chip(q)).start()
            return carry

        lax.fori_loop(1, n_chip, share, 0)

        def pass_inner(dr):
            there = peer_row(dr)
            there["col"], there["sub"] = lax.div(target, n_sub), lax.rem(target, n_sub)
            return remote(
                inner, parts.at[lane, me], v_send.at[dr], v_recv.at[lane, me], there
            )

        @pl.when(target == me)
        def _():
            parts[lane, me] = inner[...]

        pl.when(target != me)(lambda: pass_inner(0).start())
        for dr in range(1, n_row):
            pass_inner(dr).start()
        for side, by in ((0, 1), (1, n_row - 1)):
            started.append(
                send(halo_out.at[side], halo_in.at[side], e_send.at[side], e_recv.at[side],
                     peer_row(by))
            )

        def pass_block(to):
            return remote(
                comp.at[row], comp.at[row], s_send.at[to], s_recv.at[row], {"row": to}
            )

        upper = lax.div(row, n_row // 2)
        inner_row = n_row - 1 - upper * (n_row // 2)

        def pass_blocks(early):
            for to in range(n_row):
                held = to == inner_row
                go = jnp.logical_not(held) if early else held
                pl.when(jnp.logical_and(row != to, go))(lambda to=to: pass_block(to).start())

        pass_blocks(True)
        send_panels(2, 6)
        def expand(r):
            marks = comp[r, rows : rows + rb * cb, :].astype(F32)
            for i in range(rb):
                tile = comp[r, i * BLOCK : (i + 1) * BLOCK, :].astype(F32)
                at = slice(i * BLOCK, (i + 1) * BLOCK)
                for j in range(cb):
                    q = i * cb + j
                    full[r, at, j * BLOCK : (j + 1) * BLOCK] = (tile * marks[q : q + 1, :]).astype(BF16)

        def pass_on(k):
            at = pl.ds(k * step, step)
            for dc in range(1, n_col):
                slot = source(dc, 0)
                arrived(panel.at[slot, at], d_recv.at[dc, 0, k])
                for du in range(1, n_sub):
                    started.append(
                        send(panel.at[slot, at], panel.at[slot, at], f_send.at[dc, du, k],
                             d_recv.at[dc, du, k], peer(0, du))
                    )

        def pick_own(j, carry):
            lanes = pl.ds(pl.multiple_of(j * BLOCK, BLOCK), BLOCK)
            for s in range(neigh // 8):
                idx = neighbours[8 * s : 8 * s + 8, lanes]
                low, high = idx & (BLOCK - 1), idx >> 7
                part = [lookup(table[t, 0:1, :], low) for t in range(9)]
                for h in range(1, wt):
                    hit = high == h
                    for t in range(9):
                        part[t] = jnp.where(hit, lookup(table[t, h : h + 1, :], low), part[t])
                for t in range(9):
                    picked[j, s, t] = part[t]
            return carry

        def pair_tile(j, carry):
            lanes = pl.ds(pl.multiple_of(j * BLOCK, BLOCK), BLOCK)
            own = [jnp.broadcast_to(table[t, pl.ds(j, 1), :], (8, BLOCK)) for t in range(9)]
            totals = [jnp.zeros((8, BLOCK), F32) for _ in range(9)]
            for s in range(neigh // 8):
                idx = neighbours[8 * s : 8 * s + 8, lanes]
                low, high = idx & (BLOCK - 1), idx >> 7
                part = [picked[j, s, t] for t in range(9)]
                for h in range(wt, wt + 2 * nh):
                    hit = high == h
                    side, at = (h - wt) // nh, (h - wt) % nh
                    for t in range(9):
                        line = halo_in[side, t * nh + at : t * nh + at + 1, :]
                        part[t] = jnp.where(hit, lookup(line, low), part[t])
                for a in range(3):
                    for b in range(3):
                        d = [own[3 * a + c] - part[3 * b + c] for c in range(3)]
                        inv = lax.rsqrt(d[0] * d[0] + d[1] * d[1] + d[2] * d[2] + SOFTEN)
                        weight = (CHARGE[a] * CHARGE[b]) * (inv * inv * inv)
                        for c in range(3):
                            totals[3 * a + c] = totals[3 * a + c] + d[c] * weight
            for t in range(9):
                force[t, pl.ds(j, 1), :] = jnp.sum(totals[t], axis=0, keepdims=True)
            return carry

        lax.fori_loop(0, wt, pick_own, 0)

        arrived(hist.at[pl.ds(1, n_chip - 1)], h_recv)
        counts = lax.fori_loop(
            1, n_chip, lambda q, c: c + hist[q].astype(jnp.int32), hist[0].astype(jnp.int32)
        )
        potential[...] = counts.astype(F32) * UNIT
        for s in range(wide):
            for m in range(n_m):
                is_own = jnp.logical_and(target == me, jnp.logical_and(lane == s, me == m))
                pl.when(jnp.logical_not(is_own))(
                    lambda s=s, m=m: arrived(parts.at[s, m], v_recv.at[s, m])
                )
        lines = [[], [], []]
        for s in range(wide):
            total = parts[s, 0]
            for m in range(1, n_m):
                total = total + parts[s, m]
            for i in range(rb):
                j = s * rb + i
                weigh = COUPLE * potential[pl.ds(me * cb + j, 1), :]
                dip = dipole[:, j * BLOCK : (j + 1) * BLOCK].astype(F32)
                for c in range(3):
                    lines[c].append(total[4 * i + c : 4 * i + c + 1, :] + weigh * dip[c : c + 1, :])
        vector = jnp.concatenate([jnp.concatenate(line, axis=1) for line in lines], axis=0)
        coarse = vector.astype(BF16).astype(F32)
        stack = jnp.concatenate(
            [coarse, vector - coarse, dipole[...].astype(F32), jnp.zeros((7, cols), F32)], axis=0
        ).astype(BF16)
        for i in range(rb):
            got = lax.dot_general(
                stack, panel[me, i * BLOCK : (i + 1) * BLOCK, :], (((1,), (1,)), ((), ())),
                preferred_element_type=F32,
            )
            weigh = COUPLE * potential[pl.ds(row * rb + i, 1), :]
            inner2 = got[0:3, :] + got[3:6, :] + weigh * got[6:9, :]
            low_u[i] = jnp.concatenate([inner2, jnp.zeros((1, BLOCK), F32)], axis=0)
        local = jnp.concatenate(low_u, axis=0)
        field1[0] = local
        for du in range(1, n_sub):
            started.append(
                send(field1.at[0], field1.at[du], g_send.at[du], g_recv.at[du], peer(0, du))
            )
        for side in range(2):
            arrived(halo_in.at[side], e_recv.at[side])
        for du in range(1, n_sub):
            arrived(field1.at[du], g_recv.at[du])
            local = local + field1[du]
        field[0] = local.astype(BF16)

        def tell(q, carry):
            remote(field.at[0], field.at[q], q_send, q_recv, chip(q)).start()
            return carry

        lax.fori_loop(1, n_chip, tell, 0)
        pass_blocks(False)
        send_panels(6, CHUNKS + 2)
        pass_on(0)
        lax.fori_loop(0, wt, pair_tile, 0)
        pass_on(1)

        col_pot = jnp.concatenate(
            [potential[pl.ds(me * cb + j, 1), :] for j in range(cb)], axis=1
        )
        eye = (
            lax.broadcasted_iota(jnp.int32, (BLOCK, BLOCK), 0)
            == lax.broadcasted_iota(jnp.int32, (BLOCK, BLOCK), 1)
        )

        def term(slot, at):
            total = None
            for s in range(wide):
                part = jnp.dot(
                    panel[slot, at, s * rows : (s + 1) * rows], full[slot * wide + s],
                    preferred_element_type=F32,
                )
                total = part if total is None else total + part
            return total

        def blocks(slot):
            for s in range(wide):
                r = slot * wide + s
                pl.when(r != row)(lambda r=r: arrived(comp.at[r], s_recv.at[r]))
                expand(r)

        pass_on(2)
        pass_on(3)
        flip = lax.rem(upper + lax.div(col, n_col // 2), 2)
        for p in range(n_col - 1):
            dc = lax.rem(p + flip, n_col)
            for du in range(n_sub):
                slot = source(dc, du)
                if du > 0:
                    for k in range(CHUNKS):
                        arrived(panel.at[slot, pl.ds(k * step, step)], d_recv.at[dc, du, k])
                blocks(slot)
                for q in range(SPLIT):
                    at = slice(q * rows // SPLIT, (q + 1) * rows // SPLIT)
                    if p + du == 0:
                        total_out[at, :] = term(slot, at)
                    else:
                        total_out[at, :] += term(slot, at)
        arrived(field.at[pl.ds(1, n_chip - 1)], q_recv)
        small[8].wait()
        small[9].wait()
        for dr in range(n_row):
            total = field[dr * n_col].astype(F32)
            for m in range(1, n_col):
                total = total + field[dr * n_col + m].astype(F32)
            sums[lax.rem(row + n_row - dr, n_row)] = total

        forces = []
        for a in range(3):
            own = dense(owner, a)
            low, high = own & (BLOCK - 1), own >> 7
            value = [jnp.zeros((wt, BLOCK), F32)] * 3
            for h in range(nb):
                hit = high == h
                at = 4 * (h % rb)
                for c in range(3):
                    value[c] = jnp.where(
                        hit, lookup(sums[h // rb, at + c : at + c + 1, :], low), value[c]
                    )
            forces.append([force[3 * a + c] + CHARGE[a] * value[c] for c in range(3)])
        cent = [dense(centres, c) for c in range(3)]
        quat = [quats[c] for c in range(4)]
        torque = [jnp.zeros((wt, BLOCK), F32)] * 3
        for a in range(3):
            lever = [table[3 * a + c] - cent[c] for c in range(3)]
            turn = cross(lever, forces[a])
            torque = [torque[c] + turn[c] for c in range(3)]
        omega = []
        for c in range(3):
            pull = forces[0][c] + forces[1][c] + forces[2][c]
            fast = dense(velocity, c) + STEP_DT * pull / WATER_MASS
            spread(velocity_new, c, fast)
            spread(centres_new, c, cent[c] + STEP_DT * fast)
            spin = dense(angmom, c) + STEP_DT * torque[c]
            spread(angmom_new, c, spin)
            omega.append(spin / INERTIA)
        vector = quat[1:4]
        delta = [-(omega[0] * vector[0] + omega[1] * vector[1] + omega[2] * vector[2])]
        turn = cross(omega, vector)
        delta += [quat[0] * omega[c] + turn[c] for c in range(3)]
        moved = [quat[c] + 0.5 * STEP_DT * delta[c] for c in range(4)]
        length = jnp.sqrt(sum(m * m for m in moved))
        for c in range(4):
            spread(orient_new, c, moved[c] / length)

        dc = lax.rem(n_col - 1 + flip, n_col)
        for du in range(n_sub):
            blocks(source(dc, du))
        for k in range(CHUNKS):
            at = slice(k * step, (k + 1) * step)
            total = total_out[at, :]
            for du in range(n_sub):
                slot = source(dc, du)
                if du > 0:
                    arrived(panel.at[slot, at], d_recv.at[dc, du, k])
                total = total + term(slot, at)
            line = potential[pl.ds(row * rb + k, 1), :]
            row_pot = jnp.sum(jnp.where(eye, line, 0.0), axis=1, keepdims=True)
            mine = panel[me, at, :].astype(F32)
            coupled[at, :] = (total + COUPLE * (row_pot + col_pot) * mine).astype(BF16)

        arrived(hist.at[pl.ds(1, n_chip - 1)], h_send)
        arrived(field.at[pl.ds(1, n_chip - 1)], q_send)
        pl.when(target != me)(lambda: pass_inner(0).wait_send())
        for dr in range(1, n_row):
            pass_inner(dr).wait_send()
        for to in range(n_row):
            pl.when(row != to)(lambda to=to: pass_block(to).wait_send())
        for dc in range(1, n_col):
            for k in range(CHUNKS):
                panel_copy(dc, k).wait_send()
        for copy in started:
            copy.wait_send()

    hbm = pl.BlockSpec(memory_space=pltpu.HBM)
    vmem = pl.BlockSpec(memory_space=pltpu.VMEM)
    dma = lambda *s: pltpu.SemaphoreType.DMA(s)
    one = pltpu.SemaphoreType.DMA(())
    call = pl.pallas_call(
        kernel,
        out_shape=(
            pltpu.VMEM((rows, cols), BF16),
            pltpu.VMEM((3, waters), F32),
            pltpu.VMEM((3, waters), F32),
            pltpu.VMEM((3, waters), F32),
            pltpu.VMEM((4, waters), F32),
        ),
        in_specs=[hbm] * 12,
        out_specs=(vmem,) * 5,
        scratch_shapes=[
            pltpu.VMEM((rows, cols), BF16),
            pltpu.VMEM((rows, cols), BF16),
            pltpu.SMEM((rb, cb), jnp.int32),
            pltpu.SMEM((rb, cb), jnp.int32),
            pltpu.VMEM((3, cols), BF16),
            pltpu.VMEM((3, waters), jnp.int32),
            pltpu.VMEM((3, waters), F32),
            pltpu.VMEM((3, waters), F32),
            pltpu.VMEM((3, waters), F32),
            pltpu.VMEM((3, waters), F32),
            pltpu.VMEM((2, halo), jnp.int32),
            pltpu.VMEM((neigh, waters), jnp.int32),
            pltpu.VMEM((n_m, rows, cols), BF16),
            pltpu.VMEM((n_row, rows + rb * cb, BLOCK), BF16),
            pltpu.VMEM((n_row, rows, cols), BF16),
            pltpu.VMEM((rows, cols), F32),
            pltpu.VMEM((wt, neigh // 8, 9, 8, BLOCK), F32),
            pltpu.VMEM((n_chip, nb, BLOCK), jnp.int16),
            pltpu.VMEM((rb * 4, BLOCK), F32),
            pltpu.VMEM((wide, n_m, rb * 4, BLOCK), F32),
            pltpu.VMEM((n_chip, rb * 4, BLOCK), BF16),
            pltpu.VMEM((2, 24, BLOCK), F32),
            pltpu.VMEM((2, 24, BLOCK), F32),
            pltpu.VMEM((9, wt, BLOCK), F32),
            pltpu.VMEM((9, wt, BLOCK), F32),
            pltpu.VMEM((4, wt, BLOCK), F32),
            pltpu.VMEM((nb, BLOCK), F32),
            pltpu.VMEM((n_row, rb * 4, BLOCK), F32),
            pltpu.VMEM((n_sub, nb, BLOCK), jnp.int16),
            pltpu.VMEM((n_sub, rb * 4, BLOCK), F32),
            dma(11), dma(CHUNKS),
            dma(n_col, n_sub, CHUNKS), dma(n_col, n_sub, CHUNKS), dma(n_col, n_sub, CHUNKS),
            dma(n_row), dma(n_row), one, one, dma(n_row), dma(wide, n_m),
            one, one, dma(2), dma(2), pltpu.SemaphoreType.REGULAR, pltpu.SemaphoreType.REGULAR,
            dma(n_sub), dma(n_sub), dma(n_sub), dma(n_sub),
        ],
        compiler_params=pltpu.CompilerParams(
            collective_id=0, has_side_effects=True, vmem_limit_bytes=48 << 20
        ),
    )
    return call


def deliver(results):
    count = len(results)

    def kernel(*refs):
        sem = refs[2 * count]
        stores = [
            pltpu.make_async_copy(refs[n], refs[count + n], sem.at[n]) for n in range(count)
        ]
        for store in stores:
            store.start()
        for store in stores:
            store.wait()

    return pl.pallas_call(
        kernel,
        out_shape=tuple(jax.ShapeDtypeStruct(r.shape, r.dtype) for r in results),
        in_specs=[pl.BlockSpec(memory_space=pltpu.VMEM)] * count,
        out_specs=(pl.BlockSpec(memory_space=pltpu.HBM),) * count,
        scratch_shapes=[pltpu.SemaphoreType.DMA((count,))],
    )(*[pltpu.with_memory_space_constraint(r, pltpu.VMEM) for r in results])


def solution(mesh):
    n_row, n_col, n_sub = mesh.shape["row"], mesh.shape["col"], mesh.shape["sub"]

    def shards(density, margin, pattern_d, pattern_s, dipole, owner, centres, angles,
               velocity, angmom, halo_list, neighbours):
        call = make_kernel(
            n_row, n_col, n_sub, density.shape[0], density.shape[1], owner.shape[1],
            neighbours.shape[0], halo_list.shape[1],
        )
        return deliver(
            call(*[
                pltpu.with_memory_space_constraint(x, pltpu.HBM)
                for x in (density, margin, pattern_d, pattern_s, dipole, owner, centres,
                          angles, velocity, angmom, halo_list, neighbours)
            ])
        )

    block = P(("groups", "row"), ("col", "sub"))
    water = P(None, ("groups", "row", "col", "sub"))
    return jax.shard_map(
        shards,
        mesh=mesh,
        in_specs=(block,) * 4 + (P(None, ("groups", "col", "sub")),) + (water,) * 7,
        out_specs=(block,) + (water,) * 4,
        check_vma=False,
    )
```

```python
import jax
import jax.numpy as jnp
from jax import lax
from jax.experimental import pallas as pl
from jax.experimental.pallas import tpu as pltpu
from jax.sharding import PartitionSpec as P

BLOCK = 128
UNIT = 0.417
OFFSET = ((0.0, 0.0, -0.12), (0.76, 0.0, 0.47), (-0.76, 0.0, 0.47))
WEIGHT = (-2.0, 1.0, 1.0)
CHARGE = (-0.834, 0.417, 0.417)
COUPLE = 0.1
STEP_DT = 0.5
WATER_MASS = 1.0
INERTIA = 0.5
SOFTEN = 1.0
CHUNKS = 4
SPLIT = 2
F32 = jnp.float32
BF16 = jnp.bfloat16


def lookup(row, low):
    return jnp.take_along_axis(
        jnp.broadcast_to(row, low.shape), low, axis=1, mode="promise_in_bounds"
    )


def dense(ref, compo):
    count = ref.shape[1] // BLOCK
    return jnp.concatenate(
        [ref[compo : compo + 1, j * BLOCK : (j + 1) * BLOCK] for j in range(count)], axis=0
    )


def spread(ref, compo, value):
    for j in range(ref.shape[1] // BLOCK):
        ref[compo : compo + 1, j * BLOCK : (j + 1) * BLOCK] = value[j : j + 1, :]


def cross(a, b):
    return (
        a[1] * b[2] - a[2] * b[1],
        a[2] * b[0] - a[0] * b[2],
        a[0] * b[1] - a[1] * b[0],
    )


def quaternion(angles):
    cos_r, cos_p, cos_y = [jnp.cos(0.5 * a) for a in angles]
    sin_r, sin_p, sin_y = [jnp.sin(0.5 * a) for a in angles]
    return (
        cos_r * cos_p * cos_y + sin_r * sin_p * sin_y,
        sin_r * cos_p * cos_y - cos_r * sin_p * sin_y,
        cos_r * sin_p * cos_y + sin_r * cos_p * sin_y,
        cos_r * cos_p * sin_y - sin_r * sin_p * cos_y,
    )


def rotation(quat):
    w, x, y, z = quat
    return (
        (1.0 - 2.0 * (y * y + z * z), 2.0 * (x * y - w * z), 2.0 * (x * z + w * y)),
        (2.0 * (x * y + w * z), 1.0 - 2.0 * (x * x + z * z), 2.0 * (y * z - w * x)),
        (2.0 * (x * z - w * y), 2.0 * (y * z + w * x), 1.0 - 2.0 * (x * x + y * y)),
    )


def make_kernel(n_row, n_col, n_sub, rows, cols, waters, neigh, halo):
    n_m = n_col * n_sub
    n_all = n_row * n_m
    n_chip = n_row * n_col
    order = rows * n_row
    rb, cb, nb = rows // BLOCK, cols // BLOCK, order // BLOCK
    wt, nh = waters // BLOCK, halo // BLOCK
    wide = cols // rows
    step = rows // CHUNKS
    hr = 9 * nh

    def kernel(
        density_hbm, margin_hbm, pat_d_hbm, pat_s_hbm, dipole_hbm, owner_hbm, centres_hbm,
        angles_hbm, velocity_hbm, angmom_hbm, halo_list_hbm, neighbours_hbm,
        coupled, centres_new, velocity_new, angmom_new, orient_new,
        density, margin, pat_d, pat_s, dipole, owner, centres,
        angles, velocity, angmom, halo_list, neighbours,
        panel, comp, full, total_out, picked, hist, inner, parts, field, halo_out, halo_in,
        table, force, quats, potential, sums, hist1, field1,
        l_sem, c_sem, d_send, d_recv, f_send, s_send, s_recv, h_send, h_recv, v_send, v_recv,
        q_send, q_recv, e_send, e_recv, row_ready, all_ready, i_send, i_recv, g_send, g_recv,
    ):
        row, col, sub = lax.axis_index("row"), lax.axis_index("col"), lax.axis_index("sub")
        me = col * n_sub + sub

        def peer(dc, du):
            return {"col": lax.rem(col + dc, n_col), "sub": lax.rem(sub + du, n_sub)}

        def peer_row(dr):
            return {"row": lax.rem(row + dr, n_row)}

        def other(q):
            dr, dm = lax.div(q, n_m), lax.rem(q, n_m)
            return {
                "row": lax.rem(row + dr, n_row),
                "col": lax.rem(col + lax.div(dm, n_sub), n_col),
                "sub": lax.rem(sub + lax.rem(dm, n_sub), n_sub),
            }

        def chip(q):
            return {
                "row": lax.rem(row + lax.div(q, n_col), n_row),
                "col": lax.rem(col + lax.rem(q, n_col), n_col),
            }

        def source(dc, du):
            return (
                lax.rem(col + n_col - dc, n_col) * n_sub + lax.rem(sub + n_sub - du, n_sub)
            )

        started = []

        def remote(src, dst, ssem, rsem, dev):
            return pltpu.make_async_remote_copy(
                src_ref=src, dst_ref=dst, send_sem=ssem, recv_sem=rsem,
                device_id=dev, device_id_type=pl.DeviceIdType.MESH,
            )

        def send(src, dst, ssem, rsem, dev):
            copy = remote(src, dst, ssem, rsem, dev)
            copy.start()
            return copy

        def arrived(ref, sem):
            pltpu.make_async_copy(ref, ref, sem).wait()

        barrier = pltpu.get_barrier_semaphore()

        def greet(dev):
            pl.semaphore_signal(
                barrier, inc=1, device_id=dev, device_id_type=pl.DeviceIdType.MESH
            )

        near, far = 0, n_sub - 1

        def greet_near(q, carry):
            greet({"col": lax.rem(col + q, n_col), "sub": near})
            return carry

        def greet_far(q, carry):
            greet({
                "row": lax.rem(row + lax.div(q, n_col), n_row),
                "col": lax.rem(col + lax.rem(q, n_col), n_col), "sub": far,
            })
            return carry

        def in_row():
            @pl.when(sub == near)
            def _():
                pl.semaphore_wait(barrier, n_m - 1)
                for du in range(1, n_sub):
                    pl.semaphore_signal(
                        row_ready, inc=1, device_id=peer(0, du),
                        device_id_type=pl.DeviceIdType.MESH,
                    )

            pl.when(sub != near)(lambda: pl.semaphore_wait(row_ready, 1))

        def in_all():
            @pl.when(sub == far)
            def _():
                pl.semaphore_wait(barrier, n_all - n_m)
                for du in range(1, n_sub):
                    pl.semaphore_signal(
                        all_ready, inc=1, device_id=peer(0, du),
                        device_id_type=pl.DeviceIdType.MESH,
                    )

            pl.when(sub != far)(lambda: pl.semaphore_wait(all_ready, 1))

        small = [
            pltpu.make_async_copy(src, dst, l_sem.at[n])
            for n, (src, dst) in enumerate((
                (pat_d_hbm, pat_d), (pat_s_hbm, pat_s), (dipole_hbm, dipole),
                (owner_hbm, owner), (angles_hbm, angles), (centres_hbm, centres),
                (halo_list_hbm, halo_list), (neighbours_hbm, neighbours),
                (velocity_hbm, velocity), (angmom_hbm, angmom), (margin_hbm, margin),
            ))
        ]
        loads = [
            pltpu.make_async_copy(
                density_hbm.at[pl.ds(k * step, step)], density.at[pl.ds(k * step, step)],
                c_sem.at[k],
            )
            for k in range(CHUNKS)
        ]
        small[3].start()
        small[0].start()
        loads[0].start()
        for load in loads[1:]:
            load.start()
        small[10].start()
        for n in (1, 2, 4, 5, 6, 7, 8, 9):
            small[n].start()
        lax.fori_loop(1, n_col, greet_near, 0)
        pl.when(sub != near)(lambda: greet({"sub": near}))
        lax.fori_loop(n_col, n_chip, greet_far, 0)

        small[3].wait()
        lane_ids = lax.broadcasted_iota(jnp.int32, (BLOCK, waters), 0)
        high_ids = lax.broadcasted_iota(jnp.int32, (nb, waters), 0)
        counts = jnp.zeros((nb, BLOCK), F32)
        for site in range(3):
            own = owner[site : site + 1, :]
            low_hot = jnp.where(lane_ids == (own & (BLOCK - 1)), 1.0, 0.0).astype(BF16)
            high_hot = jnp.where(high_ids == (own >> 7), WEIGHT[site], 0.0).astype(BF16)
            counts = counts + lax.dot_general(
                high_hot, low_hot, (((1,), (1,)), ((), ())), preferred_element_type=F32
            )
        hist1[0] = counts.astype(jnp.int32).astype(jnp.int16)
        in_row()
        for du in range(1, n_sub):
            started.append(
                send(hist1.at[0], hist1.at[du], i_send.at[du], i_recv.at[du], peer(0, du))
            )

        small[0].wait()
        for k in range(CHUNKS):
            loads[k].wait()
            for i in range(k * step // BLOCK, (k + 1) * step // BLOCK):
                at = slice(i * BLOCK, (i + 1) * BLOCK)
                for j in range(cb):
                    ac = slice(j * BLOCK, (j + 1) * BLOCK)
                    factor = pat_d[i, j].astype(F32)
                    panel[me, at, ac] = (density[at, ac].astype(F32) * factor).astype(BF16)
        def panel_copy(dc, k):
            at = panel.at[me, pl.ds(k * step, step)]
            return remote(at, at, d_send.at[dc, 0, k], d_recv.at[dc, 0, k], peer(dc, 0))

        rank = jnp.minimum(row, 2)

        def send_panels(first, end):
            for k in range(CHUNKS):
                @pl.when(jnp.logical_and(k + rank >= first, k + rank < end))
                def _(k=k):
                    for dc in range(1, n_col):
                        panel_copy(dc, k).start()

        send_panels(0, 2)
        for k in range(CHUNKS):
            at = pl.ds(k * step, step)
            for du in range(1, n_sub):
                started.append(
                    send(panel.at[me, at], panel.at[me, at], d_send.at[0, du, k],
                         d_recv.at[0, du, k], peer(0, du))
                )

        small[1].wait()
        small[2].wait()
        small[10].wait()
        low_u = []
        for i in range(rb):
            at = slice(i * BLOCK, (i + 1) * BLOCK)
            total, chosen = None, None
            for j in range(cb):
                ac = slice(j * BLOCK, (j + 1) * BLOCK)
                factor = pat_s[i, j].astype(F32)
                term = margin[at, ac].astype(F32) * factor
                dip = dipole[:, ac].astype(F32) * factor
                total = term if total is None else total + term
                chosen = dip if chosen is None else chosen + dip
            tile = total.astype(BF16)
            comp[row, at, :] = tile
            low_u.append(
                lax.dot_general(
                    chosen.astype(BF16), tile, (((1,), (1,)), ((), ())),
                    preferred_element_type=F32,
                )
            )
        for base in range(0, rb * cb, 16):
            comp[row, rows + base : rows + base + 16, :] = jnp.concatenate(
                [
                    jnp.full((1, BLOCK), pat_s[q // cb, q % cb].astype(F32), F32)
                    for q in range(base, base + 16)
                ],
                axis=0,
            ).astype(BF16)
        target, lane = lax.div(row, wide), lax.rem(row, wide)
        for i in range(rb):
            inner[4 * i : 4 * i + 3, :] = low_u[i]
            inner[4 * i + 3 : 4 * i + 4, :] = low_u[i][0:1, :]

        for load in small[4:8]:
            load.wait()
        cent = [dense(centres, c) for c in range(3)]
        quat = quaternion([dense(angles, c) for c in range(3)])
        for c in range(4):
            quats[c] = quat[c]
        matrix = rotation(quat)
        for a in range(3):
            for c in range(3):
                table[3 * a + c] = (
                    cent[c]
                    + matrix[c][0] * OFFSET[a][0]
                    + matrix[c][1] * OFFSET[a][1]
                    + matrix[c][2] * OFFSET[a][2]
                )
        listed = [
            halo_list[side : side + 1, j * BLOCK : (j + 1) * BLOCK]
            for side in range(2) for j in range(nh)
        ]
        picks = jnp.concatenate(listed + [listed[0]] * (8 - len(listed)), axis=0)
        low, high = picks & (BLOCK - 1), picks >> 7
        for t in range(9):
            value = lookup(table[t, 0:1, :], low)
            for h in range(1, wt):
                value = jnp.where(high == h, lookup(table[t, h : h + 1, :], low), value)
            for side in range(2):
                halo_out[side, t * nh : (t + 1) * nh, :] = value[side * nh : (side + 1) * nh, :]
        in_all()

        total = hist1[0].astype(jnp.int32)
        for du in range(1, n_sub):
            arrived(hist1.at[du], i_recv.at[du])
            total = total + hist1[du].astype(jnp.int32)
        hist[0] = total.astype(jnp.int16)

        def share(q, carry):
            remote(hist.at[0], hist.at[q], h_send, h_recv, chip(q)).start()
            return carry

        lax.fori_loop(1, n_chip, share, 0)

        def pass_inner(dr):
            there = peer_row(dr)
            there["col"], there["sub"] = lax.div(target, n_sub), lax.rem(target, n_sub)
            return remote(
                inner, parts.at[lane, me], v_send.at[dr], v_recv.at[lane, me], there
            )

        @pl.when(target == me)
        def _():
            parts[lane, me] = inner[...]

        pl.when(target != me)(lambda: pass_inner(0).start())
        for dr in range(1, n_row):
            pass_inner(dr).start()
        for side, by in ((0, 1), (1, n_row - 1)):
            started.append(
                send(halo_out.at[side], halo_in.at[side], e_send.at[side], e_recv.at[side],
                     peer_row(by))
            )

        def pass_block(to):
            return remote(
                comp.at[row], comp.at[row], s_send.at[to], s_recv.at[row], {"row": to}
            )

        upper = lax.div(row, n_row // 2)
        inner_row = n_row - 1 - upper * (n_row // 2)

        def pass_blocks(early):
            for to in range(n_row):
                held = to == inner_row
                go = jnp.logical_not(held) if early else held
                pl.when(jnp.logical_and(row != to, go))(lambda to=to: pass_block(to).start())

        pass_blocks(True)
        send_panels(2, 6)
        def expand(r):
            marks = comp[r, rows : rows + rb * cb, :].astype(F32)
            for i in range(rb):
                tile = comp[r, i * BLOCK : (i + 1) * BLOCK, :].astype(F32)
                at = slice(i * BLOCK, (i + 1) * BLOCK)
                for j in range(cb):
                    q = i * cb + j
                    full[r, at, j * BLOCK : (j + 1) * BLOCK] = (tile * marks[q : q + 1, :]).astype(BF16)

        def pass_on(k):
            at = pl.ds(k * step, step)
            for dc in range(1, n_col):
                slot = source(dc, 0)
                arrived(panel.at[slot, at], d_recv.at[dc, 0, k])
                for du in range(1, n_sub):
                    started.append(
                        send(panel.at[slot, at], panel.at[slot, at], f_send.at[dc, du, k],
                             d_recv.at[dc, du, k], peer(0, du))
                    )

        def pick_own(j, carry):
            lanes = pl.ds(pl.multiple_of(j * BLOCK, BLOCK), BLOCK)
            for s in range(neigh // 8):
                idx = neighbours[8 * s : 8 * s + 8, lanes]
                low, high = idx & (BLOCK - 1), idx >> 7
                part = [lookup(table[t, 0:1, :], low) for t in range(9)]
                for h in range(1, wt):
                    hit = high == h
                    for t in range(9):
                        part[t] = jnp.where(hit, lookup(table[t, h : h + 1, :], low), part[t])
                for t in range(9):
                    picked[j, s, t] = part[t]
            return carry

        def pair_tile(j, carry):
            lanes = pl.ds(pl.multiple_of(j * BLOCK, BLOCK), BLOCK)
            own = [jnp.broadcast_to(table[t, pl.ds(j, 1), :], (8, BLOCK)) for t in range(9)]
            totals = [jnp.zeros((8, BLOCK), F32) for _ in range(9)]
            for s in range(neigh // 8):
                idx = neighbours[8 * s : 8 * s + 8, lanes]
                low, high = idx & (BLOCK - 1), idx >> 7
                part = [picked[j, s, t] for t in range(9)]
                for h in range(wt, wt + 2 * nh):
                    hit = high == h
                    side, at = (h - wt) // nh, (h - wt) % nh
                    for t in range(9):
                        line = halo_in[side, t * nh + at : t * nh + at + 1, :]
                        part[t] = jnp.where(hit, lookup(line, low), part[t])
                for a in range(3):
                    for b in range(3):
                        d = [own[3 * a + c] - part[3 * b + c] for c in range(3)]
                        inv = lax.rsqrt(d[0] * d[0] + d[1] * d[1] + d[2] * d[2] + SOFTEN)
                        weight = (CHARGE[a] * CHARGE[b]) * (inv * inv * inv)
                        for c in range(3):
                            totals[3 * a + c] = totals[3 * a + c] + d[c] * weight
            for t in range(9):
                force[t, pl.ds(j, 1), :] = jnp.sum(totals[t], axis=0, keepdims=True)
            return carry

        lax.fori_loop(0, wt, pick_own, 0)

        arrived(hist.at[pl.ds(1, n_chip - 1)], h_recv)
        counts = lax.fori_loop(
            1, n_chip, lambda q, c: c + hist[q].astype(jnp.int32), hist[0].astype(jnp.int32)
        )
        potential[...] = counts.astype(F32) * UNIT
        for s in range(wide):
            for m in range(n_m):
                is_own = jnp.logical_and(target == me, jnp.logical_and(lane == s, me == m))
                pl.when(jnp.logical_not(is_own))(
                    lambda s=s, m=m: arrived(parts.at[s, m], v_recv.at[s, m])
                )
        lines = [[], [], []]
        for s in range(wide):
            total = parts[s, 0]
            for m in range(1, n_m):
                total = total + parts[s, m]
            for i in range(rb):
                j = s * rb + i
                weigh = COUPLE * potential[pl.ds(me * cb + j, 1), :]
                dip = dipole[:, j * BLOCK : (j + 1) * BLOCK].astype(F32)
                for c in range(3):
                    lines[c].append(total[4 * i + c : 4 * i + c + 1, :] + weigh * dip[c : c + 1, :])
        vector = jnp.concatenate([jnp.concatenate(line, axis=1) for line in lines], axis=0)
        coarse = vector.astype(BF16).astype(F32)
        stack = jnp.concatenate(
            [coarse, vector - coarse, dipole[...].astype(F32), jnp.zeros((7, cols), F32)], axis=0
        ).astype(BF16)
        for i in range(rb):
            got = lax.dot_general(
                stack, panel[me, i * BLOCK : (i + 1) * BLOCK, :], (((1,), (1,)), ((), ())),
                preferred_element_type=F32,
            )
            weigh = COUPLE * potential[pl.ds(row * rb + i, 1), :]
            inner2 = got[0:3, :] + got[3:6, :] + weigh * got[6:9, :]
            low_u[i] = jnp.concatenate([inner2, jnp.zeros((1, BLOCK), F32)], axis=0)
        field[0] = jnp.concatenate(low_u, axis=0).astype(BF16)

        def tell(q, carry):
            remote(field.at[0], field.at[q], q_send, q_recv, chip(q)).start()
            return carry

        lax.fori_loop(1, n_chip, tell, 0)
        pass_blocks(False)
        send_panels(6, CHUNKS + 2)
        pass_on(0)
        for side in range(2):
            arrived(halo_in.at[side], e_recv.at[side])
        lax.fori_loop(0, wt, pair_tile, 0)
        pass_on(1)

        col_pot = jnp.concatenate(
            [potential[pl.ds(me * cb + j, 1), :] for j in range(cb)], axis=1
        )
        eye = (
            lax.broadcasted_iota(jnp.int32, (BLOCK, BLOCK), 0)
            == lax.broadcasted_iota(jnp.int32, (BLOCK, BLOCK), 1)
        )

        def term(slot, at):
            total = None
            for s in range(wide):
                part = jnp.dot(
                    panel[slot, at, s * rows : (s + 1) * rows], full[slot * wide + s],
                    preferred_element_type=F32,
                )
                total = part if total is None else total + part
            return total

        def blocks(slot):
            for s in range(wide):
                r = slot * wide + s
                pl.when(r != row)(lambda r=r: arrived(comp.at[r], s_recv.at[r]))
                expand(r)

        pass_on(2)
        arrived(field.at[pl.ds(1, n_chip - 1)], q_recv)
        for dr in range(n_row):
            total = field[dr * n_col].astype(F32)
            for m in range(1, n_col):
                total = total + field[dr * n_col + m].astype(F32)
            field1[0, lax.rem(row + n_row - dr, n_row)] = total
        for du in range(1, n_sub):
            started.append(
                send(field1.at[0], field1.at[du], g_send.at[du], g_recv.at[du], peer(0, du))
            )
        pass_on(3)
        flip = lax.rem(upper + lax.div(col, n_col // 2), 2)
        for p in range(n_col - 1):
            dc = lax.rem(p + flip, n_col)
            for du in range(n_sub):
                slot = source(dc, du)
                if du > 0:
                    for k in range(CHUNKS):
                        arrived(panel.at[slot, pl.ds(k * step, step)], d_recv.at[dc, du, k])
                blocks(slot)
                for q in range(SPLIT):
                    at = slice(q * rows // SPLIT, (q + 1) * rows // SPLIT)
                    if p + du == 0:
                        total_out[at, :] = term(slot, at)
                    else:
                        total_out[at, :] += term(slot, at)
        small[8].wait()
        small[9].wait()
        for du in range(1, n_sub):
            arrived(field1.at[du], g_recv.at[du])
        for r in range(n_row):
            total = field1[0, r]
            for du in range(1, n_sub):
                total = total + field1[du, r]
            sums[r] = total

        forces = []
        for a in range(3):
            own = dense(owner, a)
            low, high = own & (BLOCK - 1), own >> 7
            value = [jnp.zeros((wt, BLOCK), F32)] * 3
            for h in range(nb):
                hit = high == h
                at = 4 * (h % rb)
                for c in range(3):
                    value[c] = jnp.where(
                        hit, lookup(sums[h // rb, at + c : at + c + 1, :], low), value[c]
                    )
            forces.append([force[3 * a + c] + CHARGE[a] * value[c] for c in range(3)])
        cent = [dense(centres, c) for c in range(3)]
        quat = [quats[c] for c in range(4)]
        torque = [jnp.zeros((wt, BLOCK), F32)] * 3
        for a in range(3):
            lever = [table[3 * a + c] - cent[c] for c in range(3)]
            turn = cross(lever, forces[a])
            torque = [torque[c] + turn[c] for c in range(3)]
        omega = []
        for c in range(3):
            pull = forces[0][c] + forces[1][c] + forces[2][c]
            fast = dense(velocity, c) + STEP_DT * pull / WATER_MASS
            spread(velocity_new, c, fast)
            spread(centres_new, c, cent[c] + STEP_DT * fast)
            spin = dense(angmom, c) + STEP_DT * torque[c]
            spread(angmom_new, c, spin)
            omega.append(spin / INERTIA)
        vector = quat[1:4]
        delta = [-(omega[0] * vector[0] + omega[1] * vector[1] + omega[2] * vector[2])]
        turn = cross(omega, vector)
        delta += [quat[0] * omega[c] + turn[c] for c in range(3)]
        moved = [quat[c] + 0.5 * STEP_DT * delta[c] for c in range(4)]
        length = jnp.sqrt(sum(m * m for m in moved))
        for c in range(4):
            spread(orient_new, c, moved[c] / length)

        dc = lax.rem(n_col - 1 + flip, n_col)
        for du in range(n_sub):
            blocks(source(dc, du))
        for k in range(CHUNKS):
            at = slice(k * step, (k + 1) * step)
            total = total_out[at, :]
            for du in range(n_sub):
                slot = source(dc, du)
                if du > 0:
                    arrived(panel.at[slot, at], d_recv.at[dc, du, k])
                total = total + term(slot, at)
            line = potential[pl.ds(row * rb + k, 1), :]
            row_pot = jnp.sum(jnp.where(eye, line, 0.0), axis=1, keepdims=True)
            mine = panel[me, at, :].astype(F32)
            coupled[at, :] = (total + COUPLE * (row_pot + col_pot) * mine).astype(BF16)

        arrived(hist.at[pl.ds(1, n_chip - 1)], h_send)
        arrived(field.at[pl.ds(1, n_chip - 1)], q_send)
        pl.when(target != me)(lambda: pass_inner(0).wait_send())
        for dr in range(1, n_row):
            pass_inner(dr).wait_send()
        for to in range(n_row):
            pl.when(row != to)(lambda to=to: pass_block(to).wait_send())
        for dc in range(1, n_col):
            for k in range(CHUNKS):
                panel_copy(dc, k).wait_send()
        for copy in started:
            copy.wait_send()

    hbm = pl.BlockSpec(memory_space=pltpu.HBM)
    vmem = pl.BlockSpec(memory_space=pltpu.VMEM)
    dma = lambda *s: pltpu.SemaphoreType.DMA(s)
    one = pltpu.SemaphoreType.DMA(())
    call = pl.pallas_call(
        kernel,
        out_shape=(
            pltpu.VMEM((rows, cols), BF16),
            pltpu.VMEM((3, waters), F32),
            pltpu.VMEM((3, waters), F32),
            pltpu.VMEM((3, waters), F32),
            pltpu.VMEM((4, waters), F32),
        ),
        in_specs=[hbm] * 12,
        out_specs=(vmem,) * 5,
        scratch_shapes=[
            pltpu.VMEM((rows, cols), BF16),
            pltpu.VMEM((rows, cols), BF16),
            pltpu.SMEM((rb, cb), jnp.int32),
            pltpu.SMEM((rb, cb), jnp.int32),
            pltpu.VMEM((3, cols), BF16),
            pltpu.VMEM((3, waters), jnp.int32),
            pltpu.VMEM((3, waters), F32),
            pltpu.VMEM((3, waters), F32),
            pltpu.VMEM((3, waters), F32),
            pltpu.VMEM((3, waters), F32),
            pltpu.VMEM((2, halo), jnp.int32),
            pltpu.VMEM((neigh, waters), jnp.int32),
            pltpu.VMEM((n_m, rows, cols), BF16),
            pltpu.VMEM((n_row, rows + rb * cb, BLOCK), BF16),
            pltpu.VMEM((n_row, rows, cols), BF16),
            pltpu.VMEM((rows, cols), F32),
            pltpu.VMEM((wt, neigh // 8, 9, 8, BLOCK), F32),
            pltpu.VMEM((n_chip, nb, BLOCK), jnp.int16),
            pltpu.VMEM((rb * 4, BLOCK), F32),
            pltpu.VMEM((wide, n_m, rb * 4, BLOCK), F32),
            pltpu.VMEM((n_chip, rb * 4, BLOCK), BF16),
            pltpu.VMEM((2, 24, BLOCK), F32),
            pltpu.VMEM((2, 24, BLOCK), F32),
            pltpu.VMEM((9, wt, BLOCK), F32),
            pltpu.VMEM((9, wt, BLOCK), F32),
            pltpu.VMEM((4, wt, BLOCK), F32),
            pltpu.VMEM((nb, BLOCK), F32),
            pltpu.VMEM((n_row, rb * 4, BLOCK), F32),
            pltpu.VMEM((n_sub, nb, BLOCK), jnp.int16),
            pltpu.VMEM((n_sub, n_row, rb * 4, BLOCK), F32),
            dma(11), dma(CHUNKS),
            dma(n_col, n_sub, CHUNKS), dma(n_col, n_sub, CHUNKS), dma(n_col, n_sub, CHUNKS),
            dma(n_row), dma(n_row), one, one, dma(n_row), dma(wide, n_m),
            one, one, dma(2), dma(2), pltpu.SemaphoreType.REGULAR, pltpu.SemaphoreType.REGULAR,
            dma(n_sub), dma(n_sub), dma(n_sub), dma(n_sub),
        ],
        compiler_params=pltpu.CompilerParams(
            collective_id=0, has_side_effects=True, vmem_limit_bytes=48 << 20
        ),
    )
    return call


def deliver(results):
    count = len(results)

    def kernel(*refs):
        sem = refs[2 * count]
        stores = [
            pltpu.make_async_copy(refs[n], refs[count + n], sem.at[n]) for n in range(count)
        ]
        for store in stores:
            store.start()
        for store in stores:
            store.wait()

    return pl.pallas_call(
        kernel,
        out_shape=tuple(jax.ShapeDtypeStruct(r.shape, r.dtype) for r in results),
        in_specs=[pl.BlockSpec(memory_space=pltpu.VMEM)] * count,
        out_specs=(pl.BlockSpec(memory_space=pltpu.HBM),) * count,
        scratch_shapes=[pltpu.SemaphoreType.DMA((count,))],
    )(*[pltpu.with_memory_space_constraint(r, pltpu.VMEM) for r in results])


def solution(mesh):
    n_row, n_col, n_sub = mesh.shape["row"], mesh.shape["col"], mesh.shape["sub"]

    def shards(density, margin, pattern_d, pattern_s, dipole, owner, centres, angles,
               velocity, angmom, halo_list, neighbours):
        call = make_kernel(
            n_row, n_col, n_sub, density.shape[0], density.shape[1], owner.shape[1],
            neighbours.shape[0], halo_list.shape[1],
        )
        return deliver(
            call(*[
                pltpu.with_memory_space_constraint(x, pltpu.HBM)
                for x in (density, margin, pattern_d, pattern_s, dipole, owner, centres,
                          angles, velocity, angmom, halo_list, neighbours)
            ])
        )

    block = P(("groups", "row"), ("col", "sub"))
    water = P(None, ("groups", "row", "col", "sub"))
    return jax.shard_map(
        shards,
        mesh=mesh,
        in_specs=(block,) * 4 + (P(None, ("groups", "col", "sub")),) + (water,) * 7,
        out_specs=(block,) + (water,) * 4,
        check_vma=False,
    )
```

```python
import jax
import jax.numpy as jnp
from jax import lax
from jax.experimental import pallas as pl
from jax.experimental.pallas import tpu as pltpu
from jax.sharding import PartitionSpec as P

BLOCK = 128
UNIT = 0.417
OFFSET = ((0.0, 0.0, -0.12), (0.76, 0.0, 0.47), (-0.76, 0.0, 0.47))
WEIGHT = (-2.0, 1.0, 1.0)
CHARGE = (-0.834, 0.417, 0.417)
COUPLE = 0.1
STEP_DT = 0.5
WATER_MASS = 1.0
INERTIA = 0.5
SOFTEN = 1.0
CHUNKS = 4
SPLIT = 2
F32 = jnp.float32
BF16 = jnp.bfloat16


def lookup(row, low):
    return jnp.take_along_axis(
        jnp.broadcast_to(row, low.shape), low, axis=1, mode="promise_in_bounds"
    )


def dense(ref, compo):
    count = ref.shape[1] // BLOCK
    return jnp.concatenate(
        [ref[compo : compo + 1, j * BLOCK : (j + 1) * BLOCK] for j in range(count)], axis=0
    )


def spread(ref, compo, value):
    for j in range(ref.shape[1] // BLOCK):
        ref[compo : compo + 1, j * BLOCK : (j + 1) * BLOCK] = value[j : j + 1, :]


def cross(a, b):
    return (
        a[1] * b[2] - a[2] * b[1],
        a[2] * b[0] - a[0] * b[2],
        a[0] * b[1] - a[1] * b[0],
    )


def quaternion(angles):
    cos_r, cos_p, cos_y = [jnp.cos(0.5 * a) for a in angles]
    sin_r, sin_p, sin_y = [jnp.sin(0.5 * a) for a in angles]
    return (
        cos_r * cos_p * cos_y + sin_r * sin_p * sin_y,
        sin_r * cos_p * cos_y - cos_r * sin_p * sin_y,
        cos_r * sin_p * cos_y + sin_r * cos_p * sin_y,
        cos_r * cos_p * sin_y - sin_r * sin_p * cos_y,
    )


def rotation(quat):
    w, x, y, z = quat
    return (
        (1.0 - 2.0 * (y * y + z * z), 2.0 * (x * y - w * z), 2.0 * (x * z + w * y)),
        (2.0 * (x * y + w * z), 1.0 - 2.0 * (x * x + z * z), 2.0 * (y * z - w * x)),
        (2.0 * (x * z - w * y), 2.0 * (y * z + w * x), 1.0 - 2.0 * (x * x + y * y)),
    )


def make_kernel(n_row, n_col, n_sub, rows, cols, waters, neigh, halo):
    n_m = n_col * n_sub
    n_all = n_row * n_m
    n_chip = n_row * n_col
    order = rows * n_row
    rb, cb, nb = rows // BLOCK, cols // BLOCK, order // BLOCK
    wt, nh = waters // BLOCK, halo // BLOCK
    wide = cols // rows
    step = rows // CHUNKS
    hr = 9 * nh

    def kernel(
        density_hbm, margin_hbm, pat_d_hbm, pat_s_hbm, dipole_hbm, owner_hbm, centres_hbm,
        angles_hbm, velocity_hbm, angmom_hbm, halo_list_hbm, neighbours_hbm,
        coupled, centres_new, velocity_new, angmom_new, orient_new,
        density, margin, pat_d, pat_s, dipole, owner, centres,
        angles, velocity, angmom, halo_list, neighbours,
        panel, comp, full, total_out, picked, hist, inner, parts, field, halo_out, halo_in,
        table, force, quats, potential, sums, hist1, field1,
        l_sem, c_sem, d_send, d_recv, f_send, s_send, s_recv, h_send, h_recv, v_send, v_recv,
        q_send, q_recv, e_send, e_recv, row_ready, all_ready, i_send, i_recv, g_send, g_recv,
    ):
        row, col, sub = lax.axis_index("row"), lax.axis_index("col"), lax.axis_index("sub")
        me = col * n_sub + sub

        def peer(dc, du):
            return {"col": lax.rem(col + dc, n_col), "sub": lax.rem(sub + du, n_sub)}

        def peer_row(dr):
            return {"row": lax.rem(row + dr, n_row)}

        def other(q):
            dr, dm = lax.div(q, n_m), lax.rem(q, n_m)
            return {
                "row": lax.rem(row + dr, n_row),
                "col": lax.rem(col + lax.div(dm, n_sub), n_col),
                "sub": lax.rem(sub + lax.rem(dm, n_sub), n_sub),
            }

        def chip(q):
            return {
                "row": lax.rem(row + lax.div(q, n_col), n_row),
                "col": lax.rem(col + lax.rem(q, n_col), n_col),
            }

        def source(dc, du):
            return (
                lax.rem(col + n_col - dc, n_col) * n_sub + lax.rem(sub + n_sub - du, n_sub)
            )

        started = []

        def remote(src, dst, ssem, rsem, dev):
            return pltpu.make_async_remote_copy(
                src_ref=src, dst_ref=dst, send_sem=ssem, recv_sem=rsem,
                device_id=dev, device_id_type=pl.DeviceIdType.MESH,
            )

        def send(src, dst, ssem, rsem, dev):
            copy = remote(src, dst, ssem, rsem, dev)
            copy.start()
            return copy

        def arrived(ref, sem):
            pltpu.make_async_copy(ref, ref, sem).wait()

        barrier = pltpu.get_barrier_semaphore()

        def greet(dev):
            pl.semaphore_signal(
                barrier, inc=1, device_id=dev, device_id_type=pl.DeviceIdType.MESH
            )

        near, far = 0, n_sub - 1

        def greet_near(q, carry):
            greet({"col": lax.rem(col + q, n_col), "sub": near})
            return carry

        def greet_far(q, carry):
            greet({
                "row": lax.rem(row + lax.div(q, n_col), n_row),
                "col": lax.rem(col + lax.rem(q, n_col), n_col), "sub": far,
            })
            return carry

        def in_row():
            @pl.when(sub == near)
            def _():
                pl.semaphore_wait(barrier, n_m - 1)
                for du in range(1, n_sub):
                    pl.semaphore_signal(
                        row_ready, inc=1, device_id=peer(0, du),
                        device_id_type=pl.DeviceIdType.MESH,
                    )

            pl.when(sub != near)(lambda: pl.semaphore_wait(row_ready, 1))

        def in_all():
            @pl.when(sub == far)
            def _():
                pl.semaphore_wait(barrier, n_all - n_m)
                for du in range(1, n_sub):
                    pl.semaphore_signal(
                        all_ready, inc=1, device_id=peer(0, du),
                        device_id_type=pl.DeviceIdType.MESH,
                    )

            pl.when(sub != far)(lambda: pl.semaphore_wait(all_ready, 1))

        small = [
            pltpu.make_async_copy(src, dst, l_sem.at[n])
            for n, (src, dst) in enumerate((
                (pat_d_hbm, pat_d), (pat_s_hbm, pat_s), (dipole_hbm, dipole),
                (owner_hbm, owner), (angles_hbm, angles), (centres_hbm, centres),
                (halo_list_hbm, halo_list), (neighbours_hbm, neighbours),
                (velocity_hbm, velocity), (angmom_hbm, angmom), (margin_hbm, margin),
            ))
        ]
        loads = [
            pltpu.make_async_copy(
                density_hbm.at[pl.ds(k * step, step)], density.at[pl.ds(k * step, step)],
                c_sem.at[k],
            )
            for k in range(CHUNKS)
        ]
        small[3].start()
        small[0].start()
        loads[0].start()
        for load in loads[1:]:
            load.start()
        small[10].start()
        for n in (1, 2, 4, 5, 6, 7, 8, 9):
            small[n].start()
        lax.fori_loop(1, n_col, greet_near, 0)
        pl.when(sub != near)(lambda: greet({"sub": near}))
        lax.fori_loop(n_col, n_chip, greet_far, 0)

        small[3].wait()
        lane_ids = lax.broadcasted_iota(jnp.int32, (BLOCK, waters), 0)
        high_ids = lax.broadcasted_iota(jnp.int32, (nb, waters), 0)
        counts = jnp.zeros((nb, BLOCK), F32)
        for site in range(3):
            own = owner[site : site + 1, :]
            low_hot = jnp.where(lane_ids == (own & (BLOCK - 1)), 1.0, 0.0).astype(BF16)
            high_hot = jnp.where(high_ids == (own >> 7), WEIGHT[site], 0.0).astype(BF16)
            counts = counts + lax.dot_general(
                high_hot, low_hot, (((1,), (1,)), ((), ())), preferred_element_type=F32
            )
        hist1[0] = counts.astype(jnp.int32).astype(jnp.int16)
        in_row()
        for du in range(1, n_sub):
            started.append(
                send(hist1.at[0], hist1.at[du], i_send.at[du], i_recv.at[du], peer(0, du))
            )

        small[0].wait()
        for k in range(CHUNKS):
            loads[k].wait()
            for i in range(k * step // BLOCK, (k + 1) * step // BLOCK):
                at = slice(i * BLOCK, (i + 1) * BLOCK)
                for j in range(cb):
                    ac = slice(j * BLOCK, (j + 1) * BLOCK)
                    factor = pat_d[i, j].astype(F32)
                    panel[me, at, ac] = (density[at, ac].astype(F32) * factor).astype(BF16)
        def panel_copy(dc, k):
            at = panel.at[me, pl.ds(k * step, step)]
            return remote(at, at, d_send.at[dc, 0, k], d_recv.at[dc, 0, k], peer(dc, 0))

        rank = jnp.minimum(row, 2)

        def send_panels(first, end):
            for k in range(CHUNKS):
                @pl.when(jnp.logical_and(k + rank >= first, k + rank < end))
                def _(k=k):
                    for dc in range(1, n_col):
                        panel_copy(dc, k).start()

        send_panels(0, 2)
        for k in range(CHUNKS):
            at = pl.ds(k * step, step)
            for du in range(1, n_sub):
                started.append(
                    send(panel.at[me, at], panel.at[me, at], d_send.at[0, du, k],
                         d_recv.at[0, du, k], peer(0, du))
                )

        small[1].wait()
        small[2].wait()
        small[10].wait()
        low_u = []
        for i in range(rb):
            at = slice(i * BLOCK, (i + 1) * BLOCK)
            total, chosen = None, None
            for j in range(cb):
                ac = slice(j * BLOCK, (j + 1) * BLOCK)
                factor = pat_s[i, j].astype(F32)
                term = margin[at, ac].astype(F32) * factor
                dip = dipole[:, ac].astype(F32) * factor
                total = term if total is None else total + term
                chosen = dip if chosen is None else chosen + dip
            tile = total.astype(BF16)
            comp[row, at, :] = tile
            low_u.append(
                lax.dot_general(
                    chosen.astype(BF16), tile, (((1,), (1,)), ((), ())),
                    preferred_element_type=F32,
                )
            )
        for base in range(0, rb * cb, 16):
            comp[row, rows + base : rows + base + 16, :] = jnp.concatenate(
                [
                    jnp.full((1, BLOCK), pat_s[q // cb, q % cb].astype(F32), F32)
                    for q in range(base, base + 16)
                ],
                axis=0,
            ).astype(BF16)
        target, lane = lax.div(row, wide), lax.rem(row, wide)
        for i in range(rb):
            inner[4 * i : 4 * i + 3, :] = low_u[i]
            inner[4 * i + 3 : 4 * i + 4, :] = low_u[i][0:1, :]

        for load in small[4:8]:
            load.wait()
        cent = [dense(centres, c) for c in range(3)]
        quat = quaternion([dense(angles, c) for c in range(3)])
        for c in range(4):
            quats[c] = quat[c]
        matrix = rotation(quat)
        for a in range(3):
            for c in range(3):
                table[3 * a + c] = (
                    cent[c]
                    + matrix[c][0] * OFFSET[a][0]
                    + matrix[c][1] * OFFSET[a][1]
                    + matrix[c][2] * OFFSET[a][2]
                )
        listed = [
            halo_list[side : side + 1, j * BLOCK : (j + 1) * BLOCK]
            for side in range(2) for j in range(nh)
        ]
        picks = jnp.concatenate(listed + [listed[0]] * (8 - len(listed)), axis=0)
        low, high = picks & (BLOCK - 1), picks >> 7
        for t in range(9):
            value = lookup(table[t, 0:1, :], low)
            for h in range(1, wt):
                value = jnp.where(high == h, lookup(table[t, h : h + 1, :], low), value)
            for side in range(2):
                halo_out[side, t * nh : (t + 1) * nh, :] = value[side * nh : (side + 1) * nh, :]
        in_all()

        total = hist1[0].astype(jnp.int32)
        for du in range(1, n_sub):
            arrived(hist1.at[du], i_recv.at[du])
            total = total + hist1[du].astype(jnp.int32)
        hist[0] = total.astype(jnp.int16)

        def share(q, carry):
            remote(hist.at[0], hist.at[q], h_send, h_recv, chip(q)).start()
            return carry

        lax.fori_loop(1, n_chip, share, 0)

        def pass_inner(dr):
            there = peer_row(dr)
            there["col"], there["sub"] = lax.div(target, n_sub), lax.rem(target, n_sub)
            return remote(
                inner, parts.at[lane, me], v_send.at[dr], v_recv.at[lane, me], there
            )

        @pl.when(target == me)
        def _():
            parts[lane, me] = inner[...]

        pl.when(target != me)(lambda: pass_inner(0).start())
        for dr in range(1, n_row):
            pass_inner(dr).start()
        for side, by in ((0, 1), (1, n_row - 1)):
            started.append(
                send(halo_out.at[side], halo_in.at[side], e_send.at[side], e_recv.at[side],
                     peer_row(by))
            )

        def pass_block(to):
            return remote(
                comp.at[row], comp.at[row], s_send.at[to], s_recv.at[row], {"row": to}
            )

        upper = lax.div(row, n_row // 2)
        inner_row = n_row - 1 - upper * (n_row // 2)

        def pass_blocks(early):
            for to in range(n_row):
                held = to == inner_row
                go = jnp.logical_not(held) if early else held
                pl.when(jnp.logical_and(row != to, go))(lambda to=to: pass_block(to).start())

        pass_blocks(True)
        send_panels(2, 5)
        def expand(r):
            marks = comp[r, rows : rows + rb * cb, :].astype(F32)
            for i in range(rb):
                tile = comp[r, i * BLOCK : (i + 1) * BLOCK, :].astype(F32)
                at = slice(i * BLOCK, (i + 1) * BLOCK)
                for j in range(cb):
                    q = i * cb + j
                    full[r, at, j * BLOCK : (j + 1) * BLOCK] = (tile * marks[q : q + 1, :]).astype(BF16)

        def pass_on(k):
            at = pl.ds(k * step, step)
            for dc in range(1, n_col):
                slot = source(dc, 0)
                arrived(panel.at[slot, at], d_recv.at[dc, 0, k])
                for du in range(1, n_sub):
                    started.append(
                        send(panel.at[slot, at], panel.at[slot, at], f_send.at[dc, du, k],
                             d_recv.at[dc, du, k], peer(0, du))
                    )

        def pick_own(j, carry):
            lanes = pl.ds(pl.multiple_of(j * BLOCK, BLOCK), BLOCK)
            for s in range(neigh // 8):
                idx = neighbours[8 * s : 8 * s + 8, lanes]
                low, high = idx & (BLOCK - 1), idx >> 7
                part = [lookup(table[t, 0:1, :], low) for t in range(9)]
                for h in range(1, wt):
                    hit = high == h
                    for t in range(9):
                        part[t] = jnp.where(hit, lookup(table[t, h : h + 1, :], low), part[t])
                for t in range(9):
                    picked[j, s, t] = part[t]
            return carry

        def pair_tile(j, carry):
            lanes = pl.ds(pl.multiple_of(j * BLOCK, BLOCK), BLOCK)
            own = [jnp.broadcast_to(table[t, pl.ds(j, 1), :], (8, BLOCK)) for t in range(9)]
            totals = [jnp.zeros((8, BLOCK), F32) for _ in range(9)]
            for s in range(neigh // 8):
                idx = neighbours[8 * s : 8 * s + 8, lanes]
                low, high = idx & (BLOCK - 1), idx >> 7
                part = [picked[j, s, t] for t in range(9)]
                for h in range(wt, wt + 2 * nh):
                    hit = high == h
                    side, at = (h - wt) // nh, (h - wt) % nh
                    for t in range(9):
                        line = halo_in[side, t * nh + at : t * nh + at + 1, :]
                        part[t] = jnp.where(hit, lookup(line, low), part[t])
                for a in range(3):
                    for b in range(3):
                        d = [own[3 * a + c] - part[3 * b + c] for c in range(3)]
                        inv = lax.rsqrt(d[0] * d[0] + d[1] * d[1] + d[2] * d[2] + SOFTEN)
                        weight = (CHARGE[a] * CHARGE[b]) * (inv * inv * inv)
                        for c in range(3):
                            totals[3 * a + c] = totals[3 * a + c] + d[c] * weight
            for t in range(9):
                force[t, pl.ds(j, 1), :] = jnp.sum(totals[t], axis=0, keepdims=True)
            return carry

        lax.fori_loop(0, wt, pick_own, 0)

        arrived(hist.at[pl.ds(1, n_chip - 1)], h_recv)
        counts = lax.fori_loop(
            1, n_chip, lambda q, c: c + hist[q].astype(jnp.int32), hist[0].astype(jnp.int32)
        )
        potential[...] = counts.astype(F32) * UNIT
        for s in range(wide):
            for m in range(n_m):
                is_own = jnp.logical_and(target == me, jnp.logical_and(lane == s, me == m))
                pl.when(jnp.logical_not(is_own))(
                    lambda s=s, m=m: arrived(parts.at[s, m], v_recv.at[s, m])
                )
        lines = [[], [], []]
        for s in range(wide):
            total = parts[s, 0]
            for m in range(1, n_m):
                total = total + parts[s, m]
            for i in range(rb):
                j = s * rb + i
                weigh = COUPLE * potential[pl.ds(me * cb + j, 1), :]
                dip = dipole[:, j * BLOCK : (j + 1) * BLOCK].astype(F32)
                for c in range(3):
                    lines[c].append(total[4 * i + c : 4 * i + c + 1, :] + weigh * dip[c : c + 1, :])
        vector = jnp.concatenate([jnp.concatenate(line, axis=1) for line in lines], axis=0)
        coarse = vector.astype(BF16).astype(F32)
        stack = jnp.concatenate(
            [coarse, vector - coarse, dipole[...].astype(F32), jnp.zeros((7, cols), F32)], axis=0
        ).astype(BF16)
        for i in range(rb):
            got = lax.dot_general(
                stack, panel[me, i * BLOCK : (i + 1) * BLOCK, :], (((1,), (1,)), ((), ())),
                preferred_element_type=F32,
            )
            weigh = COUPLE * potential[pl.ds(row * rb + i, 1), :]
            inner2 = got[0:3, :] + got[3:6, :] + weigh * got[6:9, :]
            low_u[i] = jnp.concatenate([inner2, jnp.zeros((1, BLOCK), F32)], axis=0)
        field[0] = jnp.concatenate(low_u, axis=0).astype(BF16)

        def tell(q, carry):
            remote(field.at[0], field.at[q], q_send, q_recv, chip(q)).start()
            return carry

        lax.fori_loop(1, n_chip, tell, 0)
        pass_blocks(False)
        send_panels(5, CHUNKS + 2)
        pass_on(0)
        for side in range(2):
            arrived(halo_in.at[side], e_recv.at[side])
        lax.fori_loop(0, wt, pair_tile, 0)
        pass_on(1)

        col_pot = jnp.concatenate(
            [potential[pl.ds(me * cb + j, 1), :] for j in range(cb)], axis=1
        )
        eye = (
            lax.broadcasted_iota(jnp.int32, (BLOCK, BLOCK), 0)
            == lax.broadcasted_iota(jnp.int32, (BLOCK, BLOCK), 1)
        )

        def term(slot, at):
            total = None
            for s in range(wide):
                part = jnp.dot(
                    panel[slot, at, s * rows : (s + 1) * rows], full[slot * wide + s],
                    preferred_element_type=F32,
                )
                total = part if total is None else total + part
            return total

        def blocks(slot):
            for s in range(wide):
                r = slot * wide + s
                pl.when(r != row)(lambda r=r: arrived(comp.at[r], s_recv.at[r]))
                expand(r)

        pass_on(2)
        arrived(field.at[pl.ds(1, n_chip - 1)], q_recv)
        for dr in range(n_row):
            total = field[dr * n_col].astype(F32)
            for m in range(1, n_col):
                total = total + field[dr * n_col + m].astype(F32)
            field1[0, lax.rem(row + n_row - dr, n_row)] = total
        for du in range(1, n_sub):
            started.append(
                send(field1.at[0], field1.at[du], g_send.at[du], g_recv.at[du], peer(0, du))
            )
        pass_on(3)
        flip = lax.rem(upper + lax.div(col, n_col // 2), 2)
        for p in range(n_col - 1):
            dc = lax.rem(p + flip, n_col)
            for du in range(n_sub):
                slot = source(dc, du)
                if du > 0:
                    for k in range(CHUNKS):
                        arrived(panel.at[slot, pl.ds(k * step, step)], d_recv.at[dc, du, k])
                blocks(slot)
                for q in range(SPLIT):
                    at = slice(q * rows // SPLIT, (q + 1) * rows // SPLIT)
                    if p + du == 0:
                        total_out[at, :] = term(slot, at)
                    else:
                        total_out[at, :] += term(slot, at)
        small[8].wait()
        small[9].wait()
        for du in range(1, n_sub):
            arrived(field1.at[du], g_recv.at[du])
        for r in range(n_row):
            total = field1[0, r]
            for du in range(1, n_sub):
                total = total + field1[du, r]
            sums[r] = total

        forces = []
        for a in range(3):
            own = dense(owner, a)
            low, high = own & (BLOCK - 1), own >> 7
            value = [jnp.zeros((wt, BLOCK), F32)] * 3
            for h in range(nb):
                hit = high == h
                at = 4 * (h % rb)
                for c in range(3):
                    value[c] = jnp.where(
                        hit, lookup(sums[h // rb, at + c : at + c + 1, :], low), value[c]
                    )
            forces.append([force[3 * a + c] + CHARGE[a] * value[c] for c in range(3)])
        cent = [dense(centres, c) for c in range(3)]
        quat = [quats[c] for c in range(4)]
        torque = [jnp.zeros((wt, BLOCK), F32)] * 3
        for a in range(3):
            lever = [table[3 * a + c] - cent[c] for c in range(3)]
            turn = cross(lever, forces[a])
            torque = [torque[c] + turn[c] for c in range(3)]
        omega = []
        for c in range(3):
            pull = forces[0][c] + forces[1][c] + forces[2][c]
            fast = dense(velocity, c) + STEP_DT * pull / WATER_MASS
            spread(velocity_new, c, fast)
            spread(centres_new, c, cent[c] + STEP_DT * fast)
            spin = dense(angmom, c) + STEP_DT * torque[c]
            spread(angmom_new, c, spin)
            omega.append(spin / INERTIA)
        vector = quat[1:4]
        delta = [-(omega[0] * vector[0] + omega[1] * vector[1] + omega[2] * vector[2])]
        turn = cross(omega, vector)
        delta += [quat[0] * omega[c] + turn[c] for c in range(3)]
        moved = [quat[c] + 0.5 * STEP_DT * delta[c] for c in range(4)]
        length = jnp.sqrt(sum(m * m for m in moved))
        for c in range(4):
            spread(orient_new, c, moved[c] / length)

        dc = lax.rem(n_col - 1 + flip, n_col)
        for du in range(n_sub):
            blocks(source(dc, du))
        for k in range(CHUNKS):
            at = slice(k * step, (k + 1) * step)
            total = total_out[at, :]
            for du in range(n_sub):
                slot = source(dc, du)
                if du > 0:
                    arrived(panel.at[slot, at], d_recv.at[dc, du, k])
                total = total + term(slot, at)
            line = potential[pl.ds(row * rb + k, 1), :]
            row_pot = jnp.sum(jnp.where(eye, line, 0.0), axis=1, keepdims=True)
            mine = panel[me, at, :].astype(F32)
            coupled[at, :] = (total + COUPLE * (row_pot + col_pot) * mine).astype(BF16)

        arrived(hist.at[pl.ds(1, n_chip - 1)], h_send)
        arrived(field.at[pl.ds(1, n_chip - 1)], q_send)
        pl.when(target != me)(lambda: pass_inner(0).wait_send())
        for dr in range(1, n_row):
            pass_inner(dr).wait_send()
        for to in range(n_row):
            pl.when(row != to)(lambda to=to: pass_block(to).wait_send())
        for dc in range(1, n_col):
            for k in range(CHUNKS):
                panel_copy(dc, k).wait_send()
        for copy in started:
            copy.wait_send()

    hbm = pl.BlockSpec(memory_space=pltpu.HBM)
    vmem = pl.BlockSpec(memory_space=pltpu.VMEM)
    dma = lambda *s: pltpu.SemaphoreType.DMA(s)
    one = pltpu.SemaphoreType.DMA(())
    call = pl.pallas_call(
        kernel,
        out_shape=(
            pltpu.VMEM((rows, cols), BF16),
            pltpu.VMEM((3, waters), F32),
            pltpu.VMEM((3, waters), F32),
            pltpu.VMEM((3, waters), F32),
            pltpu.VMEM((4, waters), F32),
        ),
        in_specs=[hbm] * 12,
        out_specs=(vmem,) * 5,
        scratch_shapes=[
            pltpu.VMEM((rows, cols), BF16),
            pltpu.VMEM((rows, cols), BF16),
            pltpu.SMEM((rb, cb), jnp.int32),
            pltpu.SMEM((rb, cb), jnp.int32),
            pltpu.VMEM((3, cols), BF16),
            pltpu.VMEM((3, waters), jnp.int32),
            pltpu.VMEM((3, waters), F32),
            pltpu.VMEM((3, waters), F32),
            pltpu.VMEM((3, waters), F32),
            pltpu.VMEM((3, waters), F32),
            pltpu.VMEM((2, halo), jnp.int32),
            pltpu.VMEM((neigh, waters), jnp.int32),
            pltpu.VMEM((n_m, rows, cols), BF16),
            pltpu.VMEM((n_row, rows + rb * cb, BLOCK), BF16),
            pltpu.VMEM((n_row, rows, cols), BF16),
            pltpu.VMEM((rows, cols), F32),
            pltpu.VMEM((wt, neigh // 8, 9, 8, BLOCK), F32),
            pltpu.VMEM((n_chip, nb, BLOCK), jnp.int16),
            pltpu.VMEM((rb * 4, BLOCK), F32),
            pltpu.VMEM((wide, n_m, rb * 4, BLOCK), F32),
            pltpu.VMEM((n_chip, rb * 4, BLOCK), BF16),
            pltpu.VMEM((2, 24, BLOCK), F32),
            pltpu.VMEM((2, 24, BLOCK), F32),
            pltpu.VMEM((9, wt, BLOCK), F32),
            pltpu.VMEM((9, wt, BLOCK), F32),
            pltpu.VMEM((4, wt, BLOCK), F32),
            pltpu.VMEM((nb, BLOCK), F32),
            pltpu.VMEM((n_row, rb * 4, BLOCK), F32),
            pltpu.VMEM((n_sub, nb, BLOCK), jnp.int16),
            pltpu.VMEM((n_sub, n_row, rb * 4, BLOCK), F32),
            dma(11), dma(CHUNKS),
            dma(n_col, n_sub, CHUNKS), dma(n_col, n_sub, CHUNKS), dma(n_col, n_sub, CHUNKS),
            dma(n_row), dma(n_row), one, one, dma(n_row), dma(wide, n_m),
            one, one, dma(2), dma(2), pltpu.SemaphoreType.REGULAR, pltpu.SemaphoreType.REGULAR,
            dma(n_sub), dma(n_sub), dma(n_sub), dma(n_sub),
        ],
        compiler_params=pltpu.CompilerParams(
            collective_id=0, has_side_effects=True, vmem_limit_bytes=48 << 20
        ),
    )
    return call


def deliver(results):
    count = len(results)

    def kernel(*refs):
        sem = refs[2 * count]
        stores = [
            pltpu.make_async_copy(refs[n], refs[count + n], sem.at[n]) for n in range(count)
        ]
        for store in stores:
            store.start()
        for store in stores:
            store.wait()

    return pl.pallas_call(
        kernel,
        out_shape=tuple(jax.ShapeDtypeStruct(r.shape, r.dtype) for r in results),
        in_specs=[pl.BlockSpec(memory_space=pltpu.VMEM)] * count,
        out_specs=(pl.BlockSpec(memory_space=pltpu.HBM),) * count,
        scratch_shapes=[pltpu.SemaphoreType.DMA((count,))],
    )(*[pltpu.with_memory_space_constraint(r, pltpu.VMEM) for r in results])


def solution(mesh):
    n_row, n_col, n_sub = mesh.shape["row"], mesh.shape["col"], mesh.shape["sub"]

    def shards(density, margin, pattern_d, pattern_s, dipole, owner, centres, angles,
               velocity, angmom, halo_list, neighbours):
        call = make_kernel(
            n_row, n_col, n_sub, density.shape[0], density.shape[1], owner.shape[1],
            neighbours.shape[0], halo_list.shape[1],
        )
        return deliver(
            call(*[
                pltpu.with_memory_space_constraint(x, pltpu.HBM)
                for x in (density, margin, pattern_d, pattern_s, dipole, owner, centres,
                          angles, velocity, angmom, halo_list, neighbours)
            ])
        )

    block = P(("groups", "row"), ("col", "sub"))
    water = P(None, ("groups", "row", "col", "sub"))
    return jax.shard_map(
        shards,
        mesh=mesh,
        in_specs=(block,) * 4 + (P(None, ("groups", "col", "sub")),) + (water,) * 7,
        out_specs=(block,) + (water,) * 4,
        check_vma=False,
    )
```
